32 devices in a mesh: section: 4 (over y, x), head: 4 (over z), dp: 2 (over core).
Axes of the slice: x: 2, y: 2, z: 4, core: 2. Of those that a mesh axis runs over, the one named last changes fastest.
Arguments:
- stream: bfloat16 [4, 1024, 768], P('dp', None, 'head'), may hold values from -6 to 6
- cotangent: bfloat16 [4, 1024, 768], P('dp', None, 'head'), may hold values from -6 to 6
- lengths: int32 [4], P('dp'), may hold values from 256 to 1024, as said below
- picks: int32 [4, 12, 8, 64], P('dp', 'head'), may hold values from 0 to 959, as said below
- norm_gain: bfloat16 [4, 768], P('section'), may hold values from 0.5 to 1.5
- norm_bias: bfloat16 [4, 768], P('section'), may hold values from -1.75 to 1.75
- out_bias: bfloat16 [4, 768], P('section', 'head'), may hold values from -1.75 to 1.75
- weight_qkv: bfloat16 [2, 768, 3, 768], P(None, None, None, 'head'), may hold values from -0.21875 to 0.21875
- bias_qv: bfloat16 [2, 2, 768], P(None, None, 'head'), may hold values from -1.75 to 1.75
- weight_score: bfloat16 [2, 768, 12], P(None, None, 'head'), may hold values from -0.4375 to 0.4375
- weight_out: bfloat16 [2, 768, 768], P(None, 'head'), may hold values from -0.875 to 0.875
- weight_fc: bfloat16 [2, 768, 3072], P(None, None, 'head'), may hold values from -0.21875 to 0.21875
- bias_fc: bfloat16 [2, 3072], P(None, 'head'), may hold values from -1.75 to 1.75
- weight_proj: bfloat16 [2, 3072, 768], P(None, 'head'), may hold values from -0.15625 to 0.15625
Outputs:
- output: bfloat16 [4, 1024, 768], P('dp', 'section', 'head')
- input_grad: bfloat16 [4, 1024, 768], P('dp', 'section', 'head')
- grad_norm_gain: float32 [4, 768], P('section', 'head')
- grad_norm_bias: float32 [4, 768], P('section', 'head')
- grad_out_bias: float32 [4, 768], P('section', 'head')
- grad_qkv: float32 [2, 768, 3, 768], P(None, ('section', 'dp'), None, 'head')
- grad_qv_bias: float32 [2, 2, 768], P(None, None, 'head')
- grad_score: float32 [2, 768, 12], P(None, None, 'head')
- grad_out: float32 [2, 768, 768], P(None, 'head', ('section', 'dp'))
- grad_fc: float32 [2, 768, 3072], P(None, ('section', 'dp'), 'head')
- grad_fc_bias: float32 [2, 3072], P(None, 'head')
- grad_proj: float32 [2, 3072, 768], P(None, 'head', ('section', 'dp'))
The draws below stay inside these ranges and needn't reach their ends.
Inputs may be any that keep to these rules, and one draw needn't show every extreme that they name: `lengths`: among the 2 sequences of each index of dp, one drawn from the seed has length 1024. `picks`: for query block b every picked position is below b * 128 + 64; positions may repeat; the first of each block's 64 is b * 128 + 63.
All inputs are finite; a program needn't handle non-finite values.
Results may differ from the reference program's by a relative error of at most 0.03.
Values may be sent and summed in bfloat16 or wider, within the bound.
A program may use at most 128 MiB of HBM per device.

```python
import jax
import jax.numpy as jnp
from jax import lax

D = 768
H = 12
FF = 3072
BUCKET = 1024
BLOCK = 128
WINDOW = 64
TOPK = 64
MICRO = 2
LAYERS = 2
HALVES = 4
SEQS = 4


def draw_lengths(key, part):
    key = jax.random.fold_in(key, 11)
    first_key, second_key = jax.random.split(key)
    groups = SEQS // MICRO
    sampled = jax.random.randint(first_key, (groups, MICRO), BUCKET // 4, BUCKET + 1)
    longest = jax.random.randint(second_key, (groups, 1), 0, MICRO)
    slots = jnp.arange(MICRO)[None, :]
    filled = jnp.where(slots == longest, BUCKET, sampled)
    return filled.reshape(SEQS).astype(jnp.int32)


def draw_picks(key, part):
    key = jax.random.fold_in(key, 23)
    blocks = BUCKET // BLOCK
    limits = (jnp.arange(blocks) * BLOCK + BLOCK - WINDOW).astype(jnp.int32)
    bounds = jnp.broadcast_to(limits[None, None, :, None], (SEQS, H, blocks, TOPK))
    sampled = jax.random.randint(key, (SEQS, H, blocks, TOPK), 0, bounds)
    first_slot = jnp.arange(TOPK)[None, None, None, :] == 0
    return jnp.where(first_slot, bounds - 1, sampled).astype(jnp.int32)


def shard_levels(key, extent, shards, least, top_value):
    def one(dim, parts):
        steps = jax.random.uniform(jax.random.fold_in(jax.random.fold_in(key, 6), dim), (parts,), jnp.float32, least / len(shards), top_value / len(shards))
        return jnp.repeat(jnp.exp(steps), extent[dim] // parts).reshape((-1,) + (1,) * (len(extent) - dim - 1))

    factor_of = one(*shards[0])
    for cut in shards[1:]:
        factor_of = factor_of * one(*cut)
    return factor_of


def scatter_about(rng, dims, scale, bound, pieces=(), held_as=jnp.bfloat16):
    loudness = shard_levels(rng, dims, pieces, -0.22, 0.18) if pieces else 1.0
    values = jax.random.normal(rng, dims, jnp.float32) * scale * loudness
    return jnp.minimum(jnp.maximum(values, -bound), bound).astype(held_as)


def setup_inputs(seed: int = 0) -> dict:
    key_of = jax.random.split(jax.random.key(seed), 15)
    stream = scatter_about(key_of[0], (SEQS, BUCKET, D), 1.0, 6.0, ((0, 2), (2, 4)))
    cotangent = scatter_about(key_of[1], (SEQS, BUCKET, D), 1.0, 6.0, ((0, 2), (2, 4)))
    lengths = draw_lengths(jax.random.fold_in(key_of[14], 71), 0)
    picks = draw_picks(jax.random.fold_in(key_of[14], 71), 0)
    norm_gain = jnp.clip(1.0 + 0.1 * jax.random.normal(key_of[4], (HALVES, D), jnp.float32), 0.5, 1.5).astype(jnp.bfloat16)
    norm_bias = scatter_about(key_of[5], (HALVES, D), 0.3, 1.75, ((0, 4),))
    out_bias = scatter_about(key_of[6], (HALVES, D), 0.3, 1.75, ((0, 4), (1, 4)))
    weight_qkv = scatter_about(key_of[7], (LAYERS, D, 3, D), D ** -0.5, 0.21875, ((3, 4),))
    bias_qv = scatter_about(key_of[8], (LAYERS, 2, D), 0.3, 1.75, ((2, 4),))
    weight_score = scatter_about(key_of[9], (LAYERS, D, H), (D // 4) ** -0.5, 0.4375, ((2, 4),))
    weight_out = scatter_about(key_of[10], (LAYERS, D, D), (D // 16) ** -0.5, 0.875, ((1, 4),))
    weight_fc = scatter_about(key_of[11], (LAYERS, D, FF), D ** -0.5, 0.21875, ((2, 4),))
    bias_fc = scatter_about(key_of[12], (LAYERS, FF), 0.3, 1.75, ((1, 4),))
    weight_proj = scatter_about(key_of[13], (LAYERS, FF, D), (FF // 2) ** -0.5, 0.15625, ((1, 4),))
    return dict(stream=stream, cotangent=cotangent, lengths=lengths, picks=picks, norm_gain=norm_gain, norm_bias=norm_bias, out_bias=out_bias, weight_qkv=weight_qkv, bias_qv=bias_qv, weight_score=weight_score, weight_out=weight_out, weight_fc=weight_fc, bias_fc=bias_fc, weight_proj=weight_proj)


@jax.custom_vjp
def low(v):
    return lax.optimization_barrier(v.astype(jnp.bfloat16)).astype(jnp.float32)

@jax.custom_vjp
def low_back(v):
    return v

def low_keep(v):
    return (low(v), None)

def low_pass(kept, grad):
    return (grad,)

def back_keep(v):
    return (v, None)

def back_low(kept, grad):
    return (low(grad),)
low.defvjp(low_keep, low_pass)
low_back.defvjp(back_keep, back_low)

def matmul(left, right):
    return jnp.dot(left, right, precision=lax.Precision.HIGHEST, preferred_element_type=jnp.float32)

def normalize(stream, gain_row, shift_row):
    center = stream - lax.optimization_barrier(jnp.mean(stream, axis=-1, keepdims=True))
    inverse = lax.rsqrt(lax.optimization_barrier(jnp.mean(center * center, axis=-1, keepdims=True)) + 1e-05)
    return center * inverse * gain_row + shift_row

def split_heads(matrix, head_count):
    return matrix.reshape(matrix.shape[0], head_count, -1).transpose(1, 0, 2)

def gather_keys(headed, picked):
    head_count, blocks = (picked.shape[0], picked.shape[1])
    blocked = headed.reshape(head_count, blocks, BLOCK, -1)
    earlier = jnp.concatenate([jnp.zeros_like(blocked[:, :1]), blocked[:, :-1]], axis=1)
    chosen = headed[jnp.arange(head_count)[:, None, None], picked]
    return jnp.concatenate([earlier, blocked, chosen], axis=2)

def allowed_mask(picked, length):
    head_count, blocks = (picked.shape[0], picked.shape[1])
    positions = jnp.arange(blocks * BLOCK).reshape(blocks, BLOCK)
    window_pos = (jnp.arange(blocks) * BLOCK)[:, None] - BLOCK + jnp.arange(2 * BLOCK)[None, :]
    distance = positions[:, :, None] - window_pos[:, None, :]
    near_ok = (window_pos[:, None, :] >= 0) & (distance >= 0) & (distance < WINDOW) & ((window_pos[:, None, :] < length) | (distance == 0))
    far_ok = (picked[:, :, None, :] <= positions[None, :, :, None] - WINDOW) & (picked[:, :, None, :] < length)
    near_all = jnp.broadcast_to(near_ok[None], (head_count, blocks, BLOCK, 2 * BLOCK))
    return jnp.concatenate([near_all, far_ok], axis=3)

def attention_half(normed, qkv_layer, qv_layer, score_layer, picked, length):
    token_count = normed.shape[0]
    head_count, blocks = (picked.shape[0], picked.shape[1])
    projected = jnp.einsum('sd,dcf->scf', normed, qkv_layer, precision=lax.Precision.HIGHEST)
    queries = low(low_back(projected[:, 0] + qv_layer[0]))
    key_rows = low(low_back(projected[:, 1]))
    values = low(low_back(projected[:, 2] + qv_layer[1]))
    scores = matmul(normed, score_layer)
    gates = jax.nn.log_sigmoid(scores)
    head_range = jnp.arange(head_count)[:, None, None]
    query_blocks = split_heads(queries, head_count).reshape(head_count, blocks, BLOCK, -1)
    key_set = gather_keys(split_heads(key_rows, head_count), picked)
    value_set = gather_keys(split_heads(values, head_count), picked)
    gate_pick = jnp.transpose(gates)[head_range, picked]
    logits = jnp.einsum('hbqe,hbke->hbqk', query_blocks, key_set, precision=lax.Precision.HIGHEST) * 0.125
    gate_bias = jnp.concatenate([jnp.zeros((head_count, blocks, 2 * BLOCK), jnp.float32), gate_pick], axis=2)
    logits = low_back(logits + gate_bias[:, :, None, :])
    masked = jnp.where(allowed_mask(picked, length), logits, -1e+30)
    raised = jnp.exp(masked - lax.optimization_barrier(jnp.max(masked, axis=3, keepdims=True)))
    probs_low = low(raised / lax.optimization_barrier(jnp.sum(raised, axis=3, keepdims=True)))
    mixed = jnp.einsum('hbqk,hbke->hbqe', probs_low, value_set, precision=lax.Precision.HIGHEST)
    merged = mixed.reshape(head_count, token_count, -1).transpose(1, 0, 2).reshape(token_count, -1)
    return low(low_back(merged))

def forward_sequence(sequence, picked, length, parameters):
    norm_gain, norm_bias, out_bias, weight_qkv, bias_qv, weight_score, weight_out, weight_fc, bias_fc, weight_proj = parameters
    state = low_back(sequence)
    for sublayer in range(HALVES):
        layer_index = sublayer // 2
        normed = low(normalize(state, norm_gain[sublayer], norm_bias[sublayer]))
        if sublayer % 2 == 0:
            merged = attention_half(normed, weight_qkv[layer_index], bias_qv[layer_index], weight_score[layer_index], picked, length)
            branch = matmul(merged, weight_out[layer_index])
        else:
            preact = low_back(matmul(normed, weight_fc[layer_index]) + bias_fc[layer_index])
            hidden = low(jax.nn.gelu(preact, approximate=True))
            branch = matmul(hidden, weight_proj[layer_index])
        state = low(low_back(state + branch + out_bias[sublayer]))
    return state

def reference(stream, cotangent, lengths, picks, norm_gain, norm_bias, out_bias, weight_qkv, bias_qv, weight_score, weight_out, weight_fc, bias_fc, weight_proj):
    parameters = tuple((argument_item.astype(jnp.float32) for argument_item in (norm_gain, norm_bias, out_bias, weight_qkv, bias_qv, weight_score, weight_out, weight_fc, bias_fc, weight_proj)))

    def whole(inputs, weights):

        def single(packed):
            sequence, picked, length = packed
            return forward_sequence(sequence, picked, length, weights)
        return lax.map(jax.checkpoint(single), (inputs, picks, lengths))
    result, backward = jax.vjp(whole, stream.astype(jnp.float32), parameters)
    grad_stream, grads = backward(cotangent.astype(jnp.float32))
    return (result.astype(jnp.bfloat16), grad_stream.astype(jnp.bfloat16), grads[0], grads[1], grads[2], grads[3], grads[4], grads[5], grads[6], grads[7], grads[8], grads[9])
```

```python
import types

import jax
import jax.numpy as jnp
from jax import lax
from jax.experimental import pallas as pl
from jax.experimental.pallas import tpu as pltpu
from jax.sharding import PartitionSpec as P

MESH = pl.DeviceIdType.MESH
BLOCK = 128
WINDOW = 64
NT = (((1,), (1,)), ((), ()))
TN = (((0,), (0,)), ((), ()))
F32 = jnp.float32
BF16 = jnp.bfloat16
ROOT = 0.7978845608028654
CUBE = 0.044715


def dot(left, right, dims=(((1,), (0,)), ((), ()))):
    return lax.dot_general(left, right, dims, preferred_element_type=F32)


def lanes(shape):
    return lax.broadcasted_iota(jnp.int32, shape, len(shape) - 1)


def rows_of(shape):
    return lax.broadcasted_iota(jnp.int32, shape, len(shape) - 2)


def pieces(value, lane):
    high = value.astype(BF16)
    rest = value - high.astype(F32)
    middle = rest.astype(BF16)
    low = (rest - middle.astype(F32)).astype(BF16)
    zero = jnp.zeros_like(high)
    return jnp.where(
        lane == 64, high, jnp.where(lane == 65, middle, jnp.where(lane == 66, low, zero))
    )


def make_kernel(names, micro, part_rows):
    def kernel(*refs):
        r = types.SimpleNamespace(**dict(zip(names, refs)))
        halves = ((r.xo_f, r.xi_f), (r.xo_a, r.xi_a))
        shares = ((r.yo_f, r.yi_f), (r.yo_a, r.yi_a))
        s, h, dp = lax.axis_index("section"), lax.axis_index("head"), lax.axis_index("dp")
        d = lax.rem(dp, 2)
        pair = dp - d
        mid = (h == 1) | (h == 2)
        mate = h + 1 - 2 * lax.rem(h, 2)
        other = 3 - h
        owner = lax.div(s, micro)
        slot = lax.rem(s, micro)

        def at(section, head, core):
            return (section, head, pair + core)

        def remote(src, dst, send, recv, device):
            return pltpu.make_async_remote_copy(
                src_ref=src,
                dst_ref=dst,
                send_sem=send,
                recv_sem=recv,
                device_id=device,
                device_id_type=MESH,
            )

        partner = at(s, h, 1 - d)
        mate_id = at(s, mate, d)
        other_id = at(s, other, d)

        def arrived(dst, recv):
            remote(dst, dst, recv, recv, partner).wait_recv()

        r.small[...] = jnp.zeros_like(r.small)

        barrier = pltpu.get_barrier_semaphore()
        flat = (s * 4 + h) * 2 + d

        def greet(step, carry):
            whom = lax.rem(flat + step, 32)
            pl.semaphore_signal(
                barrier,
                inc=1,
                device_id=at(lax.div(whom, 8), lax.rem(lax.div(whom, 2), 4), lax.rem(whom, 2)),
                device_id_type=MESH,
            )
            return carry

        lax.fori_loop(1, 32, greet, 0)
        pl.semaphore_wait(barrier, 31)

        def spread(source, landing, part, first, count, sends, recvs):
            copies = []
            for hm in (1, 2):
                for core in (0, 1):
                    src = source.at[slot, pl.ds(first, count), core]
                    dst = landing.at[h, pl.ds(first, count)]
                    copies.append(
                        (
                            (h == hm) & (d == core),
                            pltpu.make_async_copy(src, dst, recvs.at[h, part]),
                            remote(
                                src,
                                dst,
                                sends.at[(hm - 1) * 2 + core, part],
                                recvs.at[h, part],
                                at(s, hm, core),
                            ),
                        )
                    )
            return copies

        def launch(copies):
            for own, local, far in copies:
                pl.when(own)(local.start)
                pl.when(jnp.logical_not(own))(far.start)

        def sent(copies):
            for own, local, far in copies:
                pl.when(jnp.logical_not(own))(far.wait_send)

        chunks = 4
        first_parts = [
            spread(r.stream, r.stream_in, 0, 0, 1, r.xs_s, r.xs_r),
            spread(r.stream, r.stream_in, 1, 1, chunks - 1, r.xs_s, r.xs_r),
            spread(r.cot, r.cot_in, 0, 0, chunks, r.xc_s, r.xc_r),
        ]
        norm_rows = []
        for step in range(4):
            section = lax.rem(s + step, 4)
            for hm in (1, 2):
                norm_rows.append(
                    (
                        (h == hm) if step == 0 else (h == 4),
                        pltpu.make_async_copy(
                            r.prm, r.prm_in.at[s, h], r.prm_r.at[s, h]
                        ),
                        remote(
                            r.prm,
                            r.prm_in.at[s, h],
                            r.prm_s.at[step, hm - 1],
                            r.prm_r.at[s, h],
                            at(section, hm, d),
                        ),
                    )
                )
        pick_copies = []
        for number, (source, landing) in enumerate(((r.pk, r.pk_in), (r.pt, r.pt_in))):
            pick_copies.append(
                (
                    pltpu.make_async_copy(source, landing.at[d], r.pick_l.at[number]),
                    remote(
                        source,
                        landing.at[d],
                        r.pick_s.at[number],
                        r.pick_r.at[number],
                        partner,
                    ),
                )
            )

        launch(norm_rows)

        @pl.when(d == owner)
        def _():
            launch(first_parts[0])
            launch(first_parts[1])

        for local, far in pick_copies:
            local.start()
            far.start()

        @pl.when(d == owner)
        def _():
            launch(first_parts[2])

        r.keyset[...] = jnp.zeros_like(r.keyset)
        r.kvg[:, 0:WINDOW] = jnp.zeros((6, WINDOW, 256), BF16)

        lane = lanes((BLOCK, 128))
        ones_tile = jnp.where((lane >= 64) & (lane < 67), 1.0, 0.0).astype(BF16)

        def norm_parts(x):
            center = x - jnp.mean(x, axis=-1, keepdims=True)
            inverse = lax.rsqrt(jnp.mean(center * center, axis=-1, keepdims=True) + 1e-05)
            return center * inverse, inverse

        def prepare():
            for c in range(4):
                for j in range(4):
                    arrived(r.prm_in.at[c, j], r.prm_r.at[c, j])
            for c in range(4):
                mine = r.prm_in[c, h].astype(F32)
                bias = mine[2:3, :] * 0.0
                for j in range(4):
                    bias = bias + r.prm_in[c, j].astype(F32)[2:3, :]
                r.par[c, 0:1] = mine[0:1]
                r.par[c, 1:2] = mine[1:2]
                r.par[c, 2:3] = bias

        def publish(c, k, state):
            r.state[c * 4 + k] = state
            scaled, _ = norm_parts(state.astype(F32))
            normed = scaled * r.par[c, 0:1] + r.par[c, 1:2]
            r.normed[c * 4 + k] = normed.astype(BF16)
            send_normed(c, k).start()

        def send_normed(c, k):
            n = c * 4 + k
            return remote(
                r.normed.at[c * 4 + k],
                r.normed.at[c * 4 + k],
                r.nx_s.at[n],
                r.nx_r.at[n],
                mate_id,
            )

        def enter(k):
            @pl.when(k == 0)
            def _():
                prepare()
                for j in range(4):
                    arrived(r.stream_in.at[j, pl.ds(0, 1)], r.xs_r.at[j, 0])

            @pl.when(k == 1)
            def _():
                for j in range(4):
                    arrived(r.stream_in.at[j, pl.ds(1, chunks - 1)], r.xs_r.at[j, 1])

            publish(0, k, jnp.concatenate([r.stream_in[j, k] for j in range(4)], axis=1))

        def project(l, k):
            x = r.normed[8 * l + k]
            block = 2 * k + d
            place = pl.ds(pl.multiple_of(WINDOW + block * BLOCK, WINDOW), BLOCK)
            for hh in range(3):
                out = dot(x, r.w1[l, :, hh * 256 : hh * 256 + 256])
                out = out + r.bq[l, :, hh * 256 : hh * 256 + 256]
                q, kv = out[:, :128], out[:, 128:]
                r.q[(l * 4 + k) * 3 + hh] = jnp.where(lane < 64, q, 0.0).astype(BF16) * jnp.asarray(
                    0.125, BF16
                )
                gates = jnp.minimum(q, 0.0) - jnp.log1p(jnp.exp(-jnp.abs(q)))
                r.sig[(l * 4 + k) * 3 + hh] = 1.0 / (1.0 + jnp.exp(q))
                r.kvg[l * 3 + hh, place, 0:128] = kv.astype(BF16)
                r.kvg[l * 3 + hh, place, 128:256] = pieces(gates, lane)
            send_kv(l, k).start()

        def send_kv(l, k):
            place = pl.ds(pl.multiple_of(WINDOW + (2 * k + d) * BLOCK, WINDOW), BLOCK)
            rows = r.kvg.at[pl.ds(l * 3, 3), place]
            return remote(rows, rows, r.kv_s.at[l * 4 + k], r.kv_r.at[l * 4 + k], partner)

        def wait_kv(l, k):
            place = pl.ds(pl.multiple_of(WINDOW + (2 * k + 1 - d) * BLOCK, WINDOW), BLOCK)
            arrived(r.kvg.at[pl.ds(l * 3, 3), place], r.kv_r.at[l * 4 + k])

        def attend(l, k):
            block = 2 * k + d
            start = block * BLOCK
            length = r.pk_in[owner, slot, 24:25, 128:384]
            column = lanes((BLOCK, 256))
            row = rows_of((BLOCK, 256))
            for hh in range(3):
                index = hh * 8 + block
                pick_col = jnp.sum(
                    jnp.where(lanes((64, 128)) == index, r.pt_in[owner, slot], 0.0),
                    axis=1,
                    keepdims=True,
                ).astype(jnp.int32)

                def gather(j, total):
                    hot = (lanes((64, 256)) + j * 256 == pick_col).astype(F32).astype(BF16)
                    rows = pl.ds(pl.multiple_of(WINDOW + j * 256, WINDOW), 256)
                    return total + dot(hot, r.kvg[l * 3 + hh, rows, :])

                chosen = lax.fori_loop(0, k + 1, gather, jnp.zeros((64, 256), F32)).astype(BF16)
                r.chosen[(l * 4 + k) * 3 + hh] = chosen[:, 0:128]
                near = pl.ds(pl.multiple_of(start, BLOCK), 192)
                r.keyset[0:192, 0:128] = r.kvg[l * 3 + hh, near, 0:128]
                r.keyset[192:256, :] = chosen
                query = jnp.concatenate([r.q[(l * 4 + k) * 3 + hh], ones_tile], axis=1)
                logits = dot(query, r.keyset[...], NT)
                pick_row = r.pk_in[owner, slot, pl.ds(index, 1), 128:384]
                distance = row + WINDOW - column
                near_pos = start - WINDOW + column
                near_ok = (
                    (near_pos >= 0)
                    & (distance >= 0)
                    & (distance < WINDOW)
                    & ((near_pos < length) | (distance == 0))
                )
                far_ok = (pick_row <= start - WINDOW + row) & (pick_row < length)
                allowed = ((column < 192) & near_ok) | ((column >= 192) & far_ok)
                masked = jnp.where(allowed, logits, -1e30)
                raised = jnp.exp(masked - jnp.max(masked, axis=1, keepdims=True))
                soft = raised / jnp.sum(raised, axis=1, keepdims=True)
                r.soft[(l * 4 + k) * 3 + hh] = soft
                mixed = dot(soft.astype(BF16), r.keyset[:, 0:128])
                r.merged[l * 4 + k, :, hh * 128 : hh * 128 + 128] = mixed.astype(BF16)
            return dot(r.merged[l * 4 + k], r.wo[l])

        def feed(l, k):
            pre = dot(r.normed[8 * l + 4 + k], r.fc[l]) + r.fcb[l]
            square = pre * pre
            wave = jnp.tanh(ROOT * pre * (1.0 + CUBE * square))
            half = 0.5 * (1.0 + wave)
            slope = half + 0.5 * pre * (1.0 - wave * wave) * (ROOT * (1.0 + 3.0 * CUBE * square))
            r.hidden[l * 4 + k] = (pre * half).astype(BF16)
            r.slope[l * 4 + k] = slope.astype(BF16)
            return dot(r.hidden[l * 4 + k], r.pj[l])

        def send_part(n):
            return remote(
                r.part_out.at[lax.rem(n, 4)],
                r.part_in.at[lax.rem(n, 8)],
                r.ps_s.at[n],
                r.ps_r.at[n],
                mate_id,
            )

        def give(n, part):
            @pl.when(mid)
            def _():
                r.own[lax.rem(n, 4)] = part

            @pl.when(jnp.logical_not(mid))
            def _():
                @pl.when(n >= 4)
                def _():
                    send_part(n - 4).wait_send()

                r.part_out[lax.rem(n, 4)] = part.astype(BF16)
                send_part(n).start()

        def send_pair(n):
            return remote(
                r.pair_out.at[lax.rem(n, 4)],
                r.pair_in.at[lax.rem(n, 8)],
                r.mm_s.at[n],
                r.mm_r.at[n],
                other_id,
            )

        def fold(n):
            arrived(r.part_in.at[lax.rem(n, 8)], r.ps_r.at[n])

            @pl.when(n >= 4)
            def _():
                send_pair(n - 4).wait_send()

            both = r.own[lax.rem(n, 4)] + r.part_in[lax.rem(n, 8)].astype(F32)
            r.pair_out[lax.rem(n, 4)] = both.astype(BF16)
            send_pair(n).start()

        def total_of(n):
            arrived(r.pair_in.at[lax.rem(n, 8)], r.mm_r.at[n])
            return r.pair_out[lax.rem(n, 4)].astype(F32) + r.pair_in[
                lax.rem(n, 8)
            ].astype(F32)

        y_way = (r.y, r.y_stage, r.y_s, r.y_r)
        dx_way = (r.dx, r.dx_stage, r.dx_s, r.dx_r)

        def hand_out(way, k, value):
            for hm in (1, 2):

                @pl.when(h == hm)
                def _():
                    for side in (0, 1):
                        target = 2 * (hm - 1) + side
                        way[1][k, side] = value[:, target * 192 : target * 192 + 192]

            for side in (0, 1):
                target = 2 * (h - 1) + side
                own = (k == s) & (target == h) & (d == owner)
                local, far = hand_copy(way, k, side)
                pl.when(own)(local.start)
                pl.when(jnp.logical_not(own))(far.start)

        def hand_copy(way, k, side):
            src = way[1].at[k, side]
            dst = way[0].at[slot, pl.ds(pl.multiple_of(d * BLOCK, BLOCK), BLOCK)]
            recv = way[3].at[slot, d]
            return (
                pltpu.make_async_copy(src, dst, recv),
                remote(
                    src, dst, way[2].at[k, side], recv, at(k, 2 * (h - 1) + side, owner)
                ),
            )

        def finish_hand(way):
            @pl.when(mid)
            def _():
                for k in range(chunks):
                    for side in (0, 1):
                        own = (k == s) & (2 * (h - 1) + side == h) & (d == owner)
                        pl.when(jnp.logical_not(own))(hand_copy(way, k, side)[1].wait_send)

            for j in range(micro):
                for core in (0, 1):
                    arrived(
                        way[0].at[j, core * BLOCK : core * BLOCK + BLOCK],
                        way[3].at[j, core],
                    )

        def leave(n):
            c, k = lax.div(n, 4), lax.rem(n, 4)
            state = (r.state[n].astype(F32) + total_of(n) + r.par[c, 2:3]).astype(BF16)

            @pl.when(c < 3)
            def _():
                publish(c + 1, k, state)

            @pl.when(c == 3)
            def _():
                hand_out(y_way, k, state)

        def send_grad(index):
            return remote(
                r.grad.at[index],
                r.grad.at[index],
                r.gx_s.at[index],
                r.gx_r.at[index],
                mate_id,
            )

        def enter_back(k):
            @pl.when(k == 3)
            def _():
                for j in range(4):
                    arrived(r.cot_in.at[j], r.xc_r.at[j, 0])

            r.grad[12 + k] = jnp.concatenate([r.cot_in[j, k] for j in range(4)], axis=1)
            send_grad(12 + k).start()

        def add_row(row, value):
            place = pl.ds(row, 1)
            r.small[place, :] = r.small[place, :] + value

        def leave_back(m):
            c, k = 3 - lax.div(m, 4), 3 - lax.rem(m, 4)
            index = c * 4 + k
            total = total_of(16 + m)
            scaled, inverse = norm_parts(r.state[index].astype(F32))
            above = r.grad[index].astype(F32)
            add_row(c * 3, jnp.sum(total * scaled, axis=0, keepdims=True))
            add_row(c * 3 + 1, jnp.sum(total, axis=0, keepdims=True))
            add_row(c * 3 + 2, jnp.sum(above, axis=0, keepdims=True))
            t = total * r.par[c, 0:1]
            inner = (
                t
                - jnp.mean(t, axis=-1, keepdims=True)
                - scaled * jnp.mean(t * scaled, axis=-1, keepdims=True)
            )
            below = (above + inverse * inner).astype(BF16)

            @pl.when(c > 0)
            def _():
                r.grad[index - 4] = below
                send_grad(index - 4).start()

            @pl.when(c == 0)
            def _():
                hand_out(dx_way, k, below)

        def send_keys(l, step):
            ring = lax.rem(step, 2) * 3
            return remote(
                r.sums.at[pl.ds(ring, 3), pl.ds(pl.multiple_of((1 - d) * BLOCK, BLOCK), BLOCK)],
                r.sums_in.at[pl.ds(ring, 3)],
                r.dk_s.at[l * 4 + step],
                r.dk_r.at[l * 4 + step],
                partner,
            )

        def attend_back(l, k):
            step = 3 - k
            ring = lax.rem(step, 2) * 3
            start = (2 * k + d) * BLOCK
            grad_merged = dot(r.grad[8 * l + k], r.wo[l], NT).astype(BF16)

            @pl.when(step == 0)
            def _():
                r.near[...] = jnp.zeros_like(r.near)

            @pl.when(step >= 2)
            def _():
                send_keys(l, step - 2).wait_send()

            for hh in range(3):
                where = (l * 4 + k) * 3 + hh
                near = pl.ds(pl.multiple_of(start, BLOCK), 192)
                r.keyset[0:192, 0:128] = r.kvg[l * 3 + hh, near, 0:128]
                r.keyset[192:256, 0:128] = r.chosen[where]
                keys = r.keyset[:, 0:128]
                mixed = grad_merged[:, hh * 128 : hh * 128 + 128]
                soft = r.soft[where]
                grad_soft = dot(mixed, keys, NT)
                grad_logits = (
                    soft * (grad_soft - jnp.sum(grad_soft * soft, axis=1, keepdims=True))
                ).astype(BF16)
                grad_query = dot(grad_logits, keys) * 0.125
                r.dqkv[k, :, hh * 256 : hh * 256 + 128] = jnp.where(
                    lane < 64, grad_query, 0.0
                ).astype(BF16)
                left = jnp.concatenate([grad_logits, soft.astype(BF16)], axis=0)
                right = jnp.concatenate(
                    [
                        jnp.concatenate([r.q[where], ones_tile], axis=1),
                        jnp.concatenate([mixed, jnp.zeros_like(ones_tile)], axis=1),
                    ],
                    axis=0,
                )
                grad_set = dot(left, right, TN)
                r.near[hh, near, :] = r.near[hh, near, :] + grad_set[0:192, 0:128]
                far = grad_set[192:256]
                high = far.astype(BF16)
                r.far[hh * 4 + k, 0:64] = high
                r.far[hh * 4 + k, 64:128] = (far - high.astype(F32)).astype(BF16)

                def scatter(kk, total):
                    pick_row = r.pk_in[owner, slot, pl.ds(hh * 8 + 2 * kk + d, 1), :][:, 0:128]
                    hot = (rows_of((256, 128)) + k * 256 == pick_row).astype(F32).astype(BF16)
                    return total + dot(hot, r.far[hh * 4 + kk])

                total = lax.fori_loop(k, 4, scatter, jnp.zeros((256, 256), F32))
                rows = pl.ds(pl.multiple_of(WINDOW + k * 256, WINDOW), 256)
                r.sums[ring + hh, :, 0:128] = total[:, 0:128] + r.near[hh, rows, :]
                r.sums[ring + hh, :, 128:256] = total[:, 128:256]
            send_keys(l, step).start()

        def finish_back(l, k):
            step = 3 - k
            ring = lax.rem(step, 2) * 3
            arrived(r.sums_in.at[pl.ds(ring, 3)], r.dk_r.at[l * 4 + step])
            mine = pl.ds(pl.multiple_of(d * BLOCK, BLOCK), BLOCK)
            for hh in range(3):
                own = r.sums[ring + hh, mine, :] + r.sums_in[ring + hh]
                scores = own[:, 128:256] * r.sig[(l * 4 + k) * 3 + hh]
                head = slice(hh * 256, hh * 256 + 128)
                r.dqkv[k, :, head] = jnp.where(
                    lane < 64, r.dqkv[k, :, head], pieces(scores, lane)
                )
                r.dqkv[k, :, hh * 256 + 128 : hh * 256 + 256] = own[:, 0:128].astype(BF16)
            return dot(r.dqkv[k], r.w1[l], NT)

        def feed_back(l, k):
            grad_hidden = dot(r.grad[8 * l + 4 + k], r.pj[l], NT)
            grad_pre = (grad_hidden * r.slope[l * 4 + k].astype(F32)).astype(BF16)
            r.dpre[k] = grad_pre
            return dot(grad_pre, r.fc[l], NT)

        def four(ref, first):
            value = ref[pl.ds(first, 4)]
            return value.reshape(4 * BLOCK, value.shape[2])

        ones_rows = jnp.ones((8, 4 * BLOCK), BF16)

        def split(kind, width):
            for section in range(4):
                rows = pl.ds(pl.multiple_of((2 * section + 1 - d) * part_rows, 8), part_rows)
                halves[kind][0][section] = r.wide[rows, 0:width].astype(BF16)
            send_half(kind).start()

        def send_half(kind):
            return remote(
                halves[kind][0],
                halves[kind][1],
                r.xh_s.at[kind],
                r.xh_r.at[kind],
                partner,
            )

        def send_share(kind, step):
            return remote(
                shares[kind][0].at[step - 1],
                shares[kind][1].at[step - 1],
                r.yh_s.at[kind, step - 1],
                r.yh_r.at[kind, step - 1],
                at(lax.rem(s + step, 4), h, d),
            )

        def share(kind, width):
            arrived(halves[kind][1], r.xh_r.at[kind])
            send_half(kind).wait_send()
            for step in (1, 2, 3, 0):
                section = lax.rem(s + step, 4)
                rows = pl.ds(pl.multiple_of((2 * section + d) * part_rows, 8), part_rows)
                both = r.wide[rows, 0:width] + halves[kind][1][section].astype(F32)
                if step:
                    shares[kind][0][step - 1] = both.astype(BF16)
                    send_share(kind, step).start()
                else:
                    r.wide[rows, 0:width] = both

        def collect(kind, width):
            rows = pl.ds(pl.multiple_of((2 * s + d) * part_rows, 8), part_rows)
            total = r.wide[rows, 0:width]
            for step in (1, 2, 3):
                arrived(shares[kind][1].at[step - 1], r.yh_r.at[kind, step - 1])
                total = total + shares[kind][1][step - 1].astype(F32)
                send_share(kind, step).wait_send()
            return total

        def weights_feed(l):
            x, g = four(r.normed, 8 * l + 4), four(r.grad, 8 * l + 4)
            grad_pre = four(r.dpre, 0)
            r.wide[:, 0:768] = dot(x, grad_pre, TN)
            r.wide[:, 768:1536] = dot(g, four(r.hidden, 4 * l), TN)
            add_row(18 + l, dot(ones_rows, grad_pre)[0:1])
            split(0, 1536)

        def weights_attend(l):
            for step in (2, 3):
                send_keys(l, step).wait_send()
            x, g = four(r.normed, 8 * l), four(r.grad, 8 * l)
            grads, merged = four(r.dqkv, 0), four(r.merged, 4 * l)
            wide_lane = lanes((4 * BLOCK, 128))
            t = [grads[:, i * 256 : i * 256 + 128].astype(F32) for i in range(3)]
            first = jnp.where(wide_lane < 64, t[0], pltpu.roll(t[1], 64, 1))
            second = (
                t[2]
                + pltpu.roll(jnp.where(wide_lane < 64, 0.0, t[0]), 3, 1)
                + pltpu.roll(jnp.where(wide_lane < 64, 0.0, t[1]), 6, 1)
            ).astype(BF16)
            packed = jnp.concatenate(
                [first.astype(BF16), second]
                + [grads[:, i * 256 + 128 : i * 256 + 256] for i in range(3)],
                axis=1,
            )
            r.wide[:, 0:640] = dot(x, packed, TN)
            u = [merged[:, i * 128 : i * 128 + 128].astype(F32) for i in range(3)]
            packed = jnp.concatenate(
                [
                    jnp.where(wide_lane < 64, pltpu.roll(u[0], 64, 1), u[1]),
                    jnp.where(wide_lane < 64, pltpu.roll(u[2], 64, 1), 0.0),
                ],
                axis=1,
            ).astype(BF16)
            r.wide[:, 640:896] = dot(g, packed, TN)
            scores = dot(second, x, TN)
            for hh, row in ((0, 67), (1, 70), (2, 64)):
                add_row(
                    24 + 4 * l + hh, scores[row : row + 1] + scores[row + 1 : row + 2] + scores[row + 2 : row + 3]
                )
            add_row(16 + l, dot(ones_rows, grads)[0:1])
            split(1, 896)

        def collect_feed(l):
            total = collect(0, 1536)
            r.o_fc[l] = total[:, 0:768]
            r.o_pj[l] = total[:, 768:1536]

        def collect_attend(l):
            total = collect(1, 896)
            r.o_qkv[3 * l] = total[:, 0:192]
            for i in (0, 1):
                r.o_qkv[3 * l + 1 + i] = jnp.concatenate(
                    [total[:, 256 + 128 * j + 64 * i : 320 + 128 * j + 64 * i] for j in range(3)],
                    axis=1,
                )
            r.o_out[l] = total[:, 640:832]

        def slot_of(n, carry):
            ahead = n < 16
            c = jnp.where(ahead, lax.div(n, 4), 7 - lax.div(n, 4))
            k = jnp.where(ahead, lax.rem(n, 4), 3 - lax.rem(n, 4))
            l = lax.div(c, 2)
            works = n < 32
            attends = lax.rem(c, 2) == 0

            @pl.when(mid & (n < 4))
            def _():
                enter(n)

            @pl.when(mid & (n >= 4) & (n < 20))
            def _():
                leave(n - 4)

            @pl.when(mid & (n >= 12) & (n < 16))
            def _():
                enter_back(15 - n)

            @pl.when(mid & (n >= 20))
            def _():
                leave_back(n - 20)

            @pl.when(jnp.logical_not(mid) & ahead)
            def _():
                arrived(r.normed.at[n], r.nx_r.at[n])

            @pl.when(jnp.logical_not(mid) & jnp.logical_not(ahead) & works)
            def _():
                arrived(r.grad.at[c * 4 + k], r.gx_r.at[c * 4 + k])

            @pl.when(ahead & attends)
            def _():
                project(l, k)

            @pl.when(n == 0)
            def _():
                for local, far in pick_copies:
                    local.wait()
                    far.wait()

            @pl.when(ahead & attends)
            def _():
                wait_kv(l, k)
                give(n, attend(l, k))

            @pl.when(ahead & jnp.logical_not(attends))
            def _():
                give(n, feed(l, k))

            @pl.when(jnp.logical_not(ahead) & works & attends)
            def _():
                attend_back(l, k)
                give(n, finish_back(l, k))

            @pl.when(jnp.logical_not(ahead) & works & jnp.logical_not(attends))
            def _():
                give(n, feed_back(l, k))

            @pl.when(mid & (n >= 2) & (n < 34))
            def _():
                fold(n - 2)

            @pl.when((n == 21) | (n == 29))
            def _():
                share(0, 1536)

            @pl.when((n == 25) | (n == 33))
            def _():
                share(1, 896)

            @pl.when((n == 23) | (n == 31))
            def _():
                collect_feed(lax.div(31 - n, 8))

            @pl.when((n == 27) | (n == 35))
            def _():
                collect_attend(lax.div(35 - n, 8))

            @pl.when((n == 19) | (n == 27))
            def _():
                weights_feed(l)

            @pl.when((n == 23) | (n == 31))
            def _():
                weights_attend(l)

            return carry

        lax.fori_loop(0, 36, slot_of, 0)

        def send_rows():
            return remote(
                r.small.at[0:16],
                r.small.at[0:16],
                r.sm_s.at[0],
                r.sm_r.at[0],
                mate_id,
            )

        @pl.when(mid)
        def _():
            send_rows().start()

        @pl.when(jnp.logical_not(mid))
        def _():
            arrived(r.small.at[0:16], r.sm_r.at[0])

        swap = remote(r.small, r.small_in, r.sm_s.at[1], r.sm_r.at[1], partner)
        swap.start()
        swap.wait()
        r.small_all[s] = r.small[...] + r.small_in[...]

        def send_small(step):
            return remote(
                r.small_all.at[s],
                r.small_all.at[s],
                r.sm_s.at[1 + step],
                r.sm_r.at[2 + s],
                at(lax.rem(s + step, 4), h, d),
            )

        for step in (1, 2, 3):
            send_small(step).start()
        for step in (1, 2, 3):
            section = lax.rem(s + step, 4)
            arrived(r.small_all.at[section], r.sm_r.at[2 + section])

        @pl.when(mid)
        def _():
            send_rows().wait_send()

        r.small[...] = (r.small_all[0] + r.small_all[1]) + (
            r.small_all[2] + r.small_all[3]
        )
        for j in range(4):

            @pl.when(h == j)
            def _():
                for i, ref in enumerate((r.o_gain, r.o_bias, r.o_ob)):
                    ref[...] = r.small[pl.ds(s * 3 + i, 1), :][:, j * 192 : j * 192 + 192]

        for l in (0, 1):
            row = r.small[16 + l : 17 + l, :]
            for i in (0, 1):
                r.o_qv[2 * l + i : 2 * l + i + 1, :] = jnp.concatenate(
                    [row[:, j * 256 + 192 * i : j * 256 + 192 * i + 64] for j in range(3)], axis=1
                )
            for j in range(3):
                r.o_score[3 * l + j : 3 * l + j + 1, :] = r.small[
                    24 + 4 * l + j : 25 + 4 * l + j, :
                ]
        r.o_fcb[...] = r.small[18:20, :]

        finish_hand(y_way)
        finish_hand(dx_way)
        for step in (1, 2, 3):
            send_small(step).wait_send()

        @pl.when(d == owner)
        def _():
            for copies in first_parts:
                sent(copies)

        sent(norm_rows)

        def drain_kv(i, carry):
            send_kv(lax.div(i, 4), lax.rem(i, 4)).wait_send()
            return carry

        lax.fori_loop(0, 8, drain_kv, 0)

        @pl.when(mid)
        def _():
            def drain(i, carry):
                send_normed(lax.div(i, 4), lax.rem(i, 4)).wait_send()
                send_grad(i).wait_send()
                return carry

            lax.fori_loop(0, 16, drain, 0)
            for n in range(28, 32):
                send_pair(n).wait_send()

        @pl.when(jnp.logical_not(mid))
        def _():
            for n in range(28, 32):
                send_part(n).wait_send()

    return kernel


def shards(
    stream,
    cotangent,
    lengths,
    picks,
    norm_gain,
    norm_bias,
    out_bias,
    weight_qkv,
    bias_qv,
    weight_score,
    weight_out,
    weight_fc,
    bias_fc,
    weight_proj,
):
    micro, tokens, local = stream.shape
    layers, width = weight_qkv.shape[0], weight_qkv.shape[1]
    h = lax.axis_index("head")
    by_head = weight_qkv.reshape(layers, width, 3, 3, 64)
    q, k, v = by_head[:, :, 0], by_head[:, :, 1], by_head[:, :, 2]
    score = weight_score[:, :, :, None]
    w1 = jnp.concatenate(
        [q, score, score, score, jnp.zeros((layers, width, 3, 61), BF16), k, v], axis=3
    ).reshape(layers, width, 768)
    bq = bias_qv.reshape(layers, 2, 3, 64).astype(F32)
    gap = jnp.zeros((layers, 3, 128), F32)
    bq = jnp.concatenate([bq[:, 0], gap, bq[:, 1]], axis=2).reshape(layers, 1, 768)
    wo = weight_out.reshape(layers, 3, 64, width)
    wo = jnp.concatenate([jnp.zeros_like(wo), wo], axis=2).reshape(layers, 384, width)
    fcb = bias_fc.astype(F32)[:, None, :]
    spread_bias = lax.dynamic_update_slice(jnp.zeros((1, 768), BF16), out_bias, (0, h * local))
    prm = jnp.concatenate([norm_gain, norm_bias, spread_bias, jnp.zeros((13, 768), BF16)], axis=0)
    flat = picks.reshape(micro, 24, 64)
    pk = jnp.concatenate(
        [flat, flat, jnp.zeros((micro, 24, 192), jnp.int32), flat], axis=2
    )
    pk = jnp.concatenate(
        [
            pk,
            jnp.broadcast_to(lengths[:, None, None], (micro, 1, 384)),
            jnp.zeros((micro, 7, 384), jnp.int32),
        ],
        axis=1,
    )
    pt = jnp.concatenate(
        [flat.transpose(0, 2, 1).astype(F32), jnp.zeros((micro, 64, 104), F32)], axis=2
    )
    stream5 = stream.reshape(micro, 4, 2, BLOCK, local)
    cot5 = cotangent.reshape(micro, 4, 2, BLOCK, local)

    inputs = dict(
        stream=stream5,
        cot=cot5,
        pk=pk,
        pt=pt,
        prm=prm,
        w1=w1,
        bq=bq,
        wo=wo,
        fc=weight_fc,
        fcb=fcb,
        pj=weight_proj,
    )
    part_rows = width // 8
    outputs = dict(
        y=((micro, 2 * BLOCK, local), BF16),
        dx=((micro, 2 * BLOCK, local), BF16),
        o_gain=((1, 192), F32),
        o_bias=((1, 192), F32),
        o_ob=((1, 192), F32),
        o_qkv=((6, part_rows, 192), F32),
        o_qv=((4, 192), F32),
        o_score=((6, 768), F32),
        o_out=((2, part_rows, 192), F32),
        o_fc=((2, part_rows, 768), F32),
        o_fcb=((2, 768), F32),
        o_pj=((2, part_rows, 768), F32),
    )
    dma = pltpu.SemaphoreType.DMA
    scratch = dict(
        stream_in=((4, 4, BLOCK, local), BF16),
        cot_in=((4, 4, BLOCK, local), BF16),
        prm_in=((4, 4, 16, 768), BF16),
        par=((4, 8, 768), F32),
        pk_in=((2,) + pk.shape, jnp.int32),
        pt_in=((2,) + pt.shape, F32),
        state=((16, BLOCK, 768), BF16),
        normed=((16, BLOCK, 768), BF16),
        q=((24, BLOCK, 128), BF16),
        sig=((24, BLOCK, 128), F32),
        kvg=((6, WINDOW + tokens, 256), BF16),
        chosen=((24, 64, 128), BF16),
        keyset=((256, 256), BF16),
        soft=((24, BLOCK, 256), F32),
        merged=((8, BLOCK, 384), BF16),
        hidden=((8, BLOCK, 768), BF16),
        slope=((8, BLOCK, 768), BF16),
        part_out=((4, BLOCK, 768), BF16),
        part_in=((8, BLOCK, 768), BF16),
        own=((4, BLOCK, 768), F32),
        pair_out=((4, BLOCK, 768), BF16),
        pair_in=((8, BLOCK, 768), BF16),
        y_stage=((4, 2, BLOCK, local), BF16),
        dx_stage=((4, 2, BLOCK, local), BF16),
        grad=((16, BLOCK, 768), BF16),
        dpre=((4, BLOCK, 768), BF16),
        dqkv=((4, BLOCK, 768), BF16),
        near=((3, WINDOW + tokens, 128), F32),
        far=((12, 128, 256), BF16),
        sums=((6, 256, 256), F32),
        sums_in=((6, BLOCK, 256), F32),
        wide=((768, 1536), F32),
        xo_f=((4, part_rows, 1536), BF16),
        xi_f=((4, part_rows, 1536), BF16),
        yo_f=((3, part_rows, 1536), BF16),
        yi_f=((3, part_rows, 1536), BF16),
        xo_a=((4, part_rows, 896), BF16),
        xi_a=((4, part_rows, 896), BF16),
        yo_a=((3, part_rows, 896), BF16),
        yi_a=((3, part_rows, 896), BF16),
        small=((32, 768), F32),
        small_in=((32, 768), F32),
        small_all=((4, 32, 768), F32),
    )
    sems = dict(
        xs_s=(4, 2),
        xs_r=(4, 2),
        xc_s=(4, 1),
        xc_r=(4, 1),
        prm_s=(4, 2),
        prm_r=(4, 4),
        pick_l=(2,),
        pick_s=(2,),
        pick_r=(2,),
        nx_s=(16,),
        nx_r=(16,),
        kv_s=(8,),
        kv_r=(8,),
        ps_s=(32,),
        ps_r=(32,),
        mm_s=(32,),
        mm_r=(32,),
        y_s=(4, 2),
        y_r=(2, 2),
        dx_s=(4, 2),
        dx_r=(2, 2),
        gx_s=(16,),
        gx_r=(16,),
        dk_s=(8,),
        dk_r=(8,),
        xh_s=(2,),
        xh_r=(2,),
        yh_s=(2, 3),
        yh_r=(2, 3),
        sm_s=(5,),
        sm_r=(6,),
    )
    names = list(inputs) + list(outputs) + list(scratch) + list(sems)
    results = pl.pallas_call(
        make_kernel(names, micro, width // 8),
        out_shape=[jax.ShapeDtypeStruct(*spec) for spec in outputs.values()],
        in_specs=[
            pl.BlockSpec(memory_space=pl.ANY if value.ndim == 5 else pltpu.VMEM)
            for value in inputs.values()
        ],
        out_specs=[pl.BlockSpec(memory_space=pltpu.VMEM) for name in outputs],
        scratch_shapes=[pltpu.VMEM(*spec) for spec in scratch.values()]
        + [dma(shape) for shape in sems.values()],
        compiler_params=pltpu.CompilerParams(
            collective_id=0, has_side_effects=True, vmem_limit_bytes=62 * 2**20
        ),
        name="blocks",
    )(*inputs.values())
    o = types.SimpleNamespace(**dict(zip(outputs, results)))
    dp_count = lax.axis_size("dp")
    if dp_count > 2:
        d = lax.rem(lax.axis_index("dp"), 2)

        def scattered(value):
            placed = jnp.zeros((value.shape[0], 2 * part_rows, value.shape[2]), F32)
            placed = lax.dynamic_update_slice(placed, value, (0, d * part_rows, 0))
            return lax.psum_scatter(placed, "dp", scatter_dimension=1, tiled=True)

        o.o_qkv, o.o_out, o.o_fc, o.o_pj = map(scattered, (o.o_qkv, o.o_out, o.o_fc, o.o_pj))
        sums = (o.o_gain, o.o_bias, o.o_ob, o.o_qv, o.o_score, o.o_fcb)
        o.o_gain, o.o_bias, o.o_ob, o.o_qv, o.o_score, o.o_fcb = jax.tree.map(
            lambda value: 0.5 * value, lax.psum(sums, "dp")
        )
    rows = o.o_fc.shape[1]
    return (
        o.y,
        o.dx,
        o.o_gain,
        o.o_bias,
        o.o_ob,
        o.o_qkv.reshape(layers, 3, rows, 192).transpose(0, 2, 1, 3),
        o.o_qv.reshape(layers, 2, 192),
        o.o_score.reshape(layers, 3, 768).transpose(0, 2, 1),
        o.o_out.transpose(0, 2, 1),
        o.o_fc,
        o.o_fcb,
        o.o_pj.transpose(0, 2, 1),
    )


def solution(mesh):
    return jax.shard_map(
        shards,
        mesh=mesh,
        in_specs=(
            P("dp", None, "head"),
            P("dp", None, "head"),
            P("dp"),
            P("dp", "head", None, None),
            P("section", None),
            P("section", None),
            P("section", "head"),
            P(None, None, None, "head"),
            P(None, None, "head"),
            P(None, None, "head"),
            P(None, "head", None),
            P(None, None, "head"),
            P(None, "head"),
            P(None, "head", None),
        ),
        out_specs=(
            P("dp", "section", "head"),
            P("dp", "section", "head"),
            P("section", "head"),
            P("section", "head"),
            P("section", "head"),
            P(None, ("section", "dp"), None, "head"),
            P(None, None, "head"),
            P(None, None, "head"),
            P(None, "head", ("section", "dp")),
            P(None, ("section", "dp"), "head"),
            P(None, "head"),
            P(None, "head", ("section", "dp")),
        ),
        check_vma=False,
    )
```

```python
import types

import jax
import jax.numpy as jnp
from jax import lax
from jax.experimental import pallas as pl
from jax.experimental.pallas import tpu as pltpu
from jax.sharding import PartitionSpec as P

MESH = pl.DeviceIdType.MESH
BLOCK = 128
WINDOW = 64
NT = (((1,), (1,)), ((), ()))
TN = (((0,), (0,)), ((), ()))
F32 = jnp.float32
BF16 = jnp.bfloat16
ROOT = 0.7978845608028654
CUBE = 0.044715


def dot(left, right, dims=(((1,), (0,)), ((), ()))):
    return lax.dot_general(left, right, dims, preferred_element_type=F32)


def lanes(shape):
    return lax.broadcasted_iota(jnp.int32, shape, len(shape) - 1)


def rows_of(shape):
    return lax.broadcasted_iota(jnp.int32, shape, len(shape) - 2)


def pieces(value, lane):
    high = value.astype(BF16)
    rest = value - high.astype(F32)
    middle = rest.astype(BF16)
    low = (rest - middle.astype(F32)).astype(BF16)
    zero = jnp.zeros_like(high)
    return jnp.where(
        lane == 64, high, jnp.where(lane == 65, middle, jnp.where(lane == 66, low, zero))
    )


def make_kernel(names, micro, part_rows, local):
    def kernel(*refs):
        r = types.SimpleNamespace(**dict(zip(names, refs)))
        halves = ((r.xo_f, r.xi_f), (r.xo_a, r.xi_a))
        shares = ((r.yo_f, r.yi_f), (r.yo_a, r.yi_a))
        s, h, dp = lax.axis_index("section"), lax.axis_index("head"), lax.axis_index("dp")
        d = lax.rem(dp, 2)
        pair = dp - d
        mid = (h == 1) | (h == 2)
        mate = h + 1 - 2 * lax.rem(h, 2)
        other = 3 - h
        owner = lax.div(s, micro)
        slot = lax.rem(s, micro)

        def at(section, head, core):
            return (section, head, pair + core)

        def remote(src, dst, send, recv, device):
            return pltpu.make_async_remote_copy(
                src_ref=src,
                dst_ref=dst,
                send_sem=send,
                recv_sem=recv,
                device_id=device,
                device_id_type=MESH,
            )

        partner = at(s, h, 1 - d)
        mate_id = at(s, mate, d)
        other_id = at(s, other, d)

        def arrived(dst, recv):
            remote(dst, dst, recv, recv, partner).wait_recv()

        r.small[...] = jnp.zeros_like(r.small)
        for j in range(micro):
            r.pk_out[j, 0:24] = r.picks[j]
            r.pk_out[j, 24:32] = jnp.zeros((8, 64), jnp.int32) + r.lengths[j]
        wide_bias = jnp.concatenate([r.ob[...].astype(F32)] * 4, axis=1)
        wide_bias = jnp.where(
            (lanes((1, 768)) >= h * local) & (lanes((1, 768)) < h * local + local), wide_bias, 0.0
        )
        row = rows_of((16, 768))
        r.prm[...] = jnp.where(
            row == 0,
            r.gain[...].astype(F32),
            jnp.where(
                row == 1, r.shift[...].astype(F32), jnp.where(row == 2, wide_bias, 0.0)
            ),
        ).astype(BF16)

        barrier = pltpu.get_barrier_semaphore()
        flat = (s * 4 + h) * 2 + d

        def greet(step, carry):
            whom = lax.rem(flat + step, 32)
            pl.semaphore_signal(
                barrier,
                inc=1,
                device_id=at(lax.div(whom, 8), lax.rem(lax.div(whom, 2), 4), lax.rem(whom, 2)),
                device_id_type=MESH,
            )
            return carry

        lax.fori_loop(1, 32, greet, 0)
        pl.semaphore_wait(barrier, 31)

        def spread(source, landing, sends, recvs, k):
            copies = []
            for hm in (1, 2):
                for core in (0, 1):
                    src = source.at[slot, :, (2 * k + core) * BLOCK : (2 * k + core + 1) * BLOCK]
                    dst = landing.at[k, pl.ds(pl.multiple_of(h * local, local), local)]
                    recv = recvs.at[h, k]
                    copies.append(
                        (
                            (h == hm) & (d == core),
                            pltpu.make_async_copy(src, dst, recv),
                            remote(
                                src, dst, sends.at[(hm - 1) * 2 + core, k], recv, at(s, hm, core)
                            ),
                        )
                    )
            return copies

        def launch(copies):
            for own, local, far in copies:
                pl.when(own)(local.start)
                pl.when(jnp.logical_not(own))(far.start)

        def sent(copies):
            for own, local, far in copies:
                pl.when(jnp.logical_not(own))(far.wait_send)

        chunks = 4
        stream_parts = [spread(r.stream, r.stream_in, r.xs_s, r.xs_r, k) for k in range(chunks)]
        cot_parts = [spread(r.cot, r.cot_in, r.xc_s, r.xc_r, k) for k in range(chunks)]
        norm_rows = []
        for step in range(4):
            section = lax.rem(s + step, 4)
            for hm in (1, 2):
                norm_rows.append(
                    (
                        (h == hm) if step == 0 else (h == 4),
                        pltpu.make_async_copy(
                            r.prm, r.prm_in.at[s, h], r.prm_r.at[s, h]
                        ),
                        remote(
                            r.prm,
                            r.prm_in.at[s, h],
                            r.prm_s.at[step, hm - 1],
                            r.prm_r.at[s, h],
                            at(section, hm, d),
                        ),
                    )
                )
        pick_copies = (
            pltpu.make_async_copy(r.pk_out, r.pk_in.at[d], r.pick_s.at[0]),
            remote(r.pk_out, r.pk_in.at[d], r.pick_s.at[1], r.pick_r.at[0], partner),
        )

        attend_loads, feed_loads = [], []
        for l in range(2):
            for hh in range(3):
                rows = slice(hh * 64, hh * 64 + 64)
                for part, place in ((0, 0), (1, 128), (2, 192)):
                    attend_loads.append(
                        pltpu.make_async_copy(
                            r.wqkv.at[l, part, rows],
                            r.w1.at[l, hh * 256 + place : hh * 256 + place + 64],
                            r.load.at[l],
                        )
                    )
                attend_loads.append(
                    pltpu.make_async_copy(
                        r.wout.at[l, rows],
                        r.wo.at[l, hh * 128 + 64 : hh * 128 + 128],
                        r.load.at[l],
                    )
                )
            feed_loads.append(pltpu.make_async_copy(r.wfc.at[l], r.fc.at[l], r.load.at[2]))
            feed_loads.append(pltpu.make_async_copy(r.wpj.at[l], r.pj.at[l], r.load.at[2]))

        launch(norm_rows)

        @pl.when(d == owner)
        def _():
            for copies in stream_parts:
                launch(copies)

        for copy in pick_copies + tuple(attend_loads) + tuple(feed_loads):
            copy.start()

        @pl.when(d == owner)
        def _():
            for copies in cot_parts:
                launch(copies)

        r.keyset[...] = jnp.zeros_like(r.keyset)
        r.kvg[:, 0:WINDOW] = jnp.zeros((6, WINDOW, 256), BF16)
        for l in range(2):
            for hh in range(3):
                score = jnp.where(
                    rows_of((64, 768)) < 3, r.wscore[hh, l : l + 1, :].astype(F32), 0.0
                )
                r.w1[l, hh * 256 + 64 : hh * 256 + 128] = score.astype(BF16)
                r.wo[l, hh * 128 : hh * 128 + 64] = jnp.zeros((64, 768), BF16)
            gap = jnp.zeros((1, 128), F32)
            r.fcb[l] = r.bfc[l : l + 1, :].astype(F32)
            bias = r.bqv[l].astype(F32)
            r.bq[l] = jnp.concatenate(
                [
                    piece
                    for hh in range(3)
                    for piece in (
                        bias[0:1, hh * 64 : hh * 64 + 64],
                        gap,
                        bias[1:2, hh * 64 : hh * 64 + 64],
                    )
                ],
                axis=1,
            )

        lane = lanes((BLOCK, 128))
        ones_tile = jnp.where((lane >= 64) & (lane < 67), 1.0, 0.0).astype(BF16)

        def norm_parts(x):
            center = x - jnp.mean(x, axis=-1, keepdims=True)
            inverse = lax.rsqrt(jnp.mean(center * center, axis=-1, keepdims=True) + 1e-05)
            return center * inverse, inverse

        def prepare():
            for c in range(4):
                for j in range(4):
                    arrived(r.prm_in.at[c, j], r.prm_r.at[c, j])
            for c in range(4):
                mine = r.prm_in[c, h].astype(F32)
                bias = mine[2:3, :] * 0.0
                for j in range(4):
                    bias = bias + r.prm_in[c, j].astype(F32)[2:3, :]
                r.par[c, 0:1] = mine[0:1]
                r.par[c, 1:2] = mine[1:2]
                r.par[c, 2:3] = bias

        def publish(c, k, state):
            r.state[c * 4 + k] = state
            scaled, _ = norm_parts(state.astype(F32))
            normed = scaled * r.par[c, 0:1] + r.par[c, 1:2]
            r.normed[c * 4 + k] = normed.astype(BF16)
            send_normed(c, k).start()

        def send_normed(c, k):
            n = c * 4 + k
            return remote(
                r.normed.at[c * 4 + k],
                r.normed.at[c * 4 + k],
                r.nx_s.at[n],
                r.nx_r.at[n],
                mate_id,
            )

        def turned(landing, recvs, k):
            for j in range(4):
                arrived(landing.at[k, j * local : j * local + local], recvs.at[j, k])
            return landing[k].astype(F32).T.astype(BF16)

        def enter(k):
            @pl.when(k == 0)
            def _():
                prepare()

            publish(0, k, turned(r.stream_in, r.xs_r, k))

        def project(l, k):
            x = r.normed[8 * l + k]
            block = 2 * k + d
            place = pl.ds(pl.multiple_of(WINDOW + block * BLOCK, WINDOW), BLOCK)
            for hh in range(3):
                out = dot(x, r.w1[l, hh * 256 : hh * 256 + 256, :], NT)
                out = out + r.bq[l, :, hh * 256 : hh * 256 + 256]
                q, kv = out[:, :128], out[:, 128:]
                r.q[(l * 4 + k) * 3 + hh] = jnp.where(lane < 64, q, 0.0).astype(BF16) * jnp.asarray(
                    0.125, BF16
                )
                gates = jnp.minimum(q, 0.0) - jnp.log1p(jnp.exp(-jnp.abs(q)))
                r.sig[(l * 4 + k) * 3 + hh] = 1.0 / (1.0 + jnp.exp(q))
                r.kvg[l * 3 + hh, place, 0:128] = kv.astype(BF16)
                r.kvg[l * 3 + hh, place, 128:256] = pieces(gates, lane)
            send_kv(l, k).start()

        def send_kv(l, k):
            place = pl.ds(pl.multiple_of(WINDOW + (2 * k + d) * BLOCK, WINDOW), BLOCK)
            rows = r.kvg.at[pl.ds(l * 3, 3), place]
            return remote(rows, rows, r.kv_s.at[l * 4 + k], r.kv_r.at[l * 4 + k], partner)

        def wait_kv(l, k):
            place = pl.ds(pl.multiple_of(WINDOW + (2 * k + 1 - d) * BLOCK, WINDOW), BLOCK)
            arrived(r.kvg.at[pl.ds(l * 3, 3), place], r.kv_r.at[l * 4 + k])

        def attend(l, k):
            block = 2 * k + d
            start = block * BLOCK
            length = r.pk[24:25, 0:1]
            column = lanes((BLOCK, 256))
            row = rows_of((BLOCK, 256))
            for hh in range(3):
                index = hh * 8 + block
                pick_col = jnp.sum(
                    jnp.where(lanes((64, 128)) == index, r.pt[...], 0.0),
                    axis=1,
                    keepdims=True,
                ).astype(jnp.int32)

                def gather(j, total):
                    hot = (lanes((64, 256)) + j * 256 == pick_col).astype(F32).astype(BF16)
                    rows = pl.ds(pl.multiple_of(WINDOW + j * 256, WINDOW), 256)
                    return total + dot(hot, r.kvg[l * 3 + hh, rows, :])

                chosen = lax.fori_loop(0, k + 1, gather, jnp.zeros((64, 256), F32)).astype(BF16)
                r.chosen[(l * 4 + k) * 3 + hh] = chosen[:, 0:128]
                near = pl.ds(pl.multiple_of(start, BLOCK), 192)
                r.keyset[0:192, 0:128] = r.kvg[l * 3 + hh, near, 0:128]
                r.keyset[192:256, :] = chosen
                query = jnp.concatenate([r.q[(l * 4 + k) * 3 + hh], ones_tile], axis=1)
                logits = dot(query, r.keyset[...], NT)
                pick_row = r.pk[pl.ds(index, 1), :][:, 128:384]
                distance = row + WINDOW - column
                near_pos = start - WINDOW + column
                near_ok = (
                    (near_pos >= 0)
                    & (distance >= 0)
                    & (distance < WINDOW)
                    & ((near_pos < length) | (distance == 0))
                )
                far_ok = (pick_row <= start - WINDOW + row) & (pick_row < length)
                allowed = ((column < 192) & near_ok) | ((column >= 192) & far_ok)
                masked = jnp.where(allowed, logits, -1e30)
                raised = jnp.exp(masked - jnp.max(masked, axis=1, keepdims=True))
                soft = raised / jnp.sum(raised, axis=1, keepdims=True)
                r.soft[(l * 4 + k) * 3 + hh] = soft
                mixed = dot(soft.astype(BF16), r.keyset[:, 0:128])
                r.merged[l * 4 + k, :, hh * 128 : hh * 128 + 128] = mixed.astype(BF16)
            return dot(r.merged[l * 4 + k], r.wo[l])

        def feed(l, k):
            pre = dot(r.normed[8 * l + 4 + k], r.fc[l]) + r.fcb[l]
            square = pre * pre
            wave = jnp.tanh(ROOT * pre * (1.0 + CUBE * square))
            half = 0.5 * (1.0 + wave)
            slope = half + 0.5 * pre * (1.0 - wave * wave) * (ROOT * (1.0 + 3.0 * CUBE * square))
            r.hidden[l * 4 + k] = (pre * half).astype(BF16)
            r.slope[l * 4 + k] = slope.astype(BF16)
            return dot(r.hidden[l * 4 + k], r.pj[l])

        def send_part(n):
            return remote(
                r.part_out.at[lax.rem(n, 4)],
                r.part_in.at[lax.rem(n, 8)],
                r.ps_s.at[n],
                r.ps_r.at[n],
                mate_id,
            )

        def give(n, part):
            @pl.when(mid)
            def _():
                r.own[lax.rem(n, 4)] = part

            @pl.when(jnp.logical_not(mid))
            def _():
                @pl.when(n >= 4)
                def _():
                    send_part(n - 4).wait_send()

                r.part_out[lax.rem(n, 4)] = part.astype(BF16)
                send_part(n).start()

        def send_pair(n):
            return remote(
                r.pair_out.at[lax.rem(n, 4)],
                r.pair_in.at[lax.rem(n, 8)],
                r.mm_s.at[n],
                r.mm_r.at[n],
                other_id,
            )

        def fold(n):
            arrived(r.part_in.at[lax.rem(n, 8)], r.ps_r.at[n])

            @pl.when(n >= 4)
            def _():
                send_pair(n - 4).wait_send()

            both = r.own[lax.rem(n, 4)] + r.part_in[lax.rem(n, 8)].astype(F32)
            r.pair_out[lax.rem(n, 4)] = both.astype(BF16)
            send_pair(n).start()

        def total_of(n):
            arrived(r.pair_in.at[lax.rem(n, 8)], r.mm_r.at[n])
            return r.pair_out[lax.rem(n, 4)].astype(F32) + r.pair_in[
                lax.rem(n, 8)
            ].astype(F32)

        y_way = (r.y, r.y_stage, r.y_s, r.y_r)
        dx_way = (r.dx, r.dx_stage, r.dx_s, r.dx_r)

        def hand_out(way, k, value):
            way[1][k] = value.astype(F32).T.astype(BF16)
            for side in (0, 1):
                target = 2 * (h - 1) + side
                own = (k == s) & (target == h) & (d == owner)
                local, far = hand_copy(way, k, side)
                pl.when(own)(local.start)
                pl.when(jnp.logical_not(own))(far.start)

        def hand_copy(way, k, side):
            src = way[1].at[k, pl.ds(pl.multiple_of((2 * (h - 1) + side) * local, local), local)]
            dst = way[0].at[slot, :, pl.ds(pl.multiple_of(d * BLOCK, BLOCK), BLOCK)]
            recv = way[3].at[slot, d]
            return (
                pltpu.make_async_copy(src, dst, recv),
                remote(
                    src, dst, way[2].at[k, side], recv, at(k, 2 * (h - 1) + side, owner)
                ),
            )

        def finish_hand(way):
            @pl.when(mid)
            def _():
                for k in range(chunks):
                    for side in (0, 1):
                        own = (k == s) & (2 * (h - 1) + side == h) & (d == owner)
                        pl.when(jnp.logical_not(own))(hand_copy(way, k, side)[1].wait_send)

            for j in range(micro):
                for core in (0, 1):
                    arrived(
                        way[0].at[j, :, core * BLOCK : core * BLOCK + BLOCK],
                        way[3].at[j, core],
                    )

        def leave(n):
            c, k = lax.div(n, 4), lax.rem(n, 4)
            state = (r.state[n].astype(F32) + total_of(n) + r.par[c, 2:3]).astype(BF16)

            @pl.when(c < 3)
            def _():
                publish(c + 1, k, state)

            @pl.when(c == 3)
            def _():
                hand_out(y_way, k, state)

        def send_grad(index):
            return remote(
                r.grad.at[index],
                r.grad.at[index],
                r.gx_s.at[index],
                r.gx_r.at[index],
                mate_id,
            )

        def enter_back(k):
            r.grad[12 + k] = turned(r.cot_in, r.xc_r, k)
            send_grad(12 + k).start()

        def add_row(row, value):
            place = pl.ds(row, 1)
            r.small[place, :] = r.small[place, :] + value

        def leave_back(m):
            c, k = 3 - lax.div(m, 4), 3 - lax.rem(m, 4)
            index = c * 4 + k
            total = total_of(16 + m)
            scaled, inverse = norm_parts(r.state[index].astype(F32))
            above = r.grad[index].astype(F32)
            add_row(c * 3, jnp.sum(total * scaled, axis=0, keepdims=True))
            add_row(c * 3 + 1, jnp.sum(total, axis=0, keepdims=True))
            add_row(c * 3 + 2, jnp.sum(above, axis=0, keepdims=True))
            t = total * r.par[c, 0:1]
            inner = (
                t
                - jnp.mean(t, axis=-1, keepdims=True)
                - scaled * jnp.mean(t * scaled, axis=-1, keepdims=True)
            )
            below = (above + inverse * inner).astype(BF16)

            @pl.when(c > 0)
            def _():
                r.grad[index - 4] = below
                send_grad(index - 4).start()

            @pl.when(c == 0)
            def _():
                hand_out(dx_way, k, below)

        def send_keys(l, step):
            ring = lax.rem(step, 2) * 3
            return remote(
                r.sums.at[pl.ds(ring, 3), pl.ds(pl.multiple_of((1 - d) * BLOCK, BLOCK), BLOCK)],
                r.sums_in.at[pl.ds(ring, 3)],
                r.dk_s.at[l * 4 + step],
                r.dk_r.at[l * 4 + step],
                partner,
            )

        def attend_back(l, k):
            step = 3 - k
            ring = lax.rem(step, 2) * 3
            start = (2 * k + d) * BLOCK
            grad_merged = dot(r.grad[8 * l + k], r.wo[l], NT).astype(BF16)

            @pl.when(step == 0)
            def _():
                r.near[...] = jnp.zeros_like(r.near)

            @pl.when(step >= 2)
            def _():
                send_keys(l, step - 2).wait_send()

            for hh in range(3):
                where = (l * 4 + k) * 3 + hh
                near = pl.ds(pl.multiple_of(start, BLOCK), 192)
                r.keyset[0:192, 0:128] = r.kvg[l * 3 + hh, near, 0:128]
                r.keyset[192:256, 0:128] = r.chosen[where]
                keys = r.keyset[:, 0:128]
                mixed = grad_merged[:, hh * 128 : hh * 128 + 128]
                soft = r.soft[where]
                grad_soft = dot(mixed, keys, NT)
                grad_logits = (
                    soft * (grad_soft - jnp.sum(grad_soft * soft, axis=1, keepdims=True))
                ).astype(BF16)
                grad_query = dot(grad_logits, keys) * 0.125
                r.dqkv[k, :, hh * 256 : hh * 256 + 128] = jnp.where(
                    lane < 64, grad_query, 0.0
                ).astype(BF16)
                left = jnp.concatenate([grad_logits, soft.astype(BF16)], axis=0)
                right = jnp.concatenate(
                    [
                        jnp.concatenate([r.q[where], ones_tile], axis=1),
                        jnp.concatenate([mixed, jnp.zeros_like(ones_tile)], axis=1),
                    ],
                    axis=0,
                )
                grad_set = dot(left, right, TN)
                r.near[hh, near, :] = r.near[hh, near, :] + grad_set[0:192, 0:128]
                far = grad_set[192:256]
                high = far.astype(BF16)
                r.far[hh * 4 + k, 0:64] = high
                r.far[hh * 4 + k, 64:128] = (far - high.astype(F32)).astype(BF16)

                def scatter(kk, total):
                    pick_row = r.pk[pl.ds(hh * 8 + 2 * kk + d, 1), :][:, 0:128]
                    hot = (rows_of((256, 128)) + k * 256 == pick_row).astype(F32).astype(BF16)
                    return total + dot(hot, r.far[hh * 4 + kk])

                total = lax.fori_loop(k, 4, scatter, jnp.zeros((256, 256), F32))
                rows = pl.ds(pl.multiple_of(WINDOW + k * 256, WINDOW), 256)
                r.sums[ring + hh, :, 0:128] = total[:, 0:128] + r.near[hh, rows, :]
                r.sums[ring + hh, :, 128:256] = total[:, 128:256]
            send_keys(l, step).start()

        def finish_back(l, k):
            step = 3 - k
            ring = lax.rem(step, 2) * 3
            arrived(r.sums_in.at[pl.ds(ring, 3)], r.dk_r.at[l * 4 + step])
            mine = pl.ds(pl.multiple_of(d * BLOCK, BLOCK), BLOCK)
            for hh in range(3):
                own = r.sums[ring + hh, mine, :] + r.sums_in[ring + hh]
                scores = own[:, 128:256] * r.sig[(l * 4 + k) * 3 + hh]
                head = slice(hh * 256, hh * 256 + 128)
                r.dqkv[k, :, head] = jnp.where(
                    lane < 64, r.dqkv[k, :, head], pieces(scores, lane)
                )
                r.dqkv[k, :, hh * 256 + 128 : hh * 256 + 256] = own[:, 0:128].astype(BF16)
            return dot(r.dqkv[k], r.w1[l])

        def feed_back(l, k):
            grad_hidden = dot(r.grad[8 * l + 4 + k], r.pj[l], NT)
            grad_pre = (grad_hidden * r.slope[l * 4 + k].astype(F32)).astype(BF16)
            r.dpre[k] = grad_pre
            return dot(grad_pre, r.fc[l], NT)

        def four(ref, first):
            value = ref[pl.ds(first, 4)]
            return value.reshape(4 * BLOCK, value.shape[2])

        ones_rows = jnp.ones((8, 4 * BLOCK), BF16)

        def split(kind, width):
            for section in range(4):
                rows = pl.ds(pl.multiple_of((2 * section + 1 - d) * part_rows, 8), part_rows)
                halves[kind][0][section] = r.wide[rows, 0:width].astype(BF16)
            send_half(kind).start()

        def send_half(kind):
            return remote(
                halves[kind][0],
                halves[kind][1],
                r.xh_s.at[kind],
                r.xh_r.at[kind],
                partner,
            )

        def send_share(kind, step):
            return remote(
                shares[kind][0].at[step - 1],
                shares[kind][1].at[step - 1],
                r.yh_s.at[kind, step - 1],
                r.yh_r.at[kind, step - 1],
                at(lax.rem(s + step, 4), h, d),
            )

        def share(kind, width):
            arrived(halves[kind][1], r.xh_r.at[kind])
            send_half(kind).wait_send()
            for step in (1, 2, 3, 0):
                section = lax.rem(s + step, 4)
                rows = pl.ds(pl.multiple_of((2 * section + d) * part_rows, 8), part_rows)
                both = r.wide[rows, 0:width] + halves[kind][1][section].astype(F32)
                if step:
                    shares[kind][0][step - 1] = both.astype(BF16)
                    send_share(kind, step).start()
                else:
                    r.wide[rows, 0:width] = both

        def collect(kind, width):
            rows = pl.ds(pl.multiple_of((2 * s + d) * part_rows, 8), part_rows)
            total = r.wide[rows, 0:width]
            for step in (1, 2, 3):
                arrived(shares[kind][1].at[step - 1], r.yh_r.at[kind, step - 1])
                total = total + shares[kind][1][step - 1].astype(F32)
                send_share(kind, step).wait_send()
            return total

        def weights_feed(l):
            x, g = four(r.normed, 8 * l + 4), four(r.grad, 8 * l + 4)
            grad_pre = four(r.dpre, 0)
            r.wide[:, 0:768] = dot(x, grad_pre, TN)
            r.wide[:, 768:1536] = dot(g, four(r.hidden, 4 * l), TN)
            add_row(18 + l, dot(ones_rows, grad_pre)[0:1])
            split(0, 1536)

        def weights_attend(l):
            for step in (2, 3):
                send_keys(l, step).wait_send()
            x, g = four(r.normed, 8 * l), four(r.grad, 8 * l)
            grads, merged = four(r.dqkv, 0), four(r.merged, 4 * l)
            wide_lane = lanes((4 * BLOCK, 128))
            t = [grads[:, i * 256 : i * 256 + 128].astype(F32) for i in range(3)]
            first = jnp.where(wide_lane < 64, t[0], pltpu.roll(t[1], 64, 1))
            second = (
                t[2]
                + pltpu.roll(jnp.where(wide_lane < 64, 0.0, t[0]), 3, 1)
                + pltpu.roll(jnp.where(wide_lane < 64, 0.0, t[1]), 6, 1)
            ).astype(BF16)
            packed = jnp.concatenate(
                [first.astype(BF16), second]
                + [grads[:, i * 256 + 128 : i * 256 + 256] for i in range(3)],
                axis=1,
            )
            r.wide[:, 0:640] = dot(x, packed, TN)
            u = [merged[:, i * 128 : i * 128 + 128].astype(F32) for i in range(3)]
            packed = jnp.concatenate(
                [
                    jnp.where(wide_lane < 64, pltpu.roll(u[0], 64, 1), u[1]),
                    jnp.where(wide_lane < 64, pltpu.roll(u[2], 64, 1), 0.0),
                ],
                axis=1,
            ).astype(BF16)
            r.wide[:, 640:896] = dot(g, packed, TN)
            scores = dot(second, x, TN)
            for hh, row in ((0, 67), (1, 70), (2, 64)):
                add_row(
                    24 + 4 * l + hh, scores[row : row + 1] + scores[row + 1 : row + 2] + scores[row + 2 : row + 3]
                )
            add_row(16 + l, dot(ones_rows, grads)[0:1])
            split(1, 896)

        def collect_feed(l):
            total = collect(0, 1536)
            r.o_fc[l] = total[:, 0:768]
            r.o_pj[l] = total[:, 768:1536]

        def collect_attend(l):
            total = collect(1, 896)
            r.o_qkv[3 * l] = total[:, 0:192]
            for i in (0, 1):
                r.o_qkv[3 * l + 1 + i] = jnp.concatenate(
                    [total[:, 256 + 128 * j + 64 * i : 320 + 128 * j + 64 * i] for j in range(3)],
                    axis=1,
                )
            r.o_out[l] = total[:, 640:896].T[0:192]

        def slot_of(n, carry):
            ahead = n < 16
            c = jnp.where(ahead, lax.div(n, 4), 7 - lax.div(n, 4))
            k = jnp.where(ahead, lax.rem(n, 4), 3 - lax.rem(n, 4))
            l = lax.div(c, 2)
            works = n < 32
            attends = lax.rem(c, 2) == 0

            @pl.when(mid & (n < 4))
            def _():
                enter(n)

            @pl.when(mid & (n >= 4) & (n < 20))
            def _():
                leave(n - 4)

            @pl.when(mid & (n >= 12) & (n < 16))
            def _():
                enter_back(15 - n)

            @pl.when(mid & (n >= 20))
            def _():
                leave_back(n - 20)

            @pl.when(jnp.logical_not(mid) & ahead)
            def _():
                arrived(r.normed.at[n], r.nx_r.at[n])

            @pl.when(jnp.logical_not(mid) & jnp.logical_not(ahead) & works)
            def _():
                arrived(r.grad.at[c * 4 + k], r.gx_r.at[c * 4 + k])

            @pl.when((n == 0) | (n == 8))
            def _():
                for copy in attend_loads[0:12]:
                    pltpu.make_async_copy(copy.src_ref, copy.dst_ref, r.load.at[l]).wait()

            @pl.when(n == 4)
            def _():
                for copy in feed_loads:
                    copy.wait()

            @pl.when(ahead & attends)
            def _():
                project(l, k)

            @pl.when(n == 0)
            def _():
                for copy in pick_copies:
                    copy.wait()
                chosen = r.pk_in[owner, slot]
                r.pk[...] = jnp.concatenate(
                    [chosen, chosen, jnp.zeros((32, 192), jnp.int32), chosen], axis=1
                )
                square = jnp.concatenate([chosen.astype(F32), jnp.zeros((32, 64), F32)], axis=1)
                square = jnp.concatenate([square, jnp.zeros((96, 128), F32)], axis=0)
                r.pt[...] = square.T[0:64]

            @pl.when(ahead & attends)
            def _():
                wait_kv(l, k)
                give(n, attend(l, k))

            @pl.when(ahead & jnp.logical_not(attends))
            def _():
                give(n, feed(l, k))

            @pl.when(jnp.logical_not(ahead) & works & attends)
            def _():
                attend_back(l, k)
                give(n, finish_back(l, k))

            @pl.when(jnp.logical_not(ahead) & works & jnp.logical_not(attends))
            def _():
                give(n, feed_back(l, k))

            @pl.when(mid & (n >= 2) & (n < 34))
            def _():
                fold(n - 2)

            @pl.when((n == 21) | (n == 29))
            def _():
                share(0, 1536)

            @pl.when((n == 25) | (n == 33))
            def _():
                share(1, 896)

            @pl.when((n == 23) | (n == 31))
            def _():
                collect_feed(lax.div(31 - n, 8))

            @pl.when((n == 27) | (n == 35))
            def _():
                collect_attend(lax.div(35 - n, 8))

            @pl.when((n == 19) | (n == 27))
            def _():
                weights_feed(l)

            @pl.when((n == 23) | (n == 31))
            def _():
                weights_attend(l)

            return carry

        lax.fori_loop(0, 36, slot_of, 0)

        def send_rows():
            return remote(
                r.small.at[0:16],
                r.small.at[0:16],
                r.sm_s.at[0],
                r.sm_r.at[0],
                mate_id,
            )

        @pl.when(mid)
        def _():
            send_rows().start()

        @pl.when(jnp.logical_not(mid))
        def _():
            arrived(r.small.at[0:16], r.sm_r.at[0])

        swap = remote(r.small, r.small_in, r.sm_s.at[1], r.sm_r.at[1], partner)
        swap.start()
        swap.wait()
        r.small_all[s] = r.small[...] + r.small_in[...]

        def send_small(step):
            return remote(
                r.small_all.at[s],
                r.small_all.at[s],
                r.sm_s.at[1 + step],
                r.sm_r.at[2 + s],
                at(lax.rem(s + step, 4), h, d),
            )

        for step in (1, 2, 3):
            send_small(step).start()
        for step in (1, 2, 3):
            section = lax.rem(s + step, 4)
            arrived(r.small_all.at[section], r.sm_r.at[2 + section])

        @pl.when(mid)
        def _():
            send_rows().wait_send()

        r.small[...] = (r.small_all[0] + r.small_all[1]) + (
            r.small_all[2] + r.small_all[3]
        )
        for j in range(4):

            @pl.when(h == j)
            def _():
                for i, ref in enumerate((r.o_gain, r.o_bias, r.o_ob)):
                    ref[...] = r.small[pl.ds(s * 3 + i, 1), :][:, j * 192 : j * 192 + 192]

        for l in (0, 1):
            row = r.small[16 + l : 17 + l, :]
            for i in (0, 1):
                r.o_qv[l, i : i + 1, :] = jnp.concatenate(
                    [row[:, j * 256 + 192 * i : j * 256 + 192 * i + 64] for j in range(3)], axis=1
                )
            for j in range(3):
                r.o_score[j, l : l + 1, :] = r.small[
                    24 + 4 * l + j : 25 + 4 * l + j, :
                ]
        r.o_fcb[...] = r.small[18:20, :]

        finish_hand(y_way)
        finish_hand(dx_way)
        for step in (1, 2, 3):
            send_small(step).wait_send()

        @pl.when(d == owner)
        def _():
            for copies in stream_parts + cot_parts:
                sent(copies)

        sent(norm_rows)

        def drain_kv(i, carry):
            send_kv(lax.div(i, 4), lax.rem(i, 4)).wait_send()
            return carry

        lax.fori_loop(0, 8, drain_kv, 0)

        @pl.when(mid)
        def _():
            def drain(i, carry):
                send_normed(lax.div(i, 4), lax.rem(i, 4)).wait_send()
                send_grad(i).wait_send()
                return carry

            lax.fori_loop(0, 16, drain, 0)
            for n in range(28, 32):
                send_pair(n).wait_send()

        @pl.when(jnp.logical_not(mid))
        def _():
            for n in range(28, 32):
                send_part(n).wait_send()

    return kernel


def hand_over(*refs):
    count = len(refs) // 2
    for i in range(count):
        refs[count + i][...] = refs[i][...]


def shards(
    stream,
    cotangent,
    lengths,
    picks,
    norm_gain,
    norm_bias,
    out_bias,
    weight_qkv,
    bias_qv,
    weight_score,
    weight_out,
    weight_fc,
    bias_fc,
    weight_proj,
):
    micro, tokens, local = stream.shape
    layers, width = weight_qkv.shape[0], weight_qkv.shape[1]
    inputs = dict(
        stream=stream.transpose(0, 2, 1),
        cot=cotangent.transpose(0, 2, 1),
        lengths=lengths,
        picks=picks.reshape(micro, 24, 64),
        gain=norm_gain,
        shift=norm_bias,
        ob=out_bias,
        wqkv=weight_qkv.transpose(0, 2, 3, 1),
        bqv=bias_qv,
        wscore=weight_score.transpose(2, 0, 1),
        wout=weight_out,
        wfc=weight_fc,
        bfc=bias_fc,
        wpj=weight_proj,
    )
    spaces = dict(
        stream=pl.ANY, cot=pl.ANY, lengths=pltpu.SMEM, wqkv=pl.ANY, wout=pl.ANY, wfc=pl.ANY, wpj=pl.ANY
    )
    part_rows = width // 8
    outputs = dict(
        y=((micro, local, 2 * BLOCK), BF16),
        dx=((micro, local, 2 * BLOCK), BF16),
        o_gain=((1, 192), F32),
        o_bias=((1, 192), F32),
        o_ob=((1, 192), F32),
        o_qkv=((6, part_rows, 192), F32),
        o_qv=((2, 2, 192), F32),
        o_score=((3, 2, 768), F32),
        o_out=((2, 192, part_rows), F32),
        o_fc=((2, part_rows, 768), F32),
        o_fcb=((2, 768), F32),
        o_pj=((2, part_rows, 768), F32),
    )
    dma = pltpu.SemaphoreType.DMA
    scratch = dict(
        stream_in=((4, 768, BLOCK), BF16),
        cot_in=((4, 768, BLOCK), BF16),
        prm=((16, 768), BF16),
        w1=((2, 768, 768), BF16),
        wo=((2, 384, 768), BF16),
        fc=((2, 768, 768), BF16),
        pj=((2, 768, 768), BF16),
        bq=((2, 1, 768), F32),
        fcb=((2, 1, 768), F32),
        prm_in=((4, 4, 16, 768), BF16),
        par=((4, 8, 768), F32),
        pk_out=((micro, 32, 64), jnp.int32),
        pk_in=((2, micro, 32, 64), jnp.int32),
        pk=((32, 384), jnp.int32),
        pt=((64, 128), F32),
        state=((16, BLOCK, 768), BF16),
        normed=((16, BLOCK, 768), BF16),
        q=((24, BLOCK, 128), BF16),
        sig=((24, BLOCK, 128), F32),
        kvg=((6, WINDOW + tokens, 256), BF16),
        chosen=((24, 64, 128), BF16),
        keyset=((256, 256), BF16),
        soft=((24, BLOCK, 256), F32),
        merged=((8, BLOCK, 384), BF16),
        hidden=((8, BLOCK, 768), BF16),
        slope=((8, BLOCK, 768), BF16),
        part_out=((4, BLOCK, 768), BF16),
        part_in=((8, BLOCK, 768), BF16),
        own=((4, BLOCK, 768), F32),
        pair_out=((4, BLOCK, 768), BF16),
        pair_in=((8, BLOCK, 768), BF16),
        y_stage=((4, 768, BLOCK), BF16),
        dx_stage=((4, 768, BLOCK), BF16),
        grad=((16, BLOCK, 768), BF16),
        dpre=((4, BLOCK, 768), BF16),
        dqkv=((4, BLOCK, 768), BF16),
        near=((3, WINDOW + tokens, 128), F32),
        far=((12, 128, 256), BF16),
        sums=((6, 256, 256), F32),
        sums_in=((6, BLOCK, 256), F32),
        wide=((768, 1536), F32),
        xo_f=((4, part_rows, 1536), BF16),
        xi_f=((4, part_rows, 1536), BF16),
        yo_f=((3, part_rows, 1536), BF16),
        yi_f=((3, part_rows, 1536), BF16),
        xo_a=((4, part_rows, 896), BF16),
        xi_a=((4, part_rows, 896), BF16),
        yo_a=((3, part_rows, 896), BF16),
        yi_a=((3, part_rows, 896), BF16),
        small=((32, 768), F32),
        small_in=((32, 768), F32),
        small_all=((4, 32, 768), F32),
    )
    sems = dict(
        xs_s=(4, 4),
        xs_r=(4, 4),
        xc_s=(4, 4),
        xc_r=(4, 4),
        load=(3,),
        prm_s=(4, 2),
        prm_r=(4, 4),
        pick_s=(2,),
        pick_r=(1,),
        nx_s=(16,),
        nx_r=(16,),
        kv_s=(8,),
        kv_r=(8,),
        ps_s=(32,),
        ps_r=(32,),
        mm_s=(32,),
        mm_r=(32,),
        y_s=(4, 2),
        y_r=(2, 2),
        dx_s=(4, 2),
        dx_r=(2, 2),
        gx_s=(16,),
        gx_r=(16,),
        dk_s=(8,),
        dk_r=(8,),
        xh_s=(2,),
        xh_r=(2,),
        yh_s=(2, 3),
        yh_r=(2, 3),
        sm_s=(5,),
        sm_r=(6,),
    )
    names = list(inputs) + list(outputs) + list(scratch) + list(sems)
    results = pl.pallas_call(
        make_kernel(names, micro, width // 8, local),
        out_shape=[jax.ShapeDtypeStruct(*spec) for spec in outputs.values()],
        in_specs=[
            pl.BlockSpec(memory_space=spaces.get(name, pltpu.VMEM))
            for name in inputs
        ],
        out_specs=[pl.BlockSpec(memory_space=pltpu.VMEM) for name in outputs],
        scratch_shapes=[pltpu.VMEM(*spec) for spec in scratch.values()]
        + [dma(shape) for shape in sems.values()],
        compiler_params=pltpu.CompilerParams(
            collective_id=0, has_side_effects=True, vmem_limit_bytes=62 * 2**20
        ),
        name="blocks",
    )(*inputs.values())
    results = pl.pallas_call(
        hand_over,
        out_shape=[jax.ShapeDtypeStruct(*spec) for spec in outputs.values()],
        in_specs=[pl.BlockSpec(memory_space=pltpu.VMEM)] * len(outputs),
        out_specs=[pl.BlockSpec(memory_space=pltpu.VMEM)] * len(outputs),
        name="results",
    )(*results)
    o = types.SimpleNamespace(**dict(zip(outputs, results)))
    dp_count = lax.axis_size("dp")
    if dp_count > 2:
        d = lax.rem(lax.axis_index("dp"), 2)

        def scattered(value):
            placed = jnp.zeros((value.shape[0], 2 * part_rows, value.shape[2]), F32)
            placed = lax.dynamic_update_slice(placed, value, (0, d * part_rows, 0))
            return lax.psum_scatter(placed, "dp", scatter_dimension=1, tiled=True)

        o.o_out = scattered(o.o_out.transpose(0, 2, 1)).transpose(0, 2, 1)
        o.o_qkv, o.o_fc, o.o_pj = map(scattered, (o.o_qkv, o.o_fc, o.o_pj))
        sums = (o.o_gain, o.o_bias, o.o_ob, o.o_qv, o.o_score, o.o_fcb)
        o.o_gain, o.o_bias, o.o_ob, o.o_qv, o.o_score, o.o_fcb = jax.tree.map(
            lambda value: 0.5 * value, lax.psum(sums, "dp")
        )
    rows = o.o_fc.shape[1]
    return (
        o.y.transpose(0, 2, 1),
        o.dx.transpose(0, 2, 1),
        o.o_gain,
        o.o_bias,
        o.o_ob,
        o.o_qkv.reshape(layers, 3, rows, 192).transpose(0, 2, 1, 3),
        o.o_qv,
        o.o_score.transpose(1, 2, 0),
        o.o_out,
        o.o_fc,
        o.o_fcb,
        o.o_pj.transpose(0, 2, 1),
    )


def solution(mesh):
    return jax.shard_map(
        shards,
        mesh=mesh,
        in_specs=(
            P("dp", None, "head"),
            P("dp", None, "head"),
            P("dp"),
            P("dp", "head", None, None),
            P("section", None),
            P("section", None),
            P("section", "head"),
            P(None, None, None, "head"),
            P(None, None, "head"),
            P(None, None, "head"),
            P(None, "head", None),
            P(None, None, "head"),
            P(None, "head"),
            P(None, "head", None),
        ),
        out_specs=(
            P("dp", "section", "head"),
            P("dp", "section", "head"),
            P("section", "head"),
            P("section", "head"),
            P("section", "head"),
            P(None, ("section", "dp"), None, "head"),
            P(None, None, "head"),
            P(None, None, "head"),
            P(None, "head", ("section", "dp")),
            P(None, ("section", "dp"), "head"),
            P(None, "head"),
            P(None, "head", ("section", "dp")),
        ),
        check_vma=False,
    )
```

```python
import types

import jax
import jax.numpy as jnp
from jax import lax
from jax.experimental import pallas as pl
from jax.experimental.pallas import tpu as pltpu
from jax.sharding import PartitionSpec as P

MESH = pl.DeviceIdType.MESH
BLOCK = 128
HALF = 64
WINDOW = 64
NT = (((1,), (1,)), ((), ()))
TN = (((0,), (0,)), ((), ()))
F32 = jnp.float32
BF16 = jnp.bfloat16
ROOT = 0.7978845608028654
CUBE = 0.044715


def dot(left, right, dims=(((1,), (0,)), ((), ()))):
    return lax.dot_general(left, right, dims, preferred_element_type=F32)


def lanes(shape):
    return lax.broadcasted_iota(jnp.int32, shape, len(shape) - 1)


def rows_of(shape):
    return lax.broadcasted_iota(jnp.int32, shape, len(shape) - 2)


def head_lanes(lane, hh):
    return (lane >= 64 + 3 * hh) & (lane < 67 + 3 * hh)


def pieces(value, lane):
    high = value.astype(BF16)
    rest = value - high.astype(F32)
    middle = rest.astype(BF16)
    low = (rest - middle.astype(F32)).astype(BF16)
    zero = jnp.zeros_like(high)
    used = (lane >= 64) & (lane < 73)
    which = lax.rem(lane - 64 + 3 * 64, 3)
    return jnp.where(
        used & (which == 0),
        high,
        jnp.where(used & (which == 1), middle, jnp.where(used & (which == 2), low, zero)),
    )


def make_kernel(names, micro, part_rows, local):
    def kernel(*refs):
        r = types.SimpleNamespace(**dict(zip(names, refs)))
        wides = (r.wide_f, r.wide_a)
        halves = ((r.xo_f, r.xi_f), (r.xo_a, r.xi_a))
        shares = ((r.yo_f, r.yi_f), (r.yo_a, r.yi_a))
        s, h, dp = lax.axis_index("section"), lax.axis_index("head"), lax.axis_index("dp")
        d = lax.rem(dp, 2)
        pair = dp - d
        mid = (h == 1) | (h == 2)
        mate = h + 1 - 2 * lax.rem(h, 2)
        other = 3 - h
        owner = lax.div(s, micro)
        slot = lax.rem(s, micro)

        def at(section, head, core):
            return (section, head, pair + core)

        def remote(src, dst, send, recv, device):
            return pltpu.make_async_remote_copy(
                src_ref=src,
                dst_ref=dst,
                send_sem=send,
                recv_sem=recv,
                device_id=device,
                device_id_type=MESH,
            )

        partner = at(s, h, 1 - d)
        mate_id = at(s, mate, d)
        other_id = at(s, other, d)

        def arrived(dst, recv):
            remote(dst, dst, recv, recv, partner).wait_recv()

        r.small[...] = jnp.zeros_like(r.small)
        for j in range(micro):
            r.pk_out[j, 0:24] = r.picks[j]
            r.pk_out[j, 24:32] = jnp.zeros((8, 64), jnp.int32) + r.lengths[j]
        wide_bias = jnp.concatenate([r.ob[...].astype(F32)] * 4, axis=1)
        wide_bias = jnp.where(
            (lanes((1, 768)) >= h * local) & (lanes((1, 768)) < h * local + local), wide_bias, 0.0
        )
        row = rows_of((16, 768))
        r.prm[...] = jnp.where(
            row == 0,
            r.gain[...].astype(F32),
            jnp.where(
                row == 1, r.shift[...].astype(F32), jnp.where(row == 2, wide_bias, 0.0)
            ),
        ).astype(BF16)

        barrier = pltpu.get_barrier_semaphore()
        flat = (s * 4 + h) * 2 + d

        def greet(step, carry):
            whom = lax.rem(flat + step, 32)
            pl.semaphore_signal(
                barrier,
                inc=1,
                device_id=at(lax.div(whom, 8), lax.rem(lax.div(whom, 2), 4), lax.rem(whom, 2)),
                device_id_type=MESH,
            )
            return carry

        lax.fori_loop(1, 32, greet, 0)
        pl.semaphore_wait(barrier, 31)

        def spread(source, landing, sends, recvs, k):
            copies = []
            for hm in (1, 2):
                for core in (0, 1):
                    src = source.at[slot, :, (2 * k + core) * BLOCK : (2 * k + core + 1) * BLOCK]
                    dst = landing.at[k, pl.ds(pl.multiple_of(h * local, local), local)]
                    recv = recvs.at[h, k]
                    copies.append(
                        (
                            (h == hm) & (d == core),
                            pltpu.make_async_copy(src, dst, recv),
                            remote(
                                src, dst, sends.at[(hm - 1) * 2 + core, k], recv, at(s, hm, core)
                            ),
                        )
                    )
            return copies

        def launch(copies):
            for own, local, far in copies:
                pl.when(own)(local.start)
                pl.when(jnp.logical_not(own))(far.start)

        def sent(copies):
            for own, local, far in copies:
                pl.when(jnp.logical_not(own))(far.wait_send)

        chunks = 4
        stream_parts = [spread(r.stream, r.stream_in, r.xs_s, r.xs_r, k) for k in range(chunks)]
        cot_parts = [spread(r.cot, r.cot_in, r.xc_s, r.xc_r, k) for k in range(chunks)]
        norm_rows = []
        for step in range(4):
            section = lax.rem(s + step, 4)
            for hm in (1, 2):
                norm_rows.append(
                    (
                        (h == hm) if step == 0 else (h == 4),
                        pltpu.make_async_copy(
                            r.prm, r.prm_in.at[s, h], r.prm_r.at[s, h]
                        ),
                        remote(
                            r.prm,
                            r.prm_in.at[s, h],
                            r.prm_s.at[step, hm - 1],
                            r.prm_r.at[s, h],
                            at(section, hm, d),
                        ),
                    )
                )
        pick_copies = (
            pltpu.make_async_copy(r.pk_out, r.pk_in.at[d], r.pick_s.at[0]),
            remote(r.pk_out, r.pk_in.at[d], r.pick_s.at[1], r.pick_r.at[0], partner),
        )

        attend_loads, feed_loads = [], []
        for l in range(2):
            for hh in range(3):
                rows = slice(hh * 64, hh * 64 + 64)
                for part, place in ((0, 0), (1, 128), (2, 192)):
                    attend_loads.append(
                        pltpu.make_async_copy(
                            r.wqkv.at[l, part, rows],
                            r.w1.at[l, hh * 256 + place : hh * 256 + place + 64],
                            r.load.at[l],
                        )
                    )
                attend_loads.append(
                    pltpu.make_async_copy(
                        r.wout.at[l, rows],
                        r.wo.at[l, hh * 128 + 64 : hh * 128 + 128],
                        r.load.at[l],
                    )
                )
            feed_loads.append(pltpu.make_async_copy(r.wfc.at[l], r.fc.at[l], r.load.at[2]))
            feed_loads.append(pltpu.make_async_copy(r.wpj.at[l], r.pj.at[l], r.load.at[2]))

        launch(norm_rows)

        @pl.when(d == owner)
        def _():
            for copies in stream_parts:
                launch(copies)

        for copy in pick_copies + tuple(attend_loads) + tuple(feed_loads):
            copy.start()

        @pl.when(d == owner)
        def _():
            for copies in cot_parts:
                launch(copies)

        r.keyset[...] = jnp.zeros_like(r.keyset)
        r.far[...] = jnp.zeros_like(r.far)
        r.kv[:, 0:WINDOW] = jnp.zeros((8, WINDOW, 128), BF16)
        for l in range(2):
            for hh in range(3):
                score = jnp.where(
                    (rows_of((64, 768)) >= 3 * hh) & (rows_of((64, 768)) < 3 * hh + 3),
                    r.wscore[hh, l : l + 1, :].astype(F32),
                    0.0,
                )
                r.w1[l, hh * 256 + 64 : hh * 256 + 128] = score.astype(BF16)
                r.wo[l, hh * 128 : hh * 128 + 64] = jnp.zeros((64, 768), BF16)
            gap = jnp.zeros((1, 128), F32)
            r.fcb[l] = r.bfc[l : l + 1, :].astype(F32)
            bias = r.bqv[l].astype(F32)
            r.bq[l] = jnp.concatenate(
                [
                    piece
                    for hh in range(3)
                    for piece in (
                        bias[0:1, hh * 64 : hh * 64 + 64],
                        gap,
                        bias[1:2, hh * 64 : hh * 64 + 64],
                    )
                ],
                axis=1,
            )

        lane = lanes((BLOCK, 128))
        ones_tiles = [jnp.where(head_lanes(lane, hh), 1.0, 0.0).astype(BF16) for hh in range(3)]

        def norm_parts(x):
            center = x - jnp.mean(x, axis=-1, keepdims=True)
            inverse = lax.rsqrt(jnp.mean(center * center, axis=-1, keepdims=True) + 1e-05)
            return center * inverse, inverse

        def prepare():
            for c in range(4):
                for j in range(4):
                    arrived(r.prm_in.at[c, j], r.prm_r.at[c, j])
            for c in range(4):
                mine = r.prm_in[c, h].astype(F32)
                bias = mine[2:3, :] * 0.0
                for j in range(4):
                    bias = bias + r.prm_in[c, j].astype(F32)[2:3, :]
                r.par[c, 0:1] = mine[0:1]
                r.par[c, 1:2] = mine[1:2]
                r.par[c, 2:3] = bias

        def publish(c, k, half, state):
            rows = slice(half * HALF, half * HALF + HALF)
            r.state[c * 4 + k, rows] = state
            scaled, _ = norm_parts(state.astype(F32))
            normed = scaled * r.par[c, 0:1] + r.par[c, 1:2]
            r.normed[c * 4 + k, rows] = normed.astype(BF16)
            send_normed(c * 4 + k, half).start()

        def send_normed(n, half):
            rows = r.normed.at[n, half * HALF : half * HALF + HALF]
            return remote(rows, rows, r.nx_s.at[n * 2 + half], r.nx_r.at[n * 2 + half], mate_id)

        def turned(landing, recvs, k):
            for j in range(4):
                arrived(landing.at[k, j * local : j * local + local], recvs.at[j, k])
            return landing[k].astype(F32).T.astype(BF16)

        def enter(k):
            @pl.when(k == 0)
            def _():
                prepare()

            state = turned(r.stream_in, r.xs_r, k)
            for half in (0, 1):
                publish(0, k, half, state[half * HALF : half * HALF + HALF])

        def project(l, k):
            x = r.normed[8 * l + k]
            block = 2 * k + d
            place = pl.ds(pl.multiple_of(WINDOW + block * BLOCK, WINDOW), BLOCK)
            score = jnp.zeros((BLOCK, 128), F32)
            for hh in range(3):
                out = dot(x, r.w1[l, hh * 256 : hh * 256 + 256, :], NT)
                out = out + r.bq[l, :, hh * 256 : hh * 256 + 256]
                q, kv = out[:, :128], out[:, 128:]
                r.q[(l * 4 + k) * 3 + hh] = jnp.where(lane < 64, q, 0.0).astype(
                    BF16
                ) * jnp.asarray(0.125, BF16)
                score = score + jnp.where(head_lanes(lane, hh), q, 0.0)
                r.kv[l * 4 + hh, place] = kv.astype(BF16)
            gates = jnp.minimum(score, 0.0) - jnp.log1p(jnp.exp(-jnp.abs(score)))
            r.sig[l * 4 + k] = 1.0 / (1.0 + jnp.exp(score))
            r.kv[l * 4 + 3, place] = pieces(gates, lane)
            send_kv(l, k).start()

        def send_kv(l, k):
            place = pl.ds(pl.multiple_of(WINDOW + (2 * k + d) * BLOCK, WINDOW), BLOCK)
            rows = r.kv.at[pl.ds(l * 4, 4), place]
            return remote(rows, rows, r.kv_s.at[l * 4 + k], r.kv_r.at[l * 4 + k], partner)

        def wait_kv(l, k):
            place = pl.ds(pl.multiple_of(WINDOW + (2 * k + 1 - d) * BLOCK, WINDOW), BLOCK)
            arrived(r.kv.at[pl.ds(l * 4, 4), place], r.kv_r.at[l * 4 + k])

        def attend(l, k):
            block = 2 * k + d
            start = block * BLOCK
            length = r.pk[24:25, 0:1]
            column = lanes((BLOCK, 256))
            row = rows_of((BLOCK, 256))
            distance = row + WINDOW - column
            near_pos = start - WINDOW + column
            near_ok = (
                (column < 192)
                & (near_pos >= 0)
                & (distance >= 0)
                & (distance < WINDOW)
                & ((near_pos < length) | (distance == 0))
            )
            pick_cols = [
                jnp.sum(
                    jnp.where(lanes((64, 128)) == hh * 8 + block, r.pt[...], 0.0),
                    axis=1,
                    keepdims=True,
                ).astype(jnp.int32)
                for hh in range(3)
            ]

            def some(first, count):
                rows = pl.ds(pl.multiple_of(WINDOW + first, WINDOW), count)
                place = lanes((64, count)) + first
                gates = r.kv[l * 4 + 3, rows]
                return tuple(
                    dot(
                        (place == pick_cols[hh]).astype(F32).astype(BF16),
                        jnp.concatenate([r.kv[l * 4 + hh, rows], gates], axis=1),
                    )
                    for hh in range(3)
                )

            def adding(totals, more):
                return tuple(total + one for total, one in zip(totals, more))

            totals = some(pl.multiple_of(k * 256, 256), BLOCK)
            totals = lax.fori_loop(0, k, lambda j, t: adding(t, some(j * 256, 256)), totals)
            totals = lax.fori_loop(0, d, lambda j, t: adding(t, some(start, BLOCK)), totals)
            near = pl.ds(pl.multiple_of(start, BLOCK), 192)
            for hh in range(3):
                index = hh * 8 + block
                chosen = totals[hh].astype(BF16)
                where = (l * 4 + k) * 3 + hh
                r.chosen[where] = chosen[:, 0:128]
                r.keyset[hh, 0:192, 0:128] = r.kv[l * 4 + hh, near]
                r.keyset[hh, 192:256, :] = chosen
                query = jnp.concatenate([r.q[where], ones_tiles[hh]], axis=1)
                logits = dot(query, r.keyset[hh], NT)
                pick_row = r.pk[pl.ds(index, 1), :][:, 128:384]
                far_ok = (
                    (column >= 192) & (pick_row <= start - WINDOW + row) & (pick_row < length)
                )
                masked = jnp.where(near_ok | far_ok, logits, -1e30)
                raised = jnp.exp(masked - jnp.max(masked, axis=1, keepdims=True))
                soft = raised / jnp.sum(raised, axis=1, keepdims=True)
                r.soft[where] = soft
                mixed = dot(soft.astype(BF16), r.keyset[hh, :, 0:128])
                r.merged[l * 4 + k, :, hh * 128 : hh * 128 + 128] = mixed.astype(BF16)
            return dot(r.merged[l * 4 + k], r.wo[l])

        def feed(l, k, half):
            rows = slice(half * HALF, half * HALF + HALF)
            pre = dot(r.normed[8 * l + 4 + k, rows], r.fc[l]) + r.fcb[l]
            square = pre * pre
            wave = jnp.tanh(ROOT * pre * (1.0 + CUBE * square))
            both = 0.5 * (1.0 + wave)
            slope = both + 0.5 * pre * (1.0 - wave * wave) * (ROOT * (1.0 + 3.0 * CUBE * square))
            hidden = (pre * both).astype(BF16)
            r.hidden[l * 4 + k, rows] = hidden
            r.slope[l * 4 + k, rows] = slope.astype(BF16)
            return dot(hidden, r.pj[l])

        def send_part(n, half):
            rows = pl.ds(half * HALF, HALF)
            return remote(
                r.part_out.at[lax.rem(n, 4), rows],
                r.part_in.at[lax.rem(n, 8), rows],
                r.ps_s.at[n * 2 + half],
                r.ps_r.at[n * 2 + half],
                mate_id,
            )

        def give(n, half, part):
            rows = slice(half * HALF, half * HALF + HALF)

            @pl.when(mid)
            def _():
                r.own[lax.rem(n, 4), rows] = part

            @pl.when(jnp.logical_not(mid))
            def _():
                @pl.when(n >= 4)
                def _():
                    send_part(n - 4, half).wait_send()

                r.part_out[lax.rem(n, 4), rows] = part.astype(BF16)
                send_part(n, half).start()

        def give_both(n, part):
            for half in (0, 1):
                give(n, half, part[half * HALF : half * HALF + HALF])

        def send_pair(n, half):
            rows = pl.ds(half * HALF, HALF)
            return remote(
                r.pair_out.at[lax.rem(n, 4), rows],
                r.pair_in.at[lax.rem(n, 8), rows],
                r.mm_s.at[n * 2 + half],
                r.mm_r.at[n * 2 + half],
                other_id,
            )

        def fold(n):
            for half in (0, 1):
                rows = slice(half * HALF, half * HALF + HALF)
                arrived(r.part_in.at[lax.rem(n, 8), rows], r.ps_r.at[n * 2 + half])

                @pl.when(n >= 4)
                def _():
                    send_pair(n - 4, half).wait_send()

                both = r.own[lax.rem(n, 4), rows] + r.part_in[lax.rem(n, 8), rows].astype(F32)
                r.pair_out[lax.rem(n, 4), rows] = both.astype(BF16)
                send_pair(n, half).start()

        def total_of(n, half):
            rows = slice(half * HALF, half * HALF + HALF)
            arrived(r.pair_in.at[lax.rem(n, 8), rows], r.mm_r.at[n * 2 + half])
            return r.pair_out[lax.rem(n, 4), rows].astype(F32) + r.pair_in[
                lax.rem(n, 8), rows
            ].astype(F32)

        y_way = (r.y, r.y_stage, r.y_s, r.y_r)
        dx_way = (r.dx, r.dx_stage, r.dx_s, r.dx_r)

        def hand_out(way, k, value):
            way[1][k] = value.astype(F32).T.astype(BF16)
            for side in (0, 1):
                target = 2 * (h - 1) + side
                own = (k == s) & (target == h) & (d == owner)
                local, far = hand_copy(way, k, side)
                pl.when(own)(local.start)
                pl.when(jnp.logical_not(own))(far.start)

        def hand_copy(way, k, side):
            src = way[1].at[k, pl.ds(pl.multiple_of((2 * (h - 1) + side) * local, local), local)]
            dst = way[0].at[slot, :, pl.ds(pl.multiple_of(d * BLOCK, BLOCK), BLOCK)]
            recv = way[3].at[slot, d]
            return (
                pltpu.make_async_copy(src, dst, recv),
                remote(
                    src, dst, way[2].at[k, side], recv, at(k, 2 * (h - 1) + side, owner)
                ),
            )

        def finish_hand(way):
            @pl.when(mid)
            def _():
                for k in range(chunks):
                    for side in (0, 1):
                        own = (k == s) & (2 * (h - 1) + side == h) & (d == owner)
                        pl.when(jnp.logical_not(own))(hand_copy(way, k, side)[1].wait_send)

            for j in range(micro):
                for core in (0, 1):
                    arrived(
                        way[0].at[j, :, core * BLOCK : core * BLOCK + BLOCK],
                        way[3].at[j, core],
                    )

        def leave(n):
            c, k = lax.div(n, 4), lax.rem(n, 4)
            states = []
            for half in (0, 1):
                rows = slice(half * HALF, half * HALF + HALF)
                state = r.state[n, rows].astype(F32) + total_of(n, half) + r.par[c, 2:3]
                states.append(state.astype(BF16))

                @pl.when(c < 3)
                def _():
                    publish(c + 1, k, half, states[half])

            @pl.when(c == 3)
            def _():
                hand_out(y_way, k, jnp.concatenate(states, axis=0))

        def send_grad(index, half):
            rows = r.grad.at[index, half * HALF : half * HALF + HALF]
            return remote(
                rows, rows, r.gx_s.at[index * 2 + half], r.gx_r.at[index * 2 + half], mate_id
            )

        def enter_back(k):
            r.grad[12 + k] = turned(r.cot_in, r.xc_r, k)
            for half in (0, 1):
                send_grad(12 + k, half).start()

        def add_row(row, value):
            place = pl.ds(row, 1)
            r.small[place, :] = r.small[place, :] + value

        def leave_back(m):
            c, k = 3 - lax.div(m, 4), 3 - lax.rem(m, 4)
            index = c * 4 + k
            sums, belows = [], []
            for half in (0, 1):
                rows = slice(half * HALF, half * HALF + HALF)
                total = total_of(16 + m, half)
                scaled, inverse = norm_parts(r.state[index, rows].astype(F32))
                above = r.grad[index, rows].astype(F32)
                sums.append(
                    [
                        jnp.sum(value, axis=0, keepdims=True)
                        for value in (total * scaled, total, above)
                    ]
                )
                t = total * r.par[c, 0:1]
                inner = (
                    t
                    - jnp.mean(t, axis=-1, keepdims=True)
                    - scaled * jnp.mean(t * scaled, axis=-1, keepdims=True)
                )
                belows.append((above + inverse * inner).astype(BF16))

                @pl.when(c > 0)
                def _():
                    r.grad[index - 4, rows] = belows[half]
                    send_grad(index - 4, half).start()

            for i in range(3):
                add_row(c * 3 + i, sums[0][i] + sums[1][i])

            @pl.when(c == 0)
            def _():
                hand_out(dx_way, k, jnp.concatenate(belows, axis=0))

        def send_keys(l, step):
            ring = lax.rem(step, 2) * 4
            return remote(
                r.sums.at[pl.ds(ring, 4), 0:BLOCK],
                r.sums_in.at[pl.ds(step * 4, 4)],
                r.dk_s.at[l * 4 + step],
                r.dk_r.at[l * 4 + step],
                partner,
            )

        def attend_back(l, k):
            step = 3 - k
            ring = lax.rem(step, 2) * 4
            block = 2 * k + d
            start = block * BLOCK
            grad_merged = dot(r.grad[8 * l + k], r.wo[l], NT).astype(BF16)

            @pl.when(step >= 2)
            def _():
                send_keys(l, step - 2).wait_send()

            gate_total = jnp.zeros((256, 128), F32)
            for hh in range(3):
                where = (l * 4 + k) * 3 + hh
                near = pl.ds(pl.multiple_of(start, BLOCK), 192)
                keys = jnp.concatenate([r.kv[l * 4 + hh, near], r.chosen[where]], axis=0)
                mixed = grad_merged[:, hh * 128 : hh * 128 + 128]
                soft = r.soft[where]
                grad_soft = dot(mixed, keys, NT)
                grad_logits = (
                    soft * (grad_soft - jnp.sum(grad_soft * soft, axis=1, keepdims=True))
                ).astype(BF16)
                grad_query = dot(grad_logits, keys) * 0.125
                r.dqkv[k, :, hh * 256 : hh * 256 + 128] = jnp.where(
                    lane < 64, grad_query, 0.0
                ).astype(BF16)
                left = jnp.concatenate([grad_logits, soft.astype(BF16)], axis=0)
                right = jnp.concatenate(
                    [
                        jnp.concatenate([r.q[where], ones_tiles[hh]], axis=1),
                        jnp.concatenate([mixed, jnp.zeros_like(mixed)], axis=1),
                    ],
                    axis=0,
                )
                grad_set = dot(left, right, TN)
                far = grad_set[192:256]
                high = far.astype(BF16)
                r.far[hh, pl.ds(k * 128, 64)] = high
                r.far[hh, pl.ds(k * 128 + 64, 64)] = (far - high.astype(F32)).astype(BF16)
                hots = []
                for kk in range(4):
                    pick_row = r.pk[pl.ds(hh * 8 + 2 * kk + d, 1), :][:, 0:128]
                    hit = rows_of((256, 128)) + (start - BLOCK) == pick_row
                    hots.append((hit & (kk >= k)).astype(F32).astype(BF16))
                total = dot(jnp.concatenate(hots, axis=1), r.far[hh])
                r.sums[ring + hh, 0:WINDOW] = total[0:WINDOW, 0:128]
                r.sums[ring + hh, WINDOW:256] = total[WINDOW:256, 0:128] + grad_set[0:192, 0:128]
                gate_total = gate_total + total[:, 128:256]
            r.sums[ring + 3] = gate_total

            @pl.when(block > 0)
            def _():
                send_keys(l, step).start()

        def finish_back(l, k):
            step = 3 - k
            ring = lax.rem(step, 2) * 4
            came = step - d

            @pl.when(came >= 0)
            def _():
                arrived(r.sums_in.at[pl.ds(came * 4, 4)], r.dk_r.at[l * 4 + came])
                for j in range(4):
                    r.sums[ring + j, BLOCK:256] = (
                        r.sums[ring + j, BLOCK:256] + r.sums_in[came * 4 + j]
                    )

            scores = pieces(r.sums[ring + 3, BLOCK:256] * r.sig[l * 4 + k], lane)
            for hh in range(3):
                head = slice(hh * 256, hh * 256 + 128)
                r.dqkv[k, :, head] = jnp.where(
                    head_lanes(lane, hh), scores, r.dqkv[k, :, head]
                )
                r.dqkv[k, :, hh * 256 + 128 : hh * 256 + 256] = r.sums[
                    ring + hh, BLOCK:256
                ].astype(BF16)
            return dot(r.dqkv[k], r.w1[l])

        def feed_back(l, k, half):
            rows = slice(half * HALF, half * HALF + HALF)
            grad_hidden = dot(r.grad[8 * l + 4 + k, rows], r.pj[l], NT)
            grad_pre = (grad_hidden * r.slope[l * 4 + k, rows].astype(F32)).astype(BF16)
            r.dpre[k, rows] = grad_pre
            return dot(grad_pre, r.fc[l], NT)

        def four(ref, first):
            value = ref[pl.ds(first, 4)]
            return value.reshape(4 * BLOCK, value.shape[2])

        ones_rows = jnp.ones((8, 4 * BLOCK), BF16)

        def split(kind, width):
            for section in range(4):
                rows = pl.ds(pl.multiple_of((2 * section + 1 - d) * part_rows, 8), part_rows)
                halves[kind][0][section] = wides[kind][rows, 0:width].astype(BF16)
            send_half(kind).start()

        def send_half(kind):
            return remote(
                halves[kind][0],
                halves[kind][1],
                r.xh_s.at[kind],
                r.xh_r.at[kind],
                partner,
            )

        def send_share(kind, step):
            return remote(
                shares[kind][0].at[step - 1],
                shares[kind][1].at[step - 1],
                r.yh_s.at[kind, step - 1],
                r.yh_r.at[kind, step - 1],
                at(lax.rem(s + step, 4), h, d),
            )

        def share(kind, width):
            arrived(halves[kind][1], r.xh_r.at[kind])
            send_half(kind).wait_send()
            for step in (1, 2, 3, 0):
                section = lax.rem(s + step, 4)
                rows = pl.ds(pl.multiple_of((2 * section + d) * part_rows, 8), part_rows)
                both = wides[kind][rows, 0:width] + halves[kind][1][section].astype(F32)
                if step:
                    shares[kind][0][step - 1] = both.astype(BF16)
                    send_share(kind, step).start()
                else:
                    wides[kind][rows, 0:width] = both

        def collect(kind, width):
            rows = pl.ds(pl.multiple_of((2 * s + d) * part_rows, 8), part_rows)
            total = wides[kind][rows, 0:width]
            for step in (1, 2, 3):
                arrived(shares[kind][1].at[step - 1], r.yh_r.at[kind, step - 1])
                total = total + shares[kind][1][step - 1].astype(F32)
                send_share(kind, step).wait_send()
            return total

        def weights_feed(l, part):
            left = four(r.normed, 8 * l + 4) if part < 2 else four(r.grad, 8 * l + 4)
            right = four(r.dpre, 0) if part < 2 else four(r.hidden, 4 * l)
            rows = slice(part % 2 * 384, part % 2 * 384 + 384)
            columns = slice(part // 2 * 768, part // 2 * 768 + 768)
            r.wide_f[rows, columns] = dot(left[:, rows], right, TN)
            if part == 0:
                add_row(18 + l, dot(ones_rows, right)[0:1])
            if part == 3:
                split(0, 1536)

        def weights_attend(l, part):
            wide_lane = lanes((4 * BLOCK, 128))
            if part == 0:
                grads = four(r.dqkv, 0)
                t = [grads[:, i * 256 : i * 256 + 128].astype(F32) for i in range(3)]
                first = jnp.where(wide_lane < 64, t[0], pltpu.roll(t[1], 64, 1))
                second = jnp.where(wide_lane < 64, t[2], t[0] + t[1] + t[2])
                r.packed[:, 0:128] = first.astype(BF16)
                r.packed[:, 128:256] = second.astype(BF16)
                for i in range(3):
                    r.packed[:, 256 + 128 * i : 384 + 128 * i] = grads[
                        :, i * 256 + 128 : i * 256 + 256
                    ]
                add_row(16 + l, dot(ones_rows, grads)[0:1])
            if part < 2:
                rows = slice(part * 384, part * 384 + 384)
                r.wide_a[rows, 0:640] = dot(four(r.normed, 8 * l)[:, rows], r.packed[...], TN)
            if part == 2:
                merged = four(r.merged, 4 * l)
                u = [merged[:, i * 128 : i * 128 + 128].astype(F32) for i in range(3)]
                packed = jnp.concatenate(
                    [
                        jnp.where(wide_lane < 64, pltpu.roll(u[0], 64, 1), u[1]),
                        jnp.where(wide_lane < 64, pltpu.roll(u[2], 64, 1), 0.0),
                    ],
                    axis=1,
                ).astype(BF16)
                r.wide_a[:, 640:896] = dot(four(r.grad, 8 * l), packed, TN)
            if part == 3:
                send_keys(l, 2).wait_send()

                @pl.when(d == 1)
                def _():
                    send_keys(l, 3).wait_send()

                scores = dot(r.packed[:, 128:256], four(r.normed, 8 * l), TN)
                for hh in range(3):
                    row = 64 + 3 * hh
                    add_row(
                        24 + 4 * l + hh,
                        scores[row : row + 1] + scores[row + 1 : row + 2] + scores[row + 2 : row + 3],
                    )
                split(1, 896)

        def collect_feed(l):
            total = collect(0, 1536)
            r.o_fc[l] = total[:, 0:768]
            r.o_pj[l] = total[:, 768:1536]

        def collect_attend(l):
            total = collect(1, 896)
            r.o_qkv[3 * l] = total[:, 0:192]
            for i in (0, 1):
                r.o_qkv[3 * l + 1 + i] = jnp.concatenate(
                    [total[:, 256 + 128 * j + 64 * i : 320 + 128 * j + 64 * i] for j in range(3)],
                    axis=1,
                )
            r.o_out[l] = total[:, 640:896].T[0:192]

        def slot_of(n, carry):
            ahead = n < 16
            c = jnp.where(ahead, lax.div(n, 4), 7 - lax.div(n, 4))
            k = jnp.where(ahead, lax.rem(n, 4), 3 - lax.rem(n, 4))
            l = lax.div(c, 2)
            works = n < 32
            attends = lax.rem(c, 2) == 0

            @pl.when(mid & (n < 4))
            def _():
                enter(n)

            @pl.when(mid & (n >= 4) & (n < 20))
            def _():
                leave(n - 4)

            @pl.when(mid & (n >= 12) & (n < 16))
            def _():
                enter_back(15 - n)

            @pl.when(mid & (n >= 20))
            def _():
                leave_back(n - 20)

            def come(half):
                rows = slice(half * HALF, half * HALF + HALF)

                @pl.when(jnp.logical_not(mid) & ahead)
                def _():
                    arrived(r.normed.at[n, rows], r.nx_r.at[n * 2 + half])

                @pl.when(jnp.logical_not(mid) & jnp.logical_not(ahead) & works)
                def _():
                    index = c * 4 + k
                    arrived(r.grad.at[index, rows], r.gx_r.at[index * 2 + half])

            @pl.when(attends)
            def _():
                come(0)
                come(1)

            @pl.when((n == 0) | (n == 8))
            def _():
                for copy in attend_loads[0:12]:
                    pltpu.make_async_copy(copy.src_ref, copy.dst_ref, r.load.at[l]).wait()

            @pl.when(n == 4)
            def _():
                for copy in feed_loads:
                    copy.wait()

            @pl.when(ahead & attends)
            def _():
                project(l, k)

            @pl.when(n == 0)
            def _():
                for copy in pick_copies:
                    copy.wait()
                chosen = r.pk_in[owner, slot]
                r.pk[...] = jnp.concatenate(
                    [chosen, chosen, jnp.zeros((32, 192), jnp.int32), chosen], axis=1
                )
                square = jnp.concatenate([chosen.astype(F32), jnp.zeros((32, 64), F32)], axis=1)
                square = jnp.concatenate([square, jnp.zeros((96, 128), F32)], axis=0)
                r.pt[...] = square.T[0:64]

            @pl.when(ahead & attends)
            def _():
                came = k - 1 + d
                pl.when(came >= 0)(lambda: wait_kv(l, came))
                give_both(n, attend(l, k))

            @pl.when(ahead & jnp.logical_not(attends))
            def _():
                for half in (0, 1):
                    come(half)
                    give(n, half, feed(l, k, half))

            @pl.when(jnp.logical_not(ahead) & works & attends)
            def _():
                attend_back(l, k)
                give_both(n, finish_back(l, k))

            @pl.when(jnp.logical_not(ahead) & works & jnp.logical_not(attends))
            def _():
                for half in (0, 1):
                    come(half)
                    give(n, half, feed_back(l, k, half))

            @pl.when(mid & (n >= 2) & (n < 34))
            def _():
                fold(n - 2)

            for part in range(4):

                @pl.when((n == 20 + part // 2) | (n == 28 + part // 2))
                def _():
                    weights_feed(lax.div(29 - n, 8), part)

                @pl.when((n == 24 + part // 2) | (n == 31 + part // 2))
                def _():
                    weights_attend(lax.div(32 - n, 7), part)

            @pl.when((n == 26) | (n == 33))
            def _():
                collect_feed(lax.div(33 - n, 7))

            @pl.when((n == 30) | (n == 35))
            def _():
                collect_attend(lax.div(35 - n, 5))

            @pl.when((n == 22) | (n == 30))
            def _():
                share(0, 1536)

            @pl.when((n == 26) | (n == 33))
            def _():
                share(1, 896)

            return carry

        lax.fori_loop(0, 36, slot_of, 0)

        def send_rows():
            return remote(
                r.small.at[0:16],
                r.small.at[0:16],
                r.sm_s.at[0],
                r.sm_r.at[0],
                mate_id,
            )

        @pl.when(mid)
        def _():
            send_rows().start()

        @pl.when(jnp.logical_not(mid))
        def _():
            arrived(r.small.at[0:16], r.sm_r.at[0])

        swap = remote(r.small, r.small_in, r.sm_s.at[1], r.sm_r.at[1], partner)
        swap.start()
        swap.wait()
        r.small_all[s] = r.small[...] + r.small_in[...]

        def send_small(step):
            return remote(
                r.small_all.at[s],
                r.small_all.at[s],
                r.sm_s.at[1 + step],
                r.sm_r.at[2 + s],
                at(lax.rem(s + step, 4), h, d),
            )

        for step in (1, 2, 3):
            send_small(step).start()
        for step in (1, 2, 3):
            section = lax.rem(s + step, 4)
            arrived(r.small_all.at[section], r.sm_r.at[2 + section])

        @pl.when(mid)
        def _():
            send_rows().wait_send()

        r.small[...] = (r.small_all[0] + r.small_all[1]) + (
            r.small_all[2] + r.small_all[3]
        )
        for j in range(4):

            @pl.when(h == j)
            def _():
                for i, ref in enumerate((r.o_gain, r.o_bias, r.o_ob)):
                    ref[...] = r.small[pl.ds(s * 3 + i, 1), :][:, j * 192 : j * 192 + 192]

        for l in (0, 1):
            row = r.small[16 + l : 17 + l, :]
            for i in (0, 1):
                r.o_qv[l, i : i + 1, :] = jnp.concatenate(
                    [row[:, j * 256 + 192 * i : j * 256 + 192 * i + 64] for j in range(3)], axis=1
                )
            for j in range(3):
                r.o_score[j, l : l + 1, :] = r.small[
                    24 + 4 * l + j : 25 + 4 * l + j, :
                ]
        r.o_fcb[...] = r.small[18:20, :]

        finish_hand(y_way)
        finish_hand(dx_way)
        for step in (1, 2, 3):
            send_small(step).wait_send()

        @pl.when(d == owner)
        def _():
            for copies in stream_parts + cot_parts:
                sent(copies)

        sent(norm_rows)

        def drain_kv(i, carry):
            send_kv(lax.div(i, 4), lax.rem(i, 4)).wait_send()
            return carry

        lax.fori_loop(0, 8, drain_kv, 0)

        @pl.when(d == 0)
        def _():
            wait_kv(0, 3)
            wait_kv(1, 3)

        @pl.when(mid)
        def _():
            def drain(i, carry):
                for half in (0, 1):
                    send_normed(i, half).wait_send()
                    send_grad(i, half).wait_send()
                return carry

            lax.fori_loop(0, 16, drain, 0)
            for n in range(28, 32):
                for half in (0, 1):
                    send_pair(n, half).wait_send()

        @pl.when(jnp.logical_not(mid))
        def _():
            for n in range(28, 32):
                for half in (0, 1):
                    send_part(n, half).wait_send()

    return kernel


def hand_over(*refs):
    count = len(refs) // 2
    for i in range(count):
        refs[count + i][...] = refs[i][...]


def shards(
    stream,
    cotangent,
    lengths,
    picks,
    norm_gain,
    norm_bias,
    out_bias,
    weight_qkv,
    bias_qv,
    weight_score,
    weight_out,
    weight_fc,
    bias_fc,
    weight_proj,
):
    micro, tokens, local = stream.shape
    layers, width = weight_qkv.shape[0], weight_qkv.shape[1]
    inputs = dict(
        stream=stream.transpose(0, 2, 1),
        cot=cotangent.transpose(0, 2, 1),
        lengths=lengths,
        picks=picks.reshape(micro, 24, 64),
        gain=norm_gain,
        shift=norm_bias,
        ob=out_bias,
        wqkv=weight_qkv.transpose(0, 2, 3, 1),
        bqv=bias_qv,
        wscore=weight_score.transpose(2, 0, 1),
        wout=weight_out,
        wfc=weight_fc,
        bfc=bias_fc,
        wpj=weight_proj,
    )
    spaces = dict(
        stream=pl.ANY, cot=pl.ANY, lengths=pltpu.SMEM, wqkv=pl.ANY, wout=pl.ANY, wfc=pl.ANY, wpj=pl.ANY
    )
    part_rows = width // 8
    outputs = dict(
        y=((micro, local, 2 * BLOCK), BF16),
        dx=((micro, local, 2 * BLOCK), BF16),
        o_gain=((1, 192), F32),
        o_bias=((1, 192), F32),
        o_ob=((1, 192), F32),
        o_qkv=((6, part_rows, 192), F32),
        o_qv=((2, 2, 192), F32),
        o_score=((3, 2, 768), F32),
        o_out=((2, 192, part_rows), F32),
        o_fc=((2, part_rows, 768), F32),
        o_fcb=((2, 768), F32),
        o_pj=((2, part_rows, 768), F32),
    )
    dma = pltpu.SemaphoreType.DMA
    scratch = dict(
        stream_in=((4, 768, BLOCK), BF16),
        cot_in=((4, 768, BLOCK), BF16),
        prm=((16, 768), BF16),
        w1=((2, 768, 768), BF16),
        wo=((2, 384, 768), BF16),
        fc=((2, 768, 768), BF16),
        pj=((2, 768, 768), BF16),
        bq=((2, 1, 768), F32),
        fcb=((2, 1, 768), F32),
        prm_in=((4, 4, 16, 768), BF16),
        par=((4, 8, 768), F32),
        pk_out=((micro, 32, 64), jnp.int32),
        pk_in=((2, micro, 32, 64), jnp.int32),
        pk=((32, 384), jnp.int32),
        pt=((64, 128), F32),
        state=((16, BLOCK, 768), BF16),
        normed=((16, BLOCK, 768), BF16),
        q=((24, BLOCK, 128), BF16),
        sig=((8, BLOCK, 128), F32),
        kv=((8, WINDOW + tokens, 128), BF16),
        chosen=((24, 64, 128), BF16),
        keyset=((3, 256, 256), BF16),
        soft=((24, BLOCK, 256), F32),
        merged=((8, BLOCK, 384), BF16),
        hidden=((8, BLOCK, 768), BF16),
        slope=((8, BLOCK, 768), BF16),
        part_out=((4, BLOCK, 768), BF16),
        part_in=((8, BLOCK, 768), BF16),
        own=((4, BLOCK, 768), F32),
        pair_out=((4, BLOCK, 768), BF16),
        pair_in=((8, BLOCK, 768), BF16),
        y_stage=((4, 768, BLOCK), BF16),
        dx_stage=((4, 768, BLOCK), BF16),
        grad=((16, BLOCK, 768), BF16),
        dpre=((4, BLOCK, 768), BF16),
        dqkv=((4, BLOCK, 768), BF16),
        far=((3, 512, 256), BF16),
        sums=((8, 256, 128), F32),
        sums_in=((16, BLOCK, 128), F32),
        wide_f=((768, 1536), F32),
        wide_a=((768, 896), F32),
        packed=((512, 640), BF16),
        xo_f=((4, part_rows, 1536), BF16),
        xi_f=((4, part_rows, 1536), BF16),
        yo_f=((3, part_rows, 1536), BF16),
        yi_f=((3, part_rows, 1536), BF16),
        xo_a=((4, part_rows, 896), BF16),
        xi_a=((4, part_rows, 896), BF16),
        yo_a=((3, part_rows, 896), BF16),
        yi_a=((3, part_rows, 896), BF16),
        small=((32, 768), F32),
        small_in=((32, 768), F32),
        small_all=((4, 32, 768), F32),
    )
    sems = dict(
        xs_s=(4, 4),
        xs_r=(4, 4),
        xc_s=(4, 4),
        xc_r=(4, 4),
        load=(3,),
        prm_s=(4, 2),
        prm_r=(4, 4),
        pick_s=(2,),
        pick_r=(1,),
        nx_s=(32,),
        nx_r=(32,),
        kv_s=(8,),
        kv_r=(8,),
        ps_s=(64,),
        ps_r=(64,),
        mm_s=(64,),
        mm_r=(64,),
        y_s=(4, 2),
        y_r=(2, 2),
        dx_s=(4, 2),
        dx_r=(2, 2),
        gx_s=(32,),
        gx_r=(32,),
        dk_s=(8,),
        dk_r=(8,),
        xh_s=(2,),
        xh_r=(2,),
        yh_s=(2, 3),
        yh_r=(2, 3),
        sm_s=(5,),
        sm_r=(6,),
    )
    names = list(inputs) + list(outputs) + list(scratch) + list(sems)
    results = pl.pallas_call(
        make_kernel(names, micro, width // 8, local),
        out_shape=[jax.ShapeDtypeStruct(*spec) for spec in outputs.values()],
        in_specs=[
            pl.BlockSpec(memory_space=spaces.get(name, pltpu.VMEM))
            for name in inputs
        ],
        out_specs=[pl.BlockSpec(memory_space=pltpu.VMEM) for name in outputs],
        scratch_shapes=[pltpu.VMEM(*spec) for spec in scratch.values()]
        + [dma(shape) for shape in sems.values()],
        compiler_params=pltpu.CompilerParams(
            collective_id=0, has_side_effects=True, vmem_limit_bytes=62 * 2**20
        ),
        name="blocks",
    )(*inputs.values())
    results = pl.pallas_call(
        hand_over,
        out_shape=[jax.ShapeDtypeStruct(*spec) for spec in outputs.values()],
        in_specs=[pl.BlockSpec(memory_space=pltpu.VMEM)] * len(outputs),
        out_specs=[pl.BlockSpec(memory_space=pltpu.VMEM)] * len(outputs),
        name="results",
    )(*results)
    o = types.SimpleNamespace(**dict(zip(outputs, results)))
    dp_count = lax.axis_size("dp")
    if dp_count > 2:
        d = lax.rem(lax.axis_index("dp"), 2)

        def scattered(value):
            placed = jnp.zeros((value.shape[0], 2 * part_rows, value.shape[2]), F32)
            placed = lax.dynamic_update_slice(placed, value, (0, d * part_rows, 0))
            return lax.psum_scatter(placed, "dp", scatter_dimension=1, tiled=True)

        o.o_out = scattered(o.o_out.transpose(0, 2, 1)).transpose(0, 2, 1)
        o.o_qkv, o.o_fc, o.o_pj = map(scattered, (o.o_qkv, o.o_fc, o.o_pj))
        sums = (o.o_gain, o.o_bias, o.o_ob, o.o_qv, o.o_score, o.o_fcb)
        o.o_gain, o.o_bias, o.o_ob, o.o_qv, o.o_score, o.o_fcb = jax.tree.map(
            lambda value: 0.5 * value, lax.psum(sums, "dp")
        )
    rows = o.o_fc.shape[1]
    return (
        o.y.transpose(0, 2, 1),
        o.dx.transpose(0, 2, 1),
        o.o_gain,
        o.o_bias,
        o.o_ob,
        o.o_qkv.reshape(layers, 3, rows, 192).transpose(0, 2, 1, 3),
        o.o_qv,
        o.o_score.transpose(1, 2, 0),
        o.o_out,
        o.o_fc,
        o.o_fcb,
        o.o_pj.transpose(0, 2, 1),
    )


def solution(mesh):
    return jax.shard_map(
        shards,
        mesh=mesh,
        in_specs=(
            P("dp", None, "head"),
            P("dp", None, "head"),
            P("dp"),
            P("dp", "head", None, None),
            P("section", None),
            P("section", None),
            P("section", "head"),
            P(None, None, None, "head"),
            P(None, None, "head"),
            P(None, None, "head"),
            P(None, "head", None),
            P(None, None, "head"),
            P(None, "head"),
            P(None, "head", None),
        ),
        out_specs=(
            P("dp", "section", "head"),
            P("dp", "section", "head"),
            P("section", "head"),
            P("section", "head"),
            P("section", "head"),
            P(None, ("section", "dp"), None, "head"),
            P(None, None, "head"),
            P(None, None, "head"),
            P(None, "head", ("section", "dp")),
            P(None, ("section", "dp"), "head"),
            P(None, "head"),
            P(None, "head", ("section", "dp")),
        ),
        check_vma=False,
    )
```

```python
import types

import jax
import jax.numpy as jnp
from jax import lax
from jax.experimental import pallas as pl
from jax.experimental.pallas import tpu as pltpu
from jax.sharding import PartitionSpec as P

MESH = pl.DeviceIdType.MESH
BLOCK = 128
HALF = 64
DIRECT = 1
WINDOW = 64
NT = (((1,), (1,)), ((), ()))
TN = (((0,), (0,)), ((), ()))
F32 = jnp.float32
BF16 = jnp.bfloat16
ROOT = 0.7978845608028654
CUBE = 0.044715


def dot(left, right, dims=(((1,), (0,)), ((), ()))):
    return lax.dot_general(left, right, dims, preferred_element_type=F32)


def lanes(shape):
    return lax.broadcasted_iota(jnp.int32, shape, len(shape) - 1)


def rows_of(shape):
    return lax.broadcasted_iota(jnp.int32, shape, len(shape) - 2)


def head_lanes(lane, hh):
    return (lane >= 64 + 3 * hh) & (lane < 67 + 3 * hh)


def pieces(value, lane):
    high = value.astype(BF16)
    rest = value - high.astype(F32)
    middle = rest.astype(BF16)
    low = (rest - middle.astype(F32)).astype(BF16)
    zero = jnp.zeros_like(high)
    used = (lane >= 64) & (lane < 73)
    which = lax.rem(lane - 64 + 3 * 64, 3)
    return jnp.where(
        used & (which == 0),
        high,
        jnp.where(used & (which == 1), middle, jnp.where(used & (which == 2), low, zero)),
    )


def make_kernel(names, micro, part_rows, local):
    def kernel(*refs):
        r = types.SimpleNamespace(**dict(zip(names, refs)))
        wides = (r.wide_f, r.wide_a)
        halves = ((r.xo_f, r.xi_f), (r.xo_a, r.xi_a))
        shares = ((r.yo_f, r.yi_f), (r.yo_a, r.yi_a))
        s, h, dp = lax.axis_index("section"), lax.axis_index("head"), lax.axis_index("dp")
        d = lax.rem(dp, 2)
        pair = dp - d
        mid = (h == 1) | (h == 2)
        mate = h + 1 - 2 * lax.rem(h, 2)
        other = 3 - h
        owner = lax.div(s, micro)
        slot = lax.rem(s, micro)

        def at(section, head, core):
            return (section, head, pair + core)

        def remote(src, dst, send, recv, device):
            return pltpu.make_async_remote_copy(
                src_ref=src,
                dst_ref=dst,
                send_sem=send,
                recv_sem=recv,
                device_id=device,
                device_id_type=MESH,
            )

        partner = at(s, h, 1 - d)
        mate_id = at(s, mate, d)
        other_id = at(s, other, d)

        def arrived(dst, recv):
            remote(dst, dst, recv, recv, partner).wait_recv()

        barrier = pltpu.get_barrier_semaphore()
        flat = (s * 4 + h) * 2 + d

        def greet(step, carry):
            whom = lax.rem(flat + step, 32)
            pl.semaphore_signal(
                barrier,
                inc=1,
                device_id=at(lax.div(whom, 8), lax.rem(lax.div(whom, 2), 4), lax.rem(whom, 2)),
                device_id_type=MESH,
            )
            return carry

        lax.fori_loop(1, 32, greet, 0)

        attend_loads, feed_loads = [], []
        for l in range(2):
            for hh in range(3):
                rows = slice(hh * 64, hh * 64 + 64)
                for part, place in ((0, 0), (1, 128), (2, 192)):
                    attend_loads.append(
                        pltpu.make_async_copy(
                            r.wqkv.at[l, part, rows],
                            r.w1.at[l, hh * 256 + place : hh * 256 + place + 64],
                            r.load.at[l],
                        )
                    )
                attend_loads.append(
                    pltpu.make_async_copy(
                        r.wout.at[l, rows],
                        r.wo.at[l, hh * 128 + 64 : hh * 128 + 128],
                        r.load.at[l],
                    )
                )
            feed_loads.append(pltpu.make_async_copy(r.wfc.at[l], r.fc.at[l], r.load.at[2]))
            feed_loads.append(pltpu.make_async_copy(r.wpj.at[l], r.pj.at[l], r.load.at[2]))

        for copy in attend_loads + feed_loads:
            copy.start()

        r.nrm[...] = jnp.zeros_like(r.nrm)
        r.sm[...] = jnp.zeros_like(r.sm)
        for j in range(micro):
            r.pk_out[j, 0:24] = r.picks[j]
            r.pk_out[j, 24:32] = jnp.zeros((8, 64), jnp.int32) + r.lengths[j]
        wide_bias = jnp.concatenate([r.ob[...].astype(F32)] * 4, axis=1)
        wide_bias = jnp.where(
            (lanes((1, 768)) >= h * local) & (lanes((1, 768)) < h * local + local), wide_bias, 0.0
        )
        row = rows_of((16, 768))
        r.prm[...] = jnp.where(
            row == 0,
            r.gain[...].astype(F32),
            jnp.where(
                row == 1, r.shift[...].astype(F32), jnp.where(row == 2, wide_bias, 0.0)
            ),
        ).astype(BF16)

        r.keyset[...] = jnp.zeros_like(r.keyset)
        r.far[...] = jnp.zeros_like(r.far)
        r.kv[:, 0:WINDOW] = jnp.zeros((8, WINDOW, 128), BF16)
        for l in range(2):
            for hh in range(3):
                score = jnp.where(
                    (rows_of((64, 768)) >= 3 * hh) & (rows_of((64, 768)) < 3 * hh + 3),
                    r.wscore[hh, l : l + 1, :].astype(F32),
                    0.0,
                )
                r.w1[l, hh * 256 + 64 : hh * 256 + 128] = score.astype(BF16)
                r.wo[l, hh * 128 : hh * 128 + 64] = jnp.zeros((64, 768), BF16)
            gap = jnp.zeros((1, 128), F32)
            r.fcb[l] = r.bfc[l : l + 1, :].astype(F32)
            bias = r.bqv[l].astype(F32)
            r.bq[l] = jnp.concatenate(
                [
                    piece
                    for hh in range(3)
                    for piece in (
                        bias[0:1, hh * 64 : hh * 64 + 64],
                        gap,
                        bias[1:2, hh * 64 : hh * 64 + 64],
                    )
                ],
                axis=1,
            )

        pl.semaphore_wait(barrier, 31)

        def spread(source, landing, sends, recvs, k, heads):
            copies = []
            for hm in heads:
                for core in (0, 1):
                    src = source.at[slot, :, (2 * k + core) * BLOCK : (2 * k + core + 1) * BLOCK]
                    dst = landing.at[k, pl.ds(pl.multiple_of(h * local, local), local)]
                    recv = recvs.at[h, k]
                    copies.append(
                        (
                            (h == hm) & (d == core),
                            pltpu.make_async_copy(src, dst, recv),
                            remote(
                                src, dst, sends.at[hm * 2 + core, k], recv, at(s, hm, core)
                            ),
                        )
                    )
            return copies

        def launch(copies):
            for own, local, far in copies:
                pl.when(own)(local.start)
                pl.when(jnp.logical_not(own))(far.start)

        def sent(copies):
            for own, local, far in copies:
                pl.when(jnp.logical_not(own))(far.wait_send)

        chunks = 4
        stream_parts = [
            spread(r.stream, r.stream_in, r.xs_s, r.xs_r, k, (1, 2, 0, 3)[: 4 if k < DIRECT else 2])
            for k in range(chunks)
        ]
        cot_parts = [
            spread(r.cot, r.cot_in, r.xc_s, r.xc_r, k, (1, 2)) for k in range(chunks)
        ]
        norm_rows = []
        for step in range(4):
            section = lax.rem(s + step, 4)
            for hm in (1, 2):
                norm_rows.append(
                    (
                        (h == hm) if step == 0 else (h == 4),
                        pltpu.make_async_copy(
                            r.prm, r.prm_in.at[s, h], r.prm_r.at[s, h]
                        ),
                        remote(
                            r.prm,
                            r.prm_in.at[s, h],
                            r.prm_s.at[step, hm - 1],
                            r.prm_r.at[s, h],
                            at(section, hm, d),
                        ),
                    )
                )
        end_rows = [
            (
                s == step,
                pltpu.make_async_copy(r.prm, r.prm_in.at[0, h], r.prm_r.at[0, h]),
                remote(
                    r.prm, r.prm_in.at[0, h], r.prm_e.at[step], r.prm_r.at[0, h], at(step, h, d)
                ),
            )
            for step in range(4)
        ]
        pick_copies = (
            pltpu.make_async_copy(r.pk_out, r.pk_in.at[d], r.pick_s.at[0]),
            remote(r.pk_out, r.pk_in.at[d], r.pick_s.at[1], r.pick_r.at[0], partner),
        )

        launch(norm_rows)

        @pl.when((s == 0) & jnp.logical_not(mid))
        def _():
            launch(end_rows)

        @pl.when(d == owner)
        def _():
            for copies in stream_parts:
                launch(copies)

        for copy in pick_copies:
            copy.start()

        lane = lanes((BLOCK, 128))
        ones_tiles = [jnp.where(head_lanes(lane, hh), 1.0, 0.0).astype(BF16) for hh in range(3)]

        def norm_parts(x):
            center = x - jnp.mean(x, axis=-1, keepdims=True)
            inverse = lax.rsqrt(jnp.mean(center * center, axis=-1, keepdims=True) + 1e-05)
            return center * inverse, inverse

        def prepare():
            @pl.when(mid)
            def _():
                for c in range(4):
                    for j in range(4):
                        arrived(r.prm_in.at[c, j], r.prm_r.at[c, j])
                for c in range(4):
                    mine = r.prm_in[c, h].astype(F32)
                    bias = mine[2:3, :] * 0.0
                    for j in range(4):
                        bias = bias + r.prm_in[c, j].astype(F32)[2:3, :]
                    r.par[c, 0:1] = mine[0:1]
                    r.par[c, 1:2] = mine[1:2]
                    r.par[c, 2:3] = bias

            @pl.when(jnp.logical_not(mid))
            def _():
                arrived(r.prm_in.at[0, h], r.prm_r.at[0, h])
                mine = r.prm_in[0, h].astype(F32)
                r.par[0, 0:1] = mine[0:1]
                r.par[0, 1:2] = mine[1:2]

        def publish(c, k, half, state):
            rows = slice(half * HALF, half * HALF + HALF)
            r.state[c * 4 + k, rows] = state
            scaled, _ = norm_parts(state.astype(F32))
            normed = scaled * r.par[c, 0:1] + r.par[c, 1:2]
            r.normed[c * 4 + k, rows] = normed.astype(BF16)
            send_normed(c * 4 + k, half).start()

        def send_normed(n, half):
            rows = r.normed.at[n, half * HALF : half * HALF + HALF]
            return remote(rows, rows, r.nx_s.at[n * 2 + half], r.nx_r.at[n * 2 + half], mate_id)

        def turned(landing, recvs, k):
            for j in range(4):
                arrived(landing.at[k, j * local : j * local + local], recvs.at[j, k])
            return landing[k].astype(F32).T.astype(BF16)

        def enter(k):
            @pl.when(k == 0)
            def _():
                prepare()

            state = turned(r.stream_in, r.xs_r, k)
            r.state[k] = state
            scaled, _ = norm_parts(state.astype(F32))
            r.normed[k] = (scaled * r.par[0, 0:1] + r.par[0, 1:2]).astype(BF16)

            @pl.when(k >= DIRECT)
            def _():
                for half in (0, 1):
                    send_normed(k, half).start()

        def project(l, k):
            x = r.normed[8 * l + k]
            block = 2 * k + d
            place = pl.ds(pl.multiple_of(WINDOW + block * BLOCK, WINDOW), BLOCK)
            score = jnp.zeros((BLOCK, 128), F32)
            for hh in range(3):
                out = dot(x, r.w1[l, hh * 256 : hh * 256 + 256, :], NT)
                out = out + r.bq[l, :, hh * 256 : hh * 256 + 256]
                q, kv = out[:, :128], out[:, 128:]
                r.q[(l * 4 + k) * 3 + hh] = jnp.where(lane < 64, q, 0.0).astype(
                    BF16
                ) * jnp.asarray(0.125, BF16)
                score = score + jnp.where(head_lanes(lane, hh), q, 0.0)
                r.kv[l * 4 + hh, place] = kv.astype(BF16)
            gates = jnp.minimum(score, 0.0) - jnp.log1p(jnp.exp(-jnp.abs(score)))
            r.sig[l * 4 + k] = 1.0 / (1.0 + jnp.exp(score))
            r.kv[l * 4 + 3, place] = pieces(gates, lane)
            send_kv(l, k).start()

        def send_kv(l, k):
            place = pl.ds(pl.multiple_of(WINDOW + (2 * k + d) * BLOCK, WINDOW), BLOCK)
            rows = r.kv.at[pl.ds(l * 4, 4), place]
            return remote(rows, rows, r.kv_s.at[l * 4 + k], r.kv_r.at[l * 4 + k], partner)

        def wait_kv(l, k):
            place = pl.ds(pl.multiple_of(WINDOW + (2 * k + 1 - d) * BLOCK, WINDOW), BLOCK)
            arrived(r.kv.at[pl.ds(l * 4, 4), place], r.kv_r.at[l * 4 + k])

        def attend(l, k):
            block = 2 * k + d
            start = block * BLOCK
            length = r.pk[24:25, 0:1]
            column = lanes((BLOCK, 256))
            row = rows_of((BLOCK, 256))
            distance = row + WINDOW - column
            near_pos = start - WINDOW + column
            near_ok = (
                (column < 192)
                & (near_pos >= 0)
                & (distance >= 0)
                & (distance < WINDOW)
                & ((near_pos < length) | (distance == 0))
            )
            pick_cols = [
                jnp.sum(
                    jnp.where(lanes((64, 128)) == hh * 8 + block, r.pt[...], 0.0),
                    axis=1,
                    keepdims=True,
                ).astype(jnp.int32)
                for hh in range(3)
            ]

            def some(first, count):
                rows = pl.ds(pl.multiple_of(WINDOW + first, WINDOW), count)
                place = lanes((64, count)) + first
                gates = r.kv[l * 4 + 3, rows]
                return tuple(
                    dot(
                        (place == pick_cols[hh]).astype(F32).astype(BF16),
                        jnp.concatenate([r.kv[l * 4 + hh, rows], gates], axis=1),
                    )
                    for hh in range(3)
                )

            def adding(totals, more):
                return tuple(total + one for total, one in zip(totals, more))

            totals = some(pl.multiple_of(k * 256, 256), BLOCK)
            totals = lax.fori_loop(0, k, lambda j, t: adding(t, some(j * 256, 256)), totals)
            totals = lax.fori_loop(0, d, lambda j, t: adding(t, some(start, BLOCK)), totals)
            near = pl.ds(pl.multiple_of(start, BLOCK), 192)
            for hh in range(3):
                index = hh * 8 + block
                chosen = totals[hh].astype(BF16)
                where = (l * 4 + k) * 3 + hh
                r.chosen[where] = chosen[:, 0:128]
                r.keyset[hh, 0:192, 0:128] = r.kv[l * 4 + hh, near]
                r.keyset[hh, 192:256, :] = chosen
                query = jnp.concatenate([r.q[where], ones_tiles[hh]], axis=1)
                logits = dot(query, r.keyset[hh], NT)
                pick_row = r.pk[pl.ds(index, 1), :][:, 128:384]
                far_ok = (
                    (column >= 192) & (pick_row <= start - WINDOW + row) & (pick_row < length)
                )
                masked = jnp.where(near_ok | far_ok, logits, -1e30)
                raised = jnp.exp(masked - jnp.max(masked, axis=1, keepdims=True))
                soft = raised / jnp.sum(raised, axis=1, keepdims=True)
                r.soft[where] = soft
                mixed = dot(soft.astype(BF16), r.keyset[hh, :, 0:128])
                r.merged[l * 4 + k, :, hh * 128 : hh * 128 + 128] = mixed.astype(BF16)
            return dot(r.merged[l * 4 + k], r.wo[l])

        def feed(l, k, half):
            rows = slice(half * HALF, half * HALF + HALF)
            pre = dot(r.normed[8 * l + 4 + k, rows], r.fc[l]) + r.fcb[l]
            square = pre * pre
            wave = jnp.tanh(ROOT * pre * (1.0 + CUBE * square))
            both = 0.5 * (1.0 + wave)
            slope = both + 0.5 * pre * (1.0 - wave * wave) * (ROOT * (1.0 + 3.0 * CUBE * square))
            hidden = (pre * both).astype(BF16)
            r.hidden[l * 4 + k, rows] = hidden
            r.slope[l * 4 + k, rows] = slope.astype(BF16)
            return dot(hidden, r.pj[l])

        def send_part(n, half):
            rows = pl.ds(half * HALF, HALF)
            return remote(
                r.part_out.at[lax.rem(n, 4), rows],
                r.part_in.at[lax.rem(n, 8), rows],
                r.ps_s.at[n * 2 + half],
                r.ps_r.at[n * 2 + half],
                mate_id,
            )

        def give(n, half, part):
            rows = slice(half * HALF, half * HALF + HALF)

            @pl.when(mid)
            def _():
                r.own[lax.rem(n, 4), rows] = part

            @pl.when(jnp.logical_not(mid))
            def _():
                @pl.when(n >= 4)
                def _():
                    send_part(n - 4, half).wait_send()

                r.part_out[lax.rem(n, 4), rows] = part.astype(BF16)
                send_part(n, half).start()

        def give_both(n, part):
            for half in (0, 1):
                give(n, half, part[half * HALF : half * HALF + HALF])

        def send_pair(n, half):
            rows = pl.ds(half * HALF, HALF)
            return remote(
                r.pair_out.at[lax.rem(n, 4), rows],
                r.pair_in.at[lax.rem(n, 8), rows],
                r.mm_s.at[n * 2 + half],
                r.mm_r.at[n * 2 + half],
                other_id,
            )

        def fold(n, half):
            rows = slice(half * HALF, half * HALF + HALF)
            arrived(r.part_in.at[lax.rem(n, 8), rows], r.ps_r.at[n * 2 + half])

            @pl.when(n >= 4)
            def _():
                send_pair(n - 4, half).wait_send()

            both = r.own[lax.rem(n, 4), rows] + r.part_in[lax.rem(n, 8), rows].astype(F32)
            r.pair_out[lax.rem(n, 4), rows] = both.astype(BF16)
            send_pair(n, half).start()

        def total_of(n, half):
            rows = slice(half * HALF, half * HALF + HALF)
            arrived(r.pair_in.at[lax.rem(n, 8), rows], r.mm_r.at[n * 2 + half])
            return r.pair_out[lax.rem(n, 4), rows].astype(F32) + r.pair_in[
                lax.rem(n, 8), rows
            ].astype(F32)

        y_way = (r.y, r.y_stage, r.y_s, r.y_r)
        dx_way = (r.dx, r.dx_stage, r.dx_s, r.dx_r)

        def hand_out(way, k, value):
            way[1][k] = value.astype(F32).T.astype(BF16)
            for side in (0, 1):
                target = 2 * (h - 1) + side
                own = (k == s) & (target == h) & (d == owner)
                local, far = hand_copy(way, k, side)
                pl.when(own)(local.start)
                pl.when(jnp.logical_not(own))(far.start)

        def hand_copy(way, k, side):
            src = way[1].at[k, pl.ds(pl.multiple_of((2 * (h - 1) + side) * local, local), local)]
            dst = way[0].at[slot, :, pl.ds(pl.multiple_of(d * BLOCK, BLOCK), BLOCK)]
            recv = way[3].at[slot, d]
            return (
                pltpu.make_async_copy(src, dst, recv),
                remote(
                    src, dst, way[2].at[k, side], recv, at(k, 2 * (h - 1) + side, owner)
                ),
            )

        def finish_hand(way):
            @pl.when(mid)
            def _():
                for k in range(chunks):
                    for side in (0, 1):
                        own = (k == s) & (2 * (h - 1) + side == h) & (d == owner)
                        pl.when(jnp.logical_not(own))(hand_copy(way, k, side)[1].wait_send)

            for j in range(micro):
                for core in (0, 1):
                    arrived(
                        way[0].at[j, :, core * BLOCK : core * BLOCK + BLOCK],
                        way[3].at[j, core],
                    )

        def leave(n, half):
            c, k = lax.div(n, 4), lax.rem(n, 4)
            rows = slice(half * HALF, half * HALF + HALF)
            state = r.state[n, rows].astype(F32) + total_of(n, half) + r.par[c, 2:3]
            state = state.astype(BF16)

            @pl.when(c < 3)
            def _():
                publish(c + 1, k, half, state)

            @pl.when(c == 3)
            def _():
                r.last[rows] = state
                if half:
                    hand_out(y_way, k, r.last[...])

        def send_grad(index, half):
            rows = r.grad.at[index, half * HALF : half * HALF + HALF]
            return remote(
                rows, rows, r.gx_s.at[index * 2 + half], r.gx_r.at[index * 2 + half], mate_id
            )

        def enter_back(k):
            r.grad[12 + k] = turned(r.cot_in, r.xc_r, k)
            for half in (0, 1):
                send_grad(12 + k, half).start()

        def send_norms(c, side, core):
            target = 2 * (h - 1) + side
            recv = r.nr_r.at[s * 2 + d]
            return (
                (c == s) & (target == h) & (d == core),
                pltpu.make_async_copy(r.nrm.at[c], r.nrm_in.at[s * 2 + d], recv),
                remote(
                    r.nrm.at[c],
                    r.nrm_in.at[s * 2 + d],
                    r.nr_s.at[c * 4 + side * 2 + core],
                    recv,
                    at(c, target, core),
                ),
            )

        def all_norms(c):
            return [send_norms(c, side, core) for side in (0, 1) for core in (0, 1)]

        def send_small(c, step):
            whom = lax.rem(s * 2 + d + step, 8)
            return remote(
                r.sm.at[c],
                r.sm_in.at[c * 8 + s * 2 + d],
                r.sm_s.at[c * 8 + step],
                r.sm_r.at[c * 8 + s * 2 + d],
                at(lax.div(whom, 2), h, lax.rem(whom, 2)),
            )

        def push_small(c):
            for step in range(1, 8):
                send_small(c, step).start()

        def leave_back(m, half):
            c, k = 3 - lax.div(m, 4), 3 - lax.rem(m, 4)
            index = c * 4 + k
            rows = slice(half * HALF, half * HALF + HALF)
            total = total_of(16 + m, half)
            scaled, inverse = norm_parts(r.state[index, rows].astype(F32))
            above = r.grad[index, rows].astype(F32)
            t = total * r.par[c, 0:1]
            inner = (
                t
                - jnp.mean(t, axis=-1, keepdims=True)
                - scaled * jnp.mean(t * scaled, axis=-1, keepdims=True)
            )
            below = (above + inverse * inner).astype(BF16)

            @pl.when(c > 0)
            def _():
                r.grad[index - 4, rows] = below
                send_grad(index - 4, half).start()

            @pl.when(c == 0)
            def _():
                r.last[rows] = below
                if half:
                    hand_out(dx_way, k, r.last[...])

            for i, value in enumerate((total * scaled, total, above)):
                r.nrm[c, i : i + 1] = r.nrm[c, i : i + 1] + jnp.sum(value, axis=0, keepdims=True)
            if half:

                @pl.when(k == 0)
                def _():
                    launch(all_norms(c))

        def send_keys(l, step):
            ring = lax.rem(step, 2) * 4
            return remote(
                r.sums.at[pl.ds(ring, 4), 0:BLOCK],
                r.sums_in.at[pl.ds(step * 4, 4)],
                r.dk_s.at[l * 4 + step],
                r.dk_r.at[l * 4 + step],
                partner,
            )

        def attend_back(l, k):
            step = 3 - k
            ring = lax.rem(step, 2) * 4
            block = 2 * k + d
            start = block * BLOCK
            grad_merged = dot(r.grad[8 * l + k], r.wo[l], NT).astype(BF16)

            @pl.when(step >= 2)
            def _():
                send_keys(l, step - 2).wait_send()

            gate_total = jnp.zeros((256, 128), F32)
            for hh in range(3):
                where = (l * 4 + k) * 3 + hh
                near = pl.ds(pl.multiple_of(start, BLOCK), 192)
                keys = jnp.concatenate([r.kv[l * 4 + hh, near], r.chosen[where]], axis=0)
                mixed = grad_merged[:, hh * 128 : hh * 128 + 128]
                soft = r.soft[where]
                grad_soft = dot(mixed, keys, NT)
                grad_logits = (
                    soft * (grad_soft - jnp.sum(grad_soft * soft, axis=1, keepdims=True))
                ).astype(BF16)
                grad_query = dot(grad_logits, keys) * 0.125
                r.dqkv[k, :, hh * 256 : hh * 256 + 128] = jnp.where(
                    lane < 64, grad_query, 0.0
                ).astype(BF16)
                left = jnp.concatenate([grad_logits, soft.astype(BF16)], axis=0)
                right = jnp.concatenate(
                    [
                        jnp.concatenate([r.q[where], ones_tiles[hh]], axis=1),
                        jnp.concatenate([mixed, jnp.zeros_like(mixed)], axis=1),
                    ],
                    axis=0,
                )
                grad_set = dot(left, right, TN)
                far = grad_set[192:256]
                high = far.astype(BF16)
                r.far[hh, pl.ds(k * 128, 64)] = high
                r.far[hh, pl.ds(k * 128 + 64, 64)] = (far - high.astype(F32)).astype(BF16)
                hots = []
                for kk in range(4):
                    pick_row = r.pk[pl.ds(hh * 8 + 2 * kk + d, 1), :][:, 0:128]
                    hit = rows_of((256, 128)) + (start - BLOCK) == pick_row
                    hots.append((hit & (kk >= k)).astype(F32).astype(BF16))
                total = dot(jnp.concatenate(hots, axis=1), r.far[hh])
                r.sums[ring + hh, 0:WINDOW] = total[0:WINDOW, 0:128]
                r.sums[ring + hh, WINDOW:256] = total[WINDOW:256, 0:128] + grad_set[0:192, 0:128]
                gate_total = gate_total + total[:, 128:256]
            r.sums[ring + 3] = gate_total

            @pl.when(block > 0)
            def _():
                send_keys(l, step).start()

        def finish_back(l, k):
            step = 3 - k
            ring = lax.rem(step, 2) * 4
            came = step - d

            @pl.when(came >= 0)
            def _():
                arrived(r.sums_in.at[pl.ds(came * 4, 4)], r.dk_r.at[l * 4 + came])
                for j in range(4):
                    r.sums[ring + j, BLOCK:256] = (
                        r.sums[ring + j, BLOCK:256] + r.sums_in[came * 4 + j]
                    )

            scores = pieces(r.sums[ring + 3, BLOCK:256] * r.sig[l * 4 + k], lane)
            for hh in range(3):
                head = slice(hh * 256, hh * 256 + 128)
                r.dqkv[k, :, head] = jnp.where(
                    head_lanes(lane, hh), scores, r.dqkv[k, :, head]
                )
                r.dqkv[k, :, hh * 256 + 128 : hh * 256 + 256] = r.sums[
                    ring + hh, BLOCK:256
                ].astype(BF16)
            return dot(r.dqkv[k], r.w1[l])

        def feed_back(l, k, half):
            rows = slice(half * HALF, half * HALF + HALF)
            grad_hidden = dot(r.grad[8 * l + 4 + k, rows], r.pj[l], NT)
            grad_pre = (grad_hidden * r.slope[l * 4 + k, rows].astype(F32)).astype(BF16)
            r.dpre[k, rows] = grad_pre
            return dot(grad_pre, r.fc[l], NT)

        def four(ref, first):
            value = ref[pl.ds(first, 4)]
            return value.reshape(4 * BLOCK, value.shape[2])

        ones_rows = jnp.ones((8, 4 * BLOCK), BF16)

        def split(kind, width):
            for section in range(4):
                rows = pl.ds(pl.multiple_of((2 * section + 1 - d) * part_rows, 8), part_rows)
                halves[kind][0][section] = wides[kind][rows, 0:width].astype(BF16)
            send_half(kind).start()

        def send_half(kind):
            return remote(
                halves[kind][0],
                halves[kind][1],
                r.xh_s.at[kind],
                r.xh_r.at[kind],
                partner,
            )

        def send_share(kind, step):
            return remote(
                shares[kind][0].at[step - 1],
                shares[kind][1].at[step - 1],
                r.yh_s.at[kind, step - 1],
                r.yh_r.at[kind, step - 1],
                at(lax.rem(s + step, 4), h, d),
            )

        def share(kind, width):
            arrived(halves[kind][1], r.xh_r.at[kind])
            send_half(kind).wait_send()
            for step in (1, 2, 3, 0):
                section = lax.rem(s + step, 4)
                rows = pl.ds(pl.multiple_of((2 * section + d) * part_rows, 8), part_rows)
                both = wides[kind][rows, 0:width] + halves[kind][1][section].astype(F32)
                if step:
                    shares[kind][0][step - 1] = both.astype(BF16)
                    send_share(kind, step).start()
                else:
                    wides[kind][rows, 0:width] = both

        def collect(kind, width):
            rows = pl.ds(pl.multiple_of((2 * s + d) * part_rows, 8), part_rows)
            total = wides[kind][rows, 0:width]
            for step in (1, 2, 3):
                arrived(shares[kind][1].at[step - 1], r.yh_r.at[kind, step - 1])
                total = total + shares[kind][1][step - 1].astype(F32)
                send_share(kind, step).wait_send()
            return total

        def weights_feed(l, part):
            left = four(r.normed, 8 * l + 4) if part < 2 else four(r.grad, 8 * l + 4)
            right = four(r.dpre, 0) if part < 2 else four(r.hidden, 4 * l)
            rows = slice(part % 2 * 384, part % 2 * 384 + 384)
            columns = slice(part // 2 * 768, part // 2 * 768 + 768)
            r.wide_f[rows, columns] = dot(left[:, rows], right, TN)
            if part == 0:
                r.sm[2 * l + 1, 0:1] = dot(ones_rows, right)[0:1]
                push_small(2 * l + 1)
            if part == 3:
                split(0, 1536)

        def weights_attend(l, part):
            wide_lane = lanes((4 * BLOCK, 128))
            if part == 0:
                grads = four(r.dqkv, 0)
                t = [grads[:, i * 256 : i * 256 + 128].astype(F32) for i in range(3)]
                first = jnp.where(wide_lane < 64, t[0], pltpu.roll(t[1], 64, 1))
                second = jnp.where(wide_lane < 64, t[2], t[0] + t[1] + t[2])
                r.packed[:, 0:128] = first.astype(BF16)
                r.packed[:, 128:256] = second.astype(BF16)
                for i in range(3):
                    r.packed[:, 256 + 128 * i : 384 + 128 * i] = grads[
                        :, i * 256 + 128 : i * 256 + 256
                    ]
                r.sm[2 * l, 0:1] = dot(ones_rows, grads)[0:1]
            if part < 2:
                rows = slice(part * 384, part * 384 + 384)
                r.wide_a[rows, 0:640] = dot(four(r.normed, 8 * l)[:, rows], r.packed[...], TN)
            if part == 2:
                merged = four(r.merged, 4 * l)
                u = [merged[:, i * 128 : i * 128 + 128].astype(F32) for i in range(3)]
                packed = jnp.concatenate(
                    [
                        jnp.where(wide_lane < 64, pltpu.roll(u[0], 64, 1), u[1]),
                        jnp.where(wide_lane < 64, pltpu.roll(u[2], 64, 1), 0.0),
                    ],
                    axis=1,
                ).astype(BF16)
                r.wide_a[:, 640:896] = dot(four(r.grad, 8 * l), packed, TN)
            if part == 3:
                send_keys(l, 2).wait_send()

                @pl.when(d == 1)
                def _():
                    send_keys(l, 3).wait_send()

                scores = dot(r.packed[:, 128:256], four(r.normed, 8 * l), TN)
                for hh in range(3):
                    row = 64 + 3 * hh
                    r.sm[2 * l, 1 + hh : 2 + hh] = (
                        scores[row : row + 1] + scores[row + 1 : row + 2] + scores[row + 2 : row + 3]
                    )
                push_small(2 * l)
                split(1, 896)

        def collect_feed(l):
            total = collect(0, 1536)
            r.o_fc[l] = total[:, 0:768]
            r.o_pj[l] = total[:, 768:1536]

        def collect_attend(l):
            total = collect(1, 896)
            r.o_qkv[3 * l] = total[:, 0:192]
            for i in (0, 1):
                r.o_qkv[3 * l + 1 + i] = jnp.concatenate(
                    [total[:, 256 + 128 * j + 64 * i : 320 + 128 * j + 64 * i] for j in range(3)],
                    axis=1,
                )
            r.o_out[l] = total[:, 640:896].T[0:192]

        def slot_of(n, carry):
            ahead = n < 16
            c = jnp.where(ahead, lax.div(n, 4), 7 - lax.div(n, 4))
            k = jnp.where(ahead, lax.rem(n, 4), 3 - lax.rem(n, 4))
            l = lax.div(c, 2)
            works = n < 32
            attends = lax.rem(c, 2) == 0

            @pl.when((n < DIRECT) | (mid & (n < 4)))
            def _():
                enter(n)

            @pl.when((n == 8) & (d == owner))
            def _():
                launch(cot_parts[3])

            @pl.when((n == 9) & (d == owner))
            def _():
                launch(cot_parts[2])

            @pl.when((n == 10) & (d == owner))
            def _():
                launch(cot_parts[1])

            @pl.when((n == 11) & (d == owner))
            def _():
                launch(cot_parts[0])

            @pl.when(mid & (n >= 4) & (n < 20))
            def _():
                leave(n - 4, 0)

            @pl.when(mid & (n >= 20))
            def _():
                leave_back(n - 20, 0)

            @pl.when(mid & (n >= 3) & (n < 35))
            def _():
                fold(n - 3, 1)

            @pl.when(mid & (n >= 4) & (n < 20))
            def _():
                leave(n - 4, 1)

            @pl.when(mid & (n >= 12) & (n < 16))
            def _():
                enter_back(15 - n)

            @pl.when(mid & (n >= 20))
            def _():
                leave_back(n - 20, 1)

            def come(half):
                rows = slice(half * HALF, half * HALF + HALF)

                @pl.when(jnp.logical_not(mid) & ahead & (n >= DIRECT))
                def _():
                    arrived(r.normed.at[n, rows], r.nx_r.at[n * 2 + half])

                @pl.when(jnp.logical_not(mid) & jnp.logical_not(ahead) & works)
                def _():
                    index = c * 4 + k
                    arrived(r.grad.at[index, rows], r.gx_r.at[index * 2 + half])

            @pl.when(attends)
            def _():
                come(0)
                come(1)

            @pl.when((n == 0) | (n == 8))
            def _():
                for copy in attend_loads[0:12]:
                    pltpu.make_async_copy(copy.src_ref, copy.dst_ref, r.load.at[l]).wait()

            @pl.when(n == 4)
            def _():
                for copy in feed_loads:
                    copy.wait()

            @pl.when(ahead & attends)
            def _():
                project(l, k)

            @pl.when(n == 0)
            def _():
                for copy in pick_copies:
                    copy.wait()
                chosen = r.pk_in[owner, slot]
                r.pk[...] = jnp.concatenate(
                    [chosen, chosen, jnp.zeros((32, 192), jnp.int32), chosen], axis=1
                )
                square = jnp.concatenate([chosen.astype(F32), jnp.zeros((32, 64), F32)], axis=1)
                square = jnp.concatenate([square, jnp.zeros((96, 128), F32)], axis=0)
                r.pt[...] = square.T[0:64]

            @pl.when(ahead & attends)
            def _():
                came = k - 1 + d
                pl.when(came >= 0)(lambda: wait_kv(l, came))
                give_both(n, attend(l, k))

            @pl.when(ahead & jnp.logical_not(attends))
            def _():
                for half in (0, 1):
                    come(half)
                    give(n, half, feed(l, k, half))

            @pl.when(jnp.logical_not(ahead) & works & attends)
            def _():
                attend_back(l, k)
                give_both(n, finish_back(l, k))

            @pl.when(jnp.logical_not(ahead) & works & jnp.logical_not(attends))
            def _():
                for half in (0, 1):
                    come(half)
                    give(n, half, feed_back(l, k, half))

            @pl.when(mid & (n >= 2) & (n < 34))
            def _():
                fold(n - 2, 0)

            for part in range(4):

                @pl.when((n == 20 + part // 2) | (n == 28 + part // 2))
                def _():
                    weights_feed(lax.div(29 - n, 8), part)

                @pl.when((n == 24 + part // 2) | (n == 31 + part // 2))
                def _():
                    weights_attend(lax.div(32 - n, 7), part)

            @pl.when((n == 26) | (n == 33))
            def _():
                collect_feed(lax.div(33 - n, 7))

            @pl.when((n == 30) | (n == 35))
            def _():
                collect_attend(lax.div(35 - n, 5))

            @pl.when((n == 22) | (n == 30))
            def _():
                share(0, 1536)

            @pl.when((n == 26) | (n == 33))
            def _():
                share(1, 896)

            return carry

        lax.fori_loop(0, 36, slot_of, 0)

        for c in range(4):
            for step in range(1, 8):
                whose = c * 8 + lax.rem(s * 2 + d + step, 8)
                arrived(r.sm_in.at[whose], r.sm_r.at[whose])
            r.sm_in[c * 8 + s * 2 + d] = r.sm[c]
            total = r.sm_in[c * 8]
            for j in range(1, 8):
                total = total + r.sm_in[c * 8 + j]
            l = c // 2
            if c % 2:
                r.o_fcb[l : l + 1, :] = total[0:1]
            else:
                for i in (0, 1):
                    r.o_qv[l, i : i + 1, :] = jnp.concatenate(
                        [total[0:1, j * 256 + 192 * i : j * 256 + 192 * i + 64] for j in range(3)],
                        axis=1,
                    )
                for j in range(3):
                    r.o_score[j, l : l + 1, :] = total[1 + j : 2 + j]
        for j in range(8):
            arrived(r.nrm_in.at[j], r.nr_r.at[j])
        total = r.nrm_in[0]
        for j in range(1, 8):
            total = total + r.nrm_in[j]
        for j in range(4):

            @pl.when(h == j)
            def _():
                for i, ref in enumerate((r.o_gain, r.o_bias, r.o_ob)):
                    ref[...] = total[i : i + 1, j * 192 : j * 192 + 192]

        finish_hand(y_way)
        finish_hand(dx_way)
        for c in range(4):
            for step in range(1, 8):
                send_small(c, step).wait_send()

        @pl.when(mid)
        def _():
            for c in range(4):
                sent(all_norms(c))

        @pl.when(d == owner)
        def _():
            for copies in stream_parts + cot_parts:
                sent(copies)

        sent(norm_rows)

        @pl.when((s == 0) & jnp.logical_not(mid))
        def _():
            sent(end_rows)

        def drain_kv(i, carry):
            send_kv(lax.div(i, 4), lax.rem(i, 4)).wait_send()
            return carry

        lax.fori_loop(0, 8, drain_kv, 0)

        @pl.when(d == 0)
        def _():
            wait_kv(0, 3)
            wait_kv(1, 3)

        @pl.when(mid)
        def _():
            def drain(i, carry):
                for half in (0, 1):
                    pl.when(i >= DIRECT)(send_normed(i, half).wait_send)
                    send_grad(i, half).wait_send()
                return carry

            lax.fori_loop(0, 16, drain, 0)
            for n in range(28, 32):
                for half in (0, 1):
                    send_pair(n, half).wait_send()

        @pl.when(jnp.logical_not(mid))
        def _():
            for n in range(28, 32):
                for half in (0, 1):
                    send_part(n, half).wait_send()

    return kernel


def hand_over(*refs):
    count = len(refs) // 2
    for i in range(count):
        refs[count + i][...] = refs[i][...]


def shards(
    stream,
    cotangent,
    lengths,
    picks,
    norm_gain,
    norm_bias,
    out_bias,
    weight_qkv,
    bias_qv,
    weight_score,
    weight_out,
    weight_fc,
    bias_fc,
    weight_proj,
):
    micro, tokens, local = stream.shape
    layers, width = weight_qkv.shape[0], weight_qkv.shape[1]
    inputs = dict(
        stream=stream.transpose(0, 2, 1),
        cot=cotangent.transpose(0, 2, 1),
        lengths=lengths,
        picks=picks.reshape(micro, 24, 64),
        gain=norm_gain,
        shift=norm_bias,
        ob=out_bias,
        wqkv=weight_qkv.transpose(0, 2, 3, 1),
        bqv=bias_qv,
        wscore=weight_score.transpose(2, 0, 1),
        wout=weight_out,
        wfc=weight_fc,
        bfc=bias_fc,
        wpj=weight_proj,
    )
    spaces = dict(
        stream=pl.ANY, cot=pl.ANY, lengths=pltpu.SMEM, wqkv=pl.ANY, wout=pl.ANY, wfc=pl.ANY, wpj=pl.ANY
    )
    part_rows = width // 8
    outputs = dict(
        y=((micro, local, 2 * BLOCK), BF16),
        dx=((micro, local, 2 * BLOCK), BF16),
        o_gain=((1, 192), F32),
        o_bias=((1, 192), F32),
        o_ob=((1, 192), F32),
        o_qkv=((6, part_rows, 192), F32),
        o_qv=((2, 2, 192), F32),
        o_score=((3, 2, 768), F32),
        o_out=((2, 192, part_rows), F32),
        o_fc=((2, part_rows, 768), F32),
        o_fcb=((2, 768), F32),
        o_pj=((2, part_rows, 768), F32),
    )
    dma = pltpu.SemaphoreType.DMA
    scratch = dict(
        stream_in=((4, 768, BLOCK), BF16),
        cot_in=((4, 768, BLOCK), BF16),
        prm=((16, 768), BF16),
        w1=((2, 768, 768), BF16),
        wo=((2, 384, 768), BF16),
        fc=((2, 768, 768), BF16),
        pj=((2, 768, 768), BF16),
        bq=((2, 1, 768), F32),
        fcb=((2, 1, 768), F32),
        prm_in=((4, 4, 16, 768), BF16),
        par=((4, 8, 768), F32),
        last=((BLOCK, 768), BF16),
        pk_out=((micro, 32, 64), jnp.int32),
        pk_in=((2, micro, 32, 64), jnp.int32),
        pk=((32, 384), jnp.int32),
        pt=((64, 128), F32),
        state=((16, BLOCK, 768), BF16),
        normed=((16, BLOCK, 768), BF16),
        q=((24, BLOCK, 128), BF16),
        sig=((8, BLOCK, 128), F32),
        kv=((8, WINDOW + tokens, 128), BF16),
        chosen=((24, 64, 128), BF16),
        keyset=((3, 256, 256), BF16),
        soft=((24, BLOCK, 256), F32),
        merged=((8, BLOCK, 384), BF16),
        hidden=((8, BLOCK, 768), BF16),
        slope=((8, BLOCK, 768), BF16),
        part_out=((4, BLOCK, 768), BF16),
        part_in=((8, BLOCK, 768), BF16),
        own=((4, BLOCK, 768), F32),
        pair_out=((4, BLOCK, 768), BF16),
        pair_in=((8, BLOCK, 768), BF16),
        y_stage=((4, 768, BLOCK), BF16),
        dx_stage=((4, 768, BLOCK), BF16),
        grad=((16, BLOCK, 768), BF16),
        dpre=((4, BLOCK, 768), BF16),
        dqkv=((4, BLOCK, 768), BF16),
        far=((3, 512, 256), BF16),
        sums=((8, 256, 128), F32),
        sums_in=((16, BLOCK, 128), F32),
        wide_f=((768, 1536), F32),
        wide_a=((768, 896), F32),
        packed=((512, 640), BF16),
        xo_f=((4, part_rows, 1536), BF16),
        xi_f=((4, part_rows, 1536), BF16),
        yo_f=((3, part_rows, 1536), BF16),
        yi_f=((3, part_rows, 1536), BF16),
        xo_a=((4, part_rows, 896), BF16),
        xi_a=((4, part_rows, 896), BF16),
        yo_a=((3, part_rows, 896), BF16),
        yi_a=((3, part_rows, 896), BF16),
        nrm=((4, 8, 768), F32),
        nrm_in=((8, 8, 768), F32),
        sm=((4, 8, 768), F32),
        sm_in=((32, 8, 768), F32),
    )
    sems = dict(
        xs_s=(8, 4),
        xs_r=(4, 4),
        xc_s=(8, 4),
        xc_r=(4, 4),
        load=(3,),
        prm_s=(4, 2),
        prm_e=(4,),
        prm_r=(4, 4),
        pick_s=(2,),
        pick_r=(1,),
        nx_s=(32,),
        nx_r=(32,),
        kv_s=(8,),
        kv_r=(8,),
        ps_s=(64,),
        ps_r=(64,),
        mm_s=(64,),
        mm_r=(64,),
        y_s=(4, 2),
        y_r=(2, 2),
        dx_s=(4, 2),
        dx_r=(2, 2),
        gx_s=(32,),
        gx_r=(32,),
        dk_s=(8,),
        dk_r=(8,),
        xh_s=(2,),
        xh_r=(2,),
        yh_s=(2, 3),
        yh_r=(2, 3),
        sm_s=(32,),
        sm_r=(32,),
        nr_s=(16,),
        nr_r=(8,),
    )
    names = list(inputs) + list(outputs) + list(scratch) + list(sems)
    results = pl.pallas_call(
        make_kernel(names, micro, width // 8, local),
        out_shape=[jax.ShapeDtypeStruct(*spec) for spec in outputs.values()],
        in_specs=[
            pl.BlockSpec(memory_space=spaces.get(name, pltpu.VMEM))
            for name in inputs
        ],
        out_specs=[pl.BlockSpec(memory_space=pltpu.VMEM) for name in outputs],
        scratch_shapes=[pltpu.VMEM(*spec) for spec in scratch.values()]
        + [dma(shape) for shape in sems.values()],
        compiler_params=pltpu.CompilerParams(
            collective_id=0, has_side_effects=True, vmem_limit_bytes=62 * 2**20
        ),
        name="blocks",
    )(*inputs.values())
    results = pl.pallas_call(
        hand_over,
        out_shape=[jax.ShapeDtypeStruct(*spec) for spec in outputs.values()],
        in_specs=[pl.BlockSpec(memory_space=pltpu.VMEM)] * len(outputs),
        out_specs=[pl.BlockSpec(memory_space=pltpu.VMEM)] * len(outputs),
        name="results",
    )(*results)
    o = types.SimpleNamespace(**dict(zip(outputs, results)))
    dp_count = lax.axis_size("dp")
    if dp_count > 2:
        d = lax.rem(lax.axis_index("dp"), 2)

        def scattered(value):
            placed = jnp.zeros((value.shape[0], 2 * part_rows, value.shape[2]), F32)
            placed = lax.dynamic_update_slice(placed, value, (0, d * part_rows, 0))
            return lax.psum_scatter(placed, "dp", scatter_dimension=1, tiled=True)

        o.o_out = scattered(o.o_out.transpose(0, 2, 1)).transpose(0, 2, 1)
        o.o_qkv, o.o_fc, o.o_pj = map(scattered, (o.o_qkv, o.o_fc, o.o_pj))
        sums = (o.o_gain, o.o_bias, o.o_ob, o.o_qv, o.o_score, o.o_fcb)
        o.o_gain, o.o_bias, o.o_ob, o.o_qv, o.o_score, o.o_fcb = jax.tree.map(
            lambda value: 0.5 * value, lax.psum(sums, "dp")
        )
    rows = o.o_fc.shape[1]
    return (
        o.y.transpose(0, 2, 1),
        o.dx.transpose(0, 2, 1),
        o.o_gain,
        o.o_bias,
        o.o_ob,
        o.o_qkv.reshape(layers, 3, rows, 192).transpose(0, 2, 1, 3),
        o.o_qv,
        o.o_score.transpose(1, 2, 0),
        o.o_out,
        o.o_fc,
        o.o_fcb,
        o.o_pj.transpose(0, 2, 1),
    )


def solution(mesh):
    return jax.shard_map(
        shards,
        mesh=mesh,
        in_specs=(
            P("dp", None, "head"),
            P("dp", None, "head"),
            P("dp"),
            P("dp", "head", None, None),
            P("section", None),
            P("section", None),
            P("section", "head"),
            P(None, None, None, "head"),
            P(None, None, "head"),
            P(None, None, "head"),
            P(None, "head", None),
            P(None, None, "head"),
            P(None, "head"),
            P(None, "head", None),
        ),
        out_specs=(
            P("dp", "section", "head"),
            P("dp", "section", "head"),
            P("section", "head"),
            P("section", "head"),
            P("section", "head"),
            P(None, ("section", "dp"), None, "head"),
            P(None, None, "head"),
            P(None, None, "head"),
            P(None, "head", ("section", "dp")),
            P(None, ("section", "dp"), "head"),
            P(None, "head"),
            P(None, "head", ("section", "dp")),
        ),
        check_vma=False,
    )
```

```python
import types

import jax
import jax.numpy as jnp
from jax import lax
from jax.experimental import pallas as pl
from jax.experimental.pallas import tpu as pltpu
from jax.sharding import PartitionSpec as P

MESH = pl.DeviceIdType.MESH
BLOCK = 128
HALF = 64
DIRECT = 1
FEED_PARTS = ((20, 20, 21, 21), (28, 28, 28, 28))
ATTEND_PARTS = ((24, 24, 25, 25), (31, 31, 31, 31))
FEED_SHARE, FEED_COLLECT = (22, 29), (26, 34)
ATTEND_SHARE, ATTEND_COLLECT = (26, 32), (30, 35)
WINDOW = 64
NT = (((1,), (1,)), ((), ()))
TN = (((0,), (0,)), ((), ()))
F32 = jnp.float32
BF16 = jnp.bfloat16
ROOT = 0.7978845608028654
CUBE = 0.044715


def dot(left, right, dims=(((1,), (0,)), ((), ()))):
    return lax.dot_general(left, right, dims, preferred_element_type=F32)


def lanes(shape):
    return lax.broadcasted_iota(jnp.int32, shape, len(shape) - 1)


def rows_of(shape):
    return lax.broadcasted_iota(jnp.int32, shape, len(shape) - 2)


def head_lanes(lane, hh):
    return (lane >= 64 + 3 * hh) & (lane < 67 + 3 * hh)


def pieces(value, lane):
    high = value.astype(BF16)
    rest = value - high.astype(F32)
    middle = rest.astype(BF16)
    low = (rest - middle.astype(F32)).astype(BF16)
    zero = jnp.zeros_like(high)
    used = (lane >= 64) & (lane < 73)
    which = lax.rem(lane - 64 + 3 * 64, 3)
    return jnp.where(
        used & (which == 0),
        high,
        jnp.where(used & (which == 1), middle, jnp.where(used & (which == 2), low, zero)),
    )


def make_kernel(names, micro, part_rows, local):
    def kernel(*refs):
        r = types.SimpleNamespace(**dict(zip(names, refs)))
        wides = (r.wide_f, r.wide_a)
        halves = ((r.xo_f, r.xi_f), (r.xo_a, r.xi_a))
        shares = ((r.yo_f, r.yi_f), (r.yo_a, r.yi_a))
        s, h, dp = lax.axis_index("section"), lax.axis_index("head"), lax.axis_index("dp")
        d = lax.rem(dp, 2)
        pair = dp - d
        mid = (h == 1) | (h == 2)
        mate = h + 1 - 2 * lax.rem(h, 2)
        other = 3 - h
        owner = lax.div(s, micro)
        slot = lax.rem(s, micro)

        def at(section, head, core):
            return (section, head, pair + core)

        def remote(src, dst, send, recv, device):
            return pltpu.make_async_remote_copy(
                src_ref=src,
                dst_ref=dst,
                send_sem=send,
                recv_sem=recv,
                device_id=device,
                device_id_type=MESH,
            )

        partner = at(s, h, 1 - d)
        mate_id = at(s, mate, d)
        other_id = at(s, other, d)

        def arrived(dst, recv):
            remote(dst, dst, recv, recv, partner).wait_recv()

        barrier = pltpu.get_barrier_semaphore()
        flat = (s * 4 + h) * 2 + d

        def greet(step, carry):
            whom = lax.rem(flat + step, 32)
            pl.semaphore_signal(
                barrier,
                inc=1,
                device_id=at(lax.div(whom, 8), lax.rem(lax.div(whom, 2), 4), lax.rem(whom, 2)),
                device_id_type=MESH,
            )
            return carry

        lax.fori_loop(1, 32, greet, 0)

        attend_loads, feed_loads = [], []
        for l in range(2):
            for hh in range(3):
                rows = slice(hh * 64, hh * 64 + 64)
                for part, place in ((0, 0), (1, 128), (2, 192)):
                    attend_loads.append(
                        pltpu.make_async_copy(
                            r.wqkv.at[l, part, rows],
                            r.w1.at[l, hh * 256 + place : hh * 256 + place + 64],
                            r.load.at[l],
                        )
                    )
                attend_loads.append(
                    pltpu.make_async_copy(
                        r.wout.at[l, rows],
                        r.wo.at[l, hh * 128 + 64 : hh * 128 + 128],
                        r.load.at[l],
                    )
                )
            feed_loads.append(pltpu.make_async_copy(r.wfc.at[l], r.fc.at[l], r.load.at[2]))
            feed_loads.append(pltpu.make_async_copy(r.wpj.at[l], r.pj.at[l], r.load.at[2]))

        for copy in attend_loads + feed_loads:
            copy.start()

        r.nrm[...] = jnp.zeros_like(r.nrm)
        r.sm[...] = jnp.zeros_like(r.sm)
        for j in range(micro):
            r.pk_out[j, 0:24] = r.picks[j]
            r.pk_out[j, 24:32] = jnp.zeros((8, 64), jnp.int32) + r.lengths[j]
        wide_bias = jnp.concatenate([r.ob[...].astype(F32)] * 4, axis=1)
        wide_bias = jnp.where(
            (lanes((1, 768)) >= h * local) & (lanes((1, 768)) < h * local + local), wide_bias, 0.0
        )
        row = rows_of((16, 768))
        r.prm[...] = jnp.where(
            row == 0,
            r.gain[...].astype(F32),
            jnp.where(
                row == 1, r.shift[...].astype(F32), jnp.where(row == 2, wide_bias, 0.0)
            ),
        ).astype(BF16)

        r.keyset[...] = jnp.zeros_like(r.keyset)
        r.far[...] = jnp.zeros_like(r.far)
        r.kv[:, 0:WINDOW] = jnp.zeros((8, WINDOW, 128), BF16)
        for l in range(2):
            for hh in range(3):
                score = jnp.where(
                    (rows_of((64, 768)) >= 3 * hh) & (rows_of((64, 768)) < 3 * hh + 3),
                    r.wscore[hh, l : l + 1, :].astype(F32),
                    0.0,
                )
                r.w1[l, hh * 256 + 64 : hh * 256 + 128] = score.astype(BF16)
                r.wo[l, hh * 128 : hh * 128 + 64] = jnp.zeros((64, 768), BF16)
            gap = jnp.zeros((1, 128), F32)
            r.fcb[l] = r.bfc[l : l + 1, :].astype(F32)
            bias = r.bqv[l].astype(F32)
            r.bq[l] = jnp.concatenate(
                [
                    piece
                    for hh in range(3)
                    for piece in (
                        bias[0:1, hh * 64 : hh * 64 + 64],
                        gap,
                        bias[1:2, hh * 64 : hh * 64 + 64],
                    )
                ],
                axis=1,
            )

        pl.semaphore_wait(barrier, 31)

        def spread(source, landing, sends, recvs, k, heads):
            copies = []
            for hm in heads:
                for core in (0, 1):
                    src = source.at[slot, :, (2 * k + core) * BLOCK : (2 * k + core + 1) * BLOCK]
                    dst = landing.at[k, pl.ds(pl.multiple_of(h * local, local), local)]
                    recv = recvs.at[h, k]
                    copies.append(
                        (
                            (h == hm) & (d == core),
                            pltpu.make_async_copy(src, dst, recv),
                            remote(
                                src, dst, sends.at[hm * 2 + core, k], recv, at(s, hm, core)
                            ),
                        )
                    )
            return copies

        def launch(copies):
            for own, local, far in copies:
                pl.when(own)(local.start)
                pl.when(jnp.logical_not(own))(far.start)

        def sent(copies):
            for own, local, far in copies:
                pl.when(jnp.logical_not(own))(far.wait_send)

        chunks = 4
        stream_parts = [
            spread(r.stream, r.stream_in, r.xs_s, r.xs_r, k, (1, 2, 0, 3)[: 4 if k < DIRECT else 2])
            for k in range(chunks)
        ]
        cot_parts = [
            spread(r.cot, r.cot_in, r.xc_s, r.xc_r, k, (1, 2)) for k in range(chunks)
        ]
        norm_rows = []
        for step in range(4):
            section = lax.rem(s + step, 4)
            for hm in (1, 2):
                norm_rows.append(
                    (
                        (h == hm) if step == 0 else (h == 4),
                        pltpu.make_async_copy(
                            r.prm, r.prm_in.at[s, h], r.prm_r.at[s, h]
                        ),
                        remote(
                            r.prm,
                            r.prm_in.at[s, h],
                            r.prm_s.at[step, hm - 1],
                            r.prm_r.at[s, h],
                            at(section, hm, d),
                        ),
                    )
                )
        end_rows = [
            (
                s == step,
                pltpu.make_async_copy(r.prm, r.prm_in.at[0, h], r.prm_r.at[0, h]),
                remote(
                    r.prm, r.prm_in.at[0, h], r.prm_e.at[step], r.prm_r.at[0, h], at(step, h, d)
                ),
            )
            for step in range(4)
        ]
        pick_copies = (
            pltpu.make_async_copy(r.pk_out, r.pk_in.at[d], r.pick_s.at[0]),
            remote(r.pk_out, r.pk_in.at[d], r.pick_s.at[1], r.pick_r.at[0], partner),
        )

        launch(norm_rows)

        @pl.when((s == 0) & jnp.logical_not(mid))
        def _():
            launch(end_rows)

        @pl.when(d == owner)
        def _():
            for copies in stream_parts:
                launch(copies)

        for copy in pick_copies:
            copy.start()

        lane = lanes((BLOCK, 128))
        ones_tiles = [jnp.where(head_lanes(lane, hh), 1.0, 0.0).astype(BF16) for hh in range(3)]

        def norm_parts(x):
            center = x - jnp.mean(x, axis=-1, keepdims=True)
            inverse = lax.rsqrt(jnp.mean(center * center, axis=-1, keepdims=True) + 1e-05)
            return center * inverse, inverse

        def prepare():
            @pl.when(mid)
            def _():
                for c in range(4):
                    for j in range(4):
                        arrived(r.prm_in.at[c, j], r.prm_r.at[c, j])
                for c in range(4):
                    mine = r.prm_in[c, h].astype(F32)
                    bias = mine[2:3, :] * 0.0
                    for j in range(4):
                        bias = bias + r.prm_in[c, j].astype(F32)[2:3, :]
                    r.par[c, 0:1] = mine[0:1]
                    r.par[c, 1:2] = mine[1:2]
                    r.par[c, 2:3] = bias

            @pl.when(jnp.logical_not(mid))
            def _():
                arrived(r.prm_in.at[0, h], r.prm_r.at[0, h])
                mine = r.prm_in[0, h].astype(F32)
                r.par[0, 0:1] = mine[0:1]
                r.par[0, 1:2] = mine[1:2]

        def publish(c, k, half, state):
            rows = slice(half * HALF, half * HALF + HALF)
            r.state[c * 4 + k, rows] = state
            scaled, _ = norm_parts(state.astype(F32))
            normed = scaled * r.par[c, 0:1] + r.par[c, 1:2]
            r.normed[c * 4 + k, rows] = normed.astype(BF16)
            send_normed(c * 4 + k, half).start()

        def send_normed(n, half):
            rows = r.normed.at[n, half * HALF : half * HALF + HALF]
            return remote(rows, rows, r.nx_s.at[n * 2 + half], r.nx_r.at[n * 2 + half], mate_id)

        def turned(landing, recvs, k):
            for j in range(4):
                arrived(landing.at[k, j * local : j * local + local], recvs.at[j, k])
            return landing[k].astype(F32).T.astype(BF16)

        def enter(k):
            @pl.when(k == 0)
            def _():
                prepare()

            state = turned(r.stream_in, r.xs_r, k)
            r.state[k] = state
            scaled, _ = norm_parts(state.astype(F32))
            r.normed[k] = (scaled * r.par[0, 0:1] + r.par[0, 1:2]).astype(BF16)

            @pl.when(k >= DIRECT)
            def _():
                for half in (0, 1):
                    send_normed(k, half).start()

        def project(l, k):
            x = r.normed[8 * l + k]
            block = 2 * k + d
            place = pl.ds(pl.multiple_of(WINDOW + block * BLOCK, WINDOW), BLOCK)
            score = jnp.zeros((BLOCK, 128), F32)
            for hh in range(3):
                out = dot(x, r.w1[l, hh * 256 : hh * 256 + 256, :], NT)
                out = out + r.bq[l, :, hh * 256 : hh * 256 + 256]
                q, kv = out[:, :128], out[:, 128:]
                r.q[(l * 4 + k) * 3 + hh] = jnp.where(lane < 64, q, 0.0).astype(
                    BF16
                ) * jnp.asarray(0.125, BF16)
                score = score + jnp.where(head_lanes(lane, hh), q, 0.0)
                r.kv[l * 4 + hh, place] = kv.astype(BF16)
            gates = jnp.minimum(score, 0.0) - jnp.log1p(jnp.exp(-jnp.abs(score)))
            r.sig[l * 4 + k] = 1.0 / (1.0 + jnp.exp(score))
            r.kv[l * 4 + 3, place] = pieces(gates, lane)
            send_kv(l, k).start()

        def send_kv(l, k):
            place = pl.ds(pl.multiple_of(WINDOW + (2 * k + d) * BLOCK, WINDOW), BLOCK)
            rows = r.kv.at[pl.ds(l * 4, 4), place]
            return remote(rows, rows, r.kv_s.at[l * 4 + k], r.kv_r.at[l * 4 + k], partner)

        def wait_kv(l, k):
            place = pl.ds(pl.multiple_of(WINDOW + (2 * k + 1 - d) * BLOCK, WINDOW), BLOCK)
            arrived(r.kv.at[pl.ds(l * 4, 4), place], r.kv_r.at[l * 4 + k])

        def attend(l, k):
            block = 2 * k + d
            start = block * BLOCK
            length = r.pk[24:25, 0:1]
            column = lanes((BLOCK, 256))
            row = rows_of((BLOCK, 256))
            distance = row + WINDOW - column
            near_pos = start - WINDOW + column
            near_ok = (
                (column < 192)
                & (near_pos >= 0)
                & (distance >= 0)
                & (distance < WINDOW)
                & ((near_pos < length) | (distance == 0))
            )
            pick_cols = [
                jnp.sum(
                    jnp.where(lanes((64, 128)) == hh * 8 + block, r.pt[...], 0.0),
                    axis=1,
                    keepdims=True,
                ).astype(jnp.int32)
                for hh in range(3)
            ]

            def some(first, count):
                rows = pl.ds(pl.multiple_of(WINDOW + first, WINDOW), count)
                place = lanes((64, count)) + first
                gates = r.kv[l * 4 + 3, rows]
                return tuple(
                    dot(
                        (place == pick_cols[hh]).astype(F32).astype(BF16),
                        jnp.concatenate([r.kv[l * 4 + hh, rows], gates], axis=1),
                    )
                    for hh in range(3)
                )

            def adding(totals, more):
                return tuple(total + one for total, one in zip(totals, more))

            totals = some(pl.multiple_of(k * 256, 256), BLOCK)
            totals = lax.fori_loop(0, k, lambda j, t: adding(t, some(j * 256, 256)), totals)
            totals = lax.fori_loop(0, d, lambda j, t: adding(t, some(start, BLOCK)), totals)
            near = pl.ds(pl.multiple_of(start, BLOCK), 192)
            for hh in range(3):
                index = hh * 8 + block
                chosen = totals[hh].astype(BF16)
                where = (l * 4 + k) * 3 + hh
                r.chosen[where] = chosen[:, 0:128]
                r.keyset[hh, 0:192, 0:128] = r.kv[l * 4 + hh, near]
                r.keyset[hh, 192:256, :] = chosen
                query = jnp.concatenate([r.q[where], ones_tiles[hh]], axis=1)
                logits = dot(query, r.keyset[hh], NT)
                pick_row = r.pk[pl.ds(index, 1), :][:, 128:384]
                far_ok = (
                    (column >= 192) & (pick_row <= start - WINDOW + row) & (pick_row < length)
                )
                masked = jnp.where(near_ok | far_ok, logits, -1e30)
                raised = jnp.exp(masked - jnp.max(masked, axis=1, keepdims=True))
                soft = raised / jnp.sum(raised, axis=1, keepdims=True)
                r.soft[where] = soft
                mixed = dot(soft.astype(BF16), r.keyset[hh, :, 0:128])
                r.merged[l * 4 + k, :, hh * 128 : hh * 128 + 128] = mixed.astype(BF16)
            return dot(r.merged[l * 4 + k], r.wo[l])

        def feed(l, k, half):
            rows = slice(half * HALF, half * HALF + HALF)
            pre = dot(r.normed[8 * l + 4 + k, rows], r.fc[l]) + r.fcb[l]
            square = pre * pre
            wave = jnp.tanh(ROOT * pre * (1.0 + CUBE * square))
            both = 0.5 * (1.0 + wave)
            slope = both + 0.5 * pre * (1.0 - wave * wave) * (ROOT * (1.0 + 3.0 * CUBE * square))
            hidden = (pre * both).astype(BF16)
            r.hidden[l * 4 + k, rows] = hidden
            r.slope[l * 4 + k, rows] = slope.astype(BF16)
            return dot(hidden, r.pj[l])

        def send_part(n, half):
            rows = pl.ds(half * HALF, HALF)
            return remote(
                r.part_out.at[lax.rem(n, 4), rows],
                r.part_in.at[lax.rem(n, 8), rows],
                r.ps_s.at[n * 2 + half],
                r.ps_r.at[n * 2 + half],
                mate_id,
            )

        def give(n, half, part):
            rows = slice(half * HALF, half * HALF + HALF)

            @pl.when(mid)
            def _():
                r.own[lax.rem(n, 4), rows] = part

            @pl.when(jnp.logical_not(mid))
            def _():
                @pl.when(n >= 4)
                def _():
                    send_part(n - 4, half).wait_send()

                r.part_out[lax.rem(n, 4), rows] = part.astype(BF16)
                send_part(n, half).start()

        def give_both(n, part):
            for half in (0, 1):
                give(n, half, part[half * HALF : half * HALF + HALF])

        def send_pair(n, half):
            rows = pl.ds(half * HALF, HALF)
            return remote(
                r.pair_out.at[lax.rem(n, 4), rows],
                r.pair_in.at[lax.rem(n, 8), rows],
                r.mm_s.at[n * 2 + half],
                r.mm_r.at[n * 2 + half],
                other_id,
            )

        def fold(n, half):
            rows = slice(half * HALF, half * HALF + HALF)
            arrived(r.part_in.at[lax.rem(n, 8), rows], r.ps_r.at[n * 2 + half])

            @pl.when(n >= 4)
            def _():
                send_pair(n - 4, half).wait_send()

            both = r.own[lax.rem(n, 4), rows] + r.part_in[lax.rem(n, 8), rows].astype(F32)
            r.pair_out[lax.rem(n, 4), rows] = both.astype(BF16)
            send_pair(n, half).start()

        def total_of(n, half):
            rows = slice(half * HALF, half * HALF + HALF)
            arrived(r.pair_in.at[lax.rem(n, 8), rows], r.mm_r.at[n * 2 + half])
            return r.pair_out[lax.rem(n, 4), rows].astype(F32) + r.pair_in[
                lax.rem(n, 8), rows
            ].astype(F32)

        y_way = (r.y, r.y_stage, r.y_s, r.y_r)
        dx_way = (r.dx, r.dx_stage, r.dx_s, r.dx_r)

        def hand_out(way, k, value):
            way[1][k] = value.astype(F32).T.astype(BF16)
            for side in (0, 1):
                target = 2 * (h - 1) + side
                own = (k == s) & (target == h) & (d == owner)
                local, far = hand_copy(way, k, side)
                pl.when(own)(local.start)
                pl.when(jnp.logical_not(own))(far.start)

        def hand_copy(way, k, side):
            src = way[1].at[k, pl.ds(pl.multiple_of((2 * (h - 1) + side) * local, local), local)]
            dst = way[0].at[slot, :, pl.ds(pl.multiple_of(d * BLOCK, BLOCK), BLOCK)]
            recv = way[3].at[slot, d]
            return (
                pltpu.make_async_copy(src, dst, recv),
                remote(
                    src, dst, way[2].at[k, side], recv, at(k, 2 * (h - 1) + side, owner)
                ),
            )

        def finish_hand(way):
            @pl.when(mid)
            def _():
                for k in range(chunks):
                    for side in (0, 1):
                        own = (k == s) & (2 * (h - 1) + side == h) & (d == owner)
                        pl.when(jnp.logical_not(own))(hand_copy(way, k, side)[1].wait_send)

            for j in range(micro):
                for core in (0, 1):
                    arrived(
                        way[0].at[j, :, core * BLOCK : core * BLOCK + BLOCK],
                        way[3].at[j, core],
                    )

        def leave(n, half):
            c, k = lax.div(n, 4), lax.rem(n, 4)
            rows = slice(half * HALF, half * HALF + HALF)
            state = r.state[n, rows].astype(F32) + total_of(n, half) + r.par[c, 2:3]
            state = state.astype(BF16)

            @pl.when(c < 3)
            def _():
                publish(c + 1, k, half, state)

            @pl.when(c == 3)
            def _():
                r.last[rows] = state
                if half:
                    hand_out(y_way, k, r.last[...])

        def send_grad(index, half):
            rows = r.grad.at[index, half * HALF : half * HALF + HALF]
            return remote(
                rows, rows, r.gx_s.at[index * 2 + half], r.gx_r.at[index * 2 + half], mate_id
            )

        def send_cot(i):
            rows = r.grad.at[
                15 - lax.div(i, 4), pl.ds(pl.multiple_of(lax.rem(i, 4) * 32, 32), 32)
            ]
            return remote(rows, rows, r.cx_s.at[i], r.cx_r.at[i], mate_id)

        def enter_back(i):
            @pl.when(lax.rem(i, 4) == 0)
            def _():
                k = 3 - lax.div(i, 4)
                r.grad[12 + k] = turned(r.cot_in, r.xc_r, k)

            send_cot(i).start()

        def send_norms(c, side, core):
            target = 2 * (h - 1) + side
            recv = r.nr_r.at[s * 2 + d]
            return (
                (c == s) & (target == h) & (d == core),
                pltpu.make_async_copy(r.nrm.at[c], r.nrm_in.at[s * 2 + d], recv),
                remote(
                    r.nrm.at[c],
                    r.nrm_in.at[s * 2 + d],
                    r.nr_s.at[c * 4 + side * 2 + core],
                    recv,
                    at(c, target, core),
                ),
            )

        def all_norms(c):
            return [send_norms(c, side, core) for side in (0, 1) for core in (0, 1)]

        def send_small(c, step):
            whom = lax.rem(s * 2 + d + step, 8)
            return remote(
                r.sm.at[c],
                r.sm_in.at[c * 8 + s * 2 + d],
                r.sm_s.at[c * 8 + step],
                r.sm_r.at[c * 8 + s * 2 + d],
                at(lax.div(whom, 2), h, lax.rem(whom, 2)),
            )

        def push_small(c):
            for step in range(1, 8):
                send_small(c, step).start()

        def leave_back(m, half):
            c, k = 3 - lax.div(m, 4), 3 - lax.rem(m, 4)
            index = c * 4 + k
            rows = slice(half * HALF, half * HALF + HALF)
            total = total_of(16 + m, half)
            scaled, inverse = norm_parts(r.state[index, rows].astype(F32))
            above = r.grad[index, rows].astype(F32)
            t = total * r.par[c, 0:1]
            inner = (
                t
                - jnp.mean(t, axis=-1, keepdims=True)
                - scaled * jnp.mean(t * scaled, axis=-1, keepdims=True)
            )
            below = (above + inverse * inner).astype(BF16)

            @pl.when(c > 0)
            def _():
                r.grad[index - 4, rows] = below
                send_grad(index - 4, half).start()

            @pl.when(c == 0)
            def _():
                r.last[rows] = below
                if half:
                    hand_out(dx_way, k, r.last[...])

            for i, value in enumerate((total * scaled, total, above)):
                r.nrm[c, i : i + 1] = r.nrm[c, i : i + 1] + jnp.sum(value, axis=0, keepdims=True)
            if half:

                @pl.when(k == 0)
                def _():
                    launch(all_norms(c))

        def send_keys(l, step):
            ring = lax.rem(step, 2) * 4
            return remote(
                r.sums.at[pl.ds(ring, 4), 0:BLOCK],
                r.sums_in.at[pl.ds(step * 4, 4)],
                r.dk_s.at[l * 4 + step],
                r.dk_r.at[l * 4 + step],
                partner,
            )

        def attend_back(l, k):
            step = 3 - k
            ring = lax.rem(step, 2) * 4
            block = 2 * k + d
            start = block * BLOCK
            grad_merged = dot(r.grad[8 * l + k], r.wo[l], NT).astype(BF16)

            @pl.when(step >= 2)
            def _():
                send_keys(l, step - 2).wait_send()

            gate_total = jnp.zeros((256, 128), F32)
            for hh in range(3):
                where = (l * 4 + k) * 3 + hh
                near = pl.ds(pl.multiple_of(start, BLOCK), 192)
                keys = jnp.concatenate([r.kv[l * 4 + hh, near], r.chosen[where]], axis=0)
                mixed = grad_merged[:, hh * 128 : hh * 128 + 128]
                soft = r.soft[where]
                grad_soft = dot(mixed, keys, NT)
                grad_logits = (
                    soft * (grad_soft - jnp.sum(grad_soft * soft, axis=1, keepdims=True))
                ).astype(BF16)
                grad_query = dot(grad_logits, keys) * 0.125
                r.dqkv[k, :, hh * 256 : hh * 256 + 128] = jnp.where(
                    lane < 64, grad_query, 0.0
                ).astype(BF16)
                left = jnp.concatenate([grad_logits, soft.astype(BF16)], axis=0)
                right = jnp.concatenate(
                    [
                        jnp.concatenate([r.q[where], ones_tiles[hh]], axis=1),
                        jnp.concatenate([mixed, jnp.zeros_like(mixed)], axis=1),
                    ],
                    axis=0,
                )
                grad_set = dot(left, right, TN)
                far = grad_set[192:256]
                high = far.astype(BF16)
                r.far[hh, pl.ds(k * 128, 64)] = high
                r.far[hh, pl.ds(k * 128 + 64, 64)] = (far - high.astype(F32)).astype(BF16)
                hots = []
                for kk in range(4):
                    pick_row = r.pk[pl.ds(hh * 8 + 2 * kk + d, 1), :][:, 0:128]
                    hit = rows_of((256, 128)) + (start - BLOCK) == pick_row
                    hots.append((hit & (kk >= k)).astype(F32).astype(BF16))
                total = dot(jnp.concatenate(hots, axis=1), r.far[hh])
                r.sums[ring + hh, 0:WINDOW] = total[0:WINDOW, 0:128]
                r.sums[ring + hh, WINDOW:256] = total[WINDOW:256, 0:128] + grad_set[0:192, 0:128]
                gate_total = gate_total + total[:, 128:256]
            r.sums[ring + 3] = gate_total

            @pl.when(block > 0)
            def _():
                send_keys(l, step).start()

        def finish_back(l, k):
            step = 3 - k
            ring = lax.rem(step, 2) * 4
            came = step - d

            @pl.when(came >= 0)
            def _():
                arrived(r.sums_in.at[pl.ds(came * 4, 4)], r.dk_r.at[l * 4 + came])
                for j in range(4):
                    r.sums[ring + j, BLOCK:256] = (
                        r.sums[ring + j, BLOCK:256] + r.sums_in[came * 4 + j]
                    )

            scores = pieces(r.sums[ring + 3, BLOCK:256] * r.sig[l * 4 + k], lane)
            for hh in range(3):
                head = slice(hh * 256, hh * 256 + 128)
                r.dqkv[k, :, head] = jnp.where(
                    head_lanes(lane, hh), scores, r.dqkv[k, :, head]
                )
                r.dqkv[k, :, hh * 256 + 128 : hh * 256 + 256] = r.sums[
                    ring + hh, BLOCK:256
                ].astype(BF16)
            return dot(r.dqkv[k], r.w1[l])

        def feed_back(l, k, half):
            rows = slice(half * HALF, half * HALF + HALF)
            grad_hidden = dot(r.grad[8 * l + 4 + k, rows], r.pj[l], NT)
            grad_pre = (grad_hidden * r.slope[l * 4 + k, rows].astype(F32)).astype(BF16)
            r.dpre[k, rows] = grad_pre
            return dot(grad_pre, r.fc[l], NT)

        def four(ref, first):
            value = ref[pl.ds(first, 4)]
            return value.reshape(4 * BLOCK, value.shape[2])

        ones_rows = jnp.ones((8, 4 * BLOCK), BF16)

        def split(kind, width):
            for section in range(4):
                rows = pl.ds(pl.multiple_of((2 * section + 1 - d) * part_rows, 8), part_rows)
                halves[kind][0][section] = wides[kind][rows, 0:width].astype(BF16)
            send_half(kind).start()

        def send_half(kind):
            return remote(
                halves[kind][0],
                halves[kind][1],
                r.xh_s.at[kind],
                r.xh_r.at[kind],
                partner,
            )

        def send_share(kind, l, step):
            place = l * 3 + step - 1
            return remote(
                shares[kind][0].at[step - 1],
                shares[kind][1].at[place],
                r.yh_s.at[kind, step - 1],
                r.yh_r.at[kind, place],
                at(lax.rem(s + step, 4), h, d),
            )

        def share(kind, width, l):
            arrived(halves[kind][1], r.xh_r.at[kind])
            send_half(kind).wait_send()
            for step in (1, 2, 3, 0):
                section = lax.rem(s + step, 4)
                rows = pl.ds(pl.multiple_of((2 * section + d) * part_rows, 8), part_rows)
                both = wides[kind][rows, 0:width] + halves[kind][1][section].astype(F32)
                if step:
                    shares[kind][0][step - 1] = both.astype(BF16)
                    send_share(kind, l, step).start()
                else:
                    wides[kind][rows, 0:width] = both

        def collect(kind, width, l):
            rows = pl.ds(pl.multiple_of((2 * s + d) * part_rows, 8), part_rows)
            total = wides[kind][rows, 0:width]
            for step in (1, 2, 3):
                place = l * 3 + step - 1
                arrived(shares[kind][1].at[place], r.yh_r.at[kind, place])
                total = total + shares[kind][1][place].astype(F32)
                send_share(kind, l, step).wait_send()
            return total

        def weights_feed(l, part):
            left = four(r.normed, 8 * l + 4) if part < 2 else four(r.grad, 8 * l + 4)
            right = four(r.dpre, 0) if part < 2 else four(r.hidden, 4 * l)
            rows = slice(part % 2 * 384, part % 2 * 384 + 384)
            columns = slice(part // 2 * 768, part // 2 * 768 + 768)
            r.wide_f[rows, columns] = dot(left[:, rows], right, TN)
            if part == 0:
                r.sm[2 * l + 1, 0:1] = dot(ones_rows, right)[0:1]
                push_small(2 * l + 1)
            if part == 3:
                split(0, 1536)

        def weights_attend(l, part):
            wide_lane = lanes((4 * BLOCK, 128))
            if part == 0:
                grads = four(r.dqkv, 0)
                t = [grads[:, i * 256 : i * 256 + 128].astype(F32) for i in range(3)]
                first = jnp.where(wide_lane < 64, t[0], pltpu.roll(t[1], 64, 1))
                second = jnp.where(wide_lane < 64, t[2], t[0] + t[1] + t[2])
                r.packed[:, 0:128] = first.astype(BF16)
                r.packed[:, 128:256] = second.astype(BF16)
                for i in range(3):
                    r.packed[:, 256 + 128 * i : 384 + 128 * i] = grads[
                        :, i * 256 + 128 : i * 256 + 256
                    ]
                r.sm[2 * l, 0:1] = dot(ones_rows, grads)[0:1]
            if part < 2:
                rows = slice(part * 384, part * 384 + 384)
                r.wide_a[rows, 0:640] = dot(four(r.normed, 8 * l)[:, rows], r.packed[...], TN)
            if part == 2:
                merged = four(r.merged, 4 * l)
                u = [merged[:, i * 128 : i * 128 + 128].astype(F32) for i in range(3)]
                packed = jnp.concatenate(
                    [
                        jnp.where(wide_lane < 64, pltpu.roll(u[0], 64, 1), u[1]),
                        jnp.where(wide_lane < 64, pltpu.roll(u[2], 64, 1), 0.0),
                    ],
                    axis=1,
                ).astype(BF16)
                r.wide_a[:, 640:896] = dot(four(r.grad, 8 * l), packed, TN)
            if part == 3:
                send_keys(l, 2).wait_send()

                @pl.when(d == 1)
                def _():
                    send_keys(l, 3).wait_send()

                scores = dot(r.packed[:, 128:256], four(r.normed, 8 * l), TN)
                for hh in range(3):
                    row = 64 + 3 * hh
                    r.sm[2 * l, 1 + hh : 2 + hh] = (
                        scores[row : row + 1] + scores[row + 1 : row + 2] + scores[row + 2 : row + 3]
                    )
                push_small(2 * l)
                split(1, 896)

        def collect_feed(l):
            total = collect(0, 1536, l)
            r.o_fc[l] = total[:, 0:768]
            r.o_pj[l] = total[:, 768:1536]

        def collect_attend(l):
            total = collect(1, 896, l)
            r.o_qkv[3 * l] = total[:, 0:192]
            for i in (0, 1):
                r.o_qkv[3 * l + 1 + i] = jnp.concatenate(
                    [total[:, 256 + 128 * j + 64 * i : 320 + 128 * j + 64 * i] for j in range(3)],
                    axis=1,
                )
            r.o_out[l] = total[:, 640:896].T[0:192]

        def slot_of(n, carry):
            ahead = n < 16
            c = jnp.where(ahead, lax.div(n, 4), 7 - lax.div(n, 4))
            k = jnp.where(ahead, lax.rem(n, 4), 3 - lax.rem(n, 4))
            l = lax.div(c, 2)
            works = n < 32
            attends = lax.rem(c, 2) == 0

            @pl.when((n < DIRECT) | (mid & (n < 4)))
            def _():
                enter(n)

            @pl.when((n == 0) & (d == owner))
            def _():
                launch(cot_parts[3])

            @pl.when((n == 4) & (d == owner))
            def _():
                launch(cot_parts[2])

            @pl.when((n == 8) & (d == owner))
            def _():
                launch(cot_parts[1])

            @pl.when((n == 12) & (d == owner))
            def _():
                launch(cot_parts[0])

            @pl.when(mid & (n >= 4) & (n < 20))
            def _():
                leave(n - 4, 0)

            @pl.when(mid & (n >= 20))
            def _():
                leave_back(n - 20, 0)

            @pl.when(mid & (n >= 3) & (n < 35))
            def _():
                fold(n - 3, 1)

            @pl.when(mid & (n >= 4) & (n < 20))
            def _():
                leave(n - 4, 1)

            @pl.when(mid & (n >= 3) & (n < 19))
            def _():
                enter_back(n - 3)

            @pl.when(mid & (n >= 20))
            def _():
                leave_back(n - 20, 1)

            def come(half):
                rows = slice(half * HALF, half * HALF + HALF)

                @pl.when(jnp.logical_not(mid) & ahead & (n >= DIRECT))
                def _():
                    arrived(r.normed.at[n, rows], r.nx_r.at[n * 2 + half])

                @pl.when(jnp.logical_not(mid) & (n >= 16) & (n < 20))
                def _():
                    for i in (0, 1):
                        piece = (n - 16) * 4 + half * 2 + i
                        arrived(r.grad.at[c * 4 + k, pl.ds(half * HALF + i * 32, 32)], r.cx_r.at[piece])

                @pl.when(jnp.logical_not(mid) & (n >= 20) & works)
                def _():
                    index = c * 4 + k
                    arrived(r.grad.at[index, rows], r.gx_r.at[index * 2 + half])

            @pl.when(attends)
            def _():
                come(0)
                come(1)

            @pl.when((n == 0) | (n == 8))
            def _():
                for copy in attend_loads[0:12]:
                    pltpu.make_async_copy(copy.src_ref, copy.dst_ref, r.load.at[l]).wait()

            @pl.when(n == 4)
            def _():
                for copy in feed_loads:
                    copy.wait()

            @pl.when(ahead & attends)
            def _():
                project(l, k)

            @pl.when(n == 0)
            def _():
                for copy in pick_copies:
                    copy.wait()
                chosen = r.pk_in[owner, slot]
                r.pk[...] = jnp.concatenate(
                    [chosen, chosen, jnp.zeros((32, 192), jnp.int32), chosen], axis=1
                )
                square = jnp.concatenate([chosen.astype(F32), jnp.zeros((32, 64), F32)], axis=1)
                square = jnp.concatenate([square, jnp.zeros((96, 128), F32)], axis=0)
                r.pt[...] = square.T[0:64]

            @pl.when(ahead & attends)
            def _():
                came = k - 1 + d
                pl.when(came >= 0)(lambda: wait_kv(l, came))
                give_both(n, attend(l, k))

            @pl.when(ahead & jnp.logical_not(attends))
            def _():
                for half in (0, 1):
                    come(half)
                    give(n, half, feed(l, k, half))

            @pl.when(jnp.logical_not(ahead) & works & attends)
            def _():
                attend_back(l, k)
                give_both(n, finish_back(l, k))

            @pl.when(jnp.logical_not(ahead) & works & jnp.logical_not(attends))
            def _():
                for half in (0, 1):
                    come(half)
                    give(n, half, feed_back(l, k, half))

            @pl.when(mid & (n >= 2) & (n < 34))
            def _():
                fold(n - 2, 0)

            feed_l, attend_l = 1 - lax.div(n, 28), 1 - lax.div(n, 31)
            for part in range(4):

                @pl.when((n == FEED_PARTS[0][part]) | (n == FEED_PARTS[1][part]))
                def _():
                    weights_feed(feed_l, part)

                @pl.when((n == ATTEND_PARTS[0][part]) | (n == ATTEND_PARTS[1][part]))
                def _():
                    weights_attend(attend_l, part)

            @pl.when((n == FEED_COLLECT[0]) | (n == FEED_COLLECT[1]))
            def _():
                collect_feed(feed_l)

            @pl.when((n == ATTEND_COLLECT[0]) | (n == ATTEND_COLLECT[1]))
            def _():
                collect_attend(attend_l)

            @pl.when((n == FEED_SHARE[0]) | (n == FEED_SHARE[1]))
            def _():
                share(0, 1536, feed_l)

            @pl.when((n == ATTEND_SHARE[0]) | (n == ATTEND_SHARE[1]))
            def _():
                share(1, 896, attend_l)

            return carry

        lax.fori_loop(0, 36, slot_of, 0)

        for c in range(4):
            for step in range(1, 8):
                whose = c * 8 + lax.rem(s * 2 + d + step, 8)
                arrived(r.sm_in.at[whose], r.sm_r.at[whose])
            r.sm_in[c * 8 + s * 2 + d] = r.sm[c]
            total = r.sm_in[c * 8]
            for j in range(1, 8):
                total = total + r.sm_in[c * 8 + j]
            l = c // 2
            if c % 2:
                r.o_fcb[l : l + 1, :] = total[0:1]
            else:
                for i in (0, 1):
                    r.o_qv[l, i : i + 1, :] = jnp.concatenate(
                        [total[0:1, j * 256 + 192 * i : j * 256 + 192 * i + 64] for j in range(3)],
                        axis=1,
                    )
                for j in range(3):
                    r.o_score[j, l : l + 1, :] = total[1 + j : 2 + j]
        for j in range(8):
            arrived(r.nrm_in.at[j], r.nr_r.at[j])
        total = r.nrm_in[0]
        for j in range(1, 8):
            total = total + r.nrm_in[j]
        for j in range(4):

            @pl.when(h == j)
            def _():
                for i, ref in enumerate((r.o_gain, r.o_bias, r.o_ob)):
                    ref[...] = total[i : i + 1, j * 192 : j * 192 + 192]

        finish_hand(y_way)
        finish_hand(dx_way)
        for c in range(4):
            for step in range(1, 8):
                send_small(c, step).wait_send()

        @pl.when(mid)
        def _():
            for c in range(4):
                sent(all_norms(c))

        @pl.when(d == owner)
        def _():
            for copies in stream_parts + cot_parts:
                sent(copies)

        sent(norm_rows)

        @pl.when((s == 0) & jnp.logical_not(mid))
        def _():
            sent(end_rows)

        def drain_kv(i, carry):
            send_kv(lax.div(i, 4), lax.rem(i, 4)).wait_send()
            return carry

        lax.fori_loop(0, 8, drain_kv, 0)

        @pl.when(d == 0)
        def _():
            wait_kv(0, 3)
            wait_kv(1, 3)

        @pl.when(mid)
        def _():
            def drain(i, carry):
                for half in (0, 1):
                    pl.when(i >= DIRECT)(send_normed(i, half).wait_send)
                    pl.when(i < 12)(send_grad(i, half).wait_send)
                send_cot(i).wait_send()
                return carry

            lax.fori_loop(0, 16, drain, 0)
            for n in range(28, 32):
                for half in (0, 1):
                    send_pair(n, half).wait_send()

        @pl.when(jnp.logical_not(mid))
        def _():
            for n in range(28, 32):
                for half in (0, 1):
                    send_part(n, half).wait_send()

    return kernel


def hand_over(*refs):
    count = len(refs) // 2
    for i in range(count):
        refs[count + i][...] = refs[i][...]


def shards(
    stream,
    cotangent,
    lengths,
    picks,
    norm_gain,
    norm_bias,
    out_bias,
    weight_qkv,
    bias_qv,
    weight_score,
    weight_out,
    weight_fc,
    bias_fc,
    weight_proj,
):
    micro, tokens, local = stream.shape
    layers, width = weight_qkv.shape[0], weight_qkv.shape[1]
    inputs = dict(
        stream=stream.transpose(0, 2, 1),
        cot=cotangent.transpose(0, 2, 1),
        lengths=lengths,
        picks=picks.reshape(micro, 24, 64),
        gain=norm_gain,
        shift=norm_bias,
        ob=out_bias,
        wqkv=weight_qkv.transpose(0, 2, 3, 1),
        bqv=bias_qv,
        wscore=weight_score.transpose(2, 0, 1),
        wout=weight_out,
        wfc=weight_fc,
        bfc=bias_fc,
        wpj=weight_proj,
    )
    spaces = dict(
        stream=pl.ANY, cot=pl.ANY, lengths=pltpu.SMEM, wqkv=pl.ANY, wout=pl.ANY, wfc=pl.ANY, wpj=pl.ANY
    )
    part_rows = width // 8
    outputs = dict(
        y=((micro, local, 2 * BLOCK), BF16),
        dx=((micro, local, 2 * BLOCK), BF16),
        o_gain=((1, 192), F32),
        o_bias=((1, 192), F32),
        o_ob=((1, 192), F32),
        o_qkv=((6, part_rows, 192), F32),
        o_qv=((2, 2, 192), F32),
        o_score=((3, 2, 768), F32),
        o_out=((2, 192, part_rows), F32),
        o_fc=((2, part_rows, 768), F32),
        o_fcb=((2, 768), F32),
        o_pj=((2, part_rows, 768), F32),
    )
    dma = pltpu.SemaphoreType.DMA
    scratch = dict(
        stream_in=((4, 768, BLOCK), BF16),
        cot_in=((4, 768, BLOCK), BF16),
        prm=((16, 768), BF16),
        w1=((2, 768, 768), BF16),
        wo=((2, 384, 768), BF16),
        fc=((2, 768, 768), BF16),
        pj=((2, 768, 768), BF16),
        bq=((2, 1, 768), F32),
        fcb=((2, 1, 768), F32),
        prm_in=((4, 4, 16, 768), BF16),
        par=((4, 8, 768), F32),
        last=((BLOCK, 768), BF16),
        pk_out=((micro, 32, 64), jnp.int32),
        pk_in=((2, micro, 32, 64), jnp.int32),
        pk=((32, 384), jnp.int32),
        pt=((64, 128), F32),
        state=((16, BLOCK, 768), BF16),
        normed=((16, BLOCK, 768), BF16),
        q=((24, BLOCK, 128), BF16),
        sig=((8, BLOCK, 128), F32),
        kv=((8, WINDOW + tokens, 128), BF16),
        chosen=((24, 64, 128), BF16),
        keyset=((3, 256, 256), BF16),
        soft=((24, BLOCK, 256), F32),
        merged=((8, BLOCK, 384), BF16),
        hidden=((8, BLOCK, 768), BF16),
        slope=((8, BLOCK, 768), BF16),
        part_out=((4, BLOCK, 768), BF16),
        part_in=((8, BLOCK, 768), BF16),
        own=((4, BLOCK, 768), F32),
        pair_out=((4, BLOCK, 768), BF16),
        pair_in=((8, BLOCK, 768), BF16),
        y_stage=((4, 768, BLOCK), BF16),
        dx_stage=((4, 768, BLOCK), BF16),
        grad=((16, BLOCK, 768), BF16),
        dpre=((4, BLOCK, 768), BF16),
        dqkv=((4, BLOCK, 768), BF16),
        far=((3, 512, 256), BF16),
        sums=((8, 256, 128), F32),
        sums_in=((16, BLOCK, 128), F32),
        wide_f=((768, 1536), F32),
        wide_a=((768, 896), F32),
        packed=((512, 640), BF16),
        xo_f=((4, part_rows, 1536), BF16),
        xi_f=((4, part_rows, 1536), BF16),
        yo_f=((3, part_rows, 1536), BF16),
        yi_f=((6, part_rows, 1536), BF16),
        xo_a=((4, part_rows, 896), BF16),
        xi_a=((4, part_rows, 896), BF16),
        yo_a=((3, part_rows, 896), BF16),
        yi_a=((6, part_rows, 896), BF16),
        nrm=((4, 8, 768), F32),
        nrm_in=((8, 8, 768), F32),
        sm=((4, 8, 768), F32),
        sm_in=((32, 8, 768), F32),
    )
    sems = dict(
        xs_s=(8, 4),
        xs_r=(4, 4),
        xc_s=(8, 4),
        xc_r=(4, 4),
        load=(3,),
        prm_s=(4, 2),
        prm_e=(4,),
        prm_r=(4, 4),
        pick_s=(2,),
        pick_r=(1,),
        nx_s=(32,),
        nx_r=(32,),
        kv_s=(8,),
        kv_r=(8,),
        ps_s=(64,),
        ps_r=(64,),
        mm_s=(64,),
        mm_r=(64,),
        y_s=(4, 2),
        y_r=(2, 2),
        dx_s=(4, 2),
        dx_r=(2, 2),
        cx_s=(16,),
        cx_r=(16,),
        gx_s=(32,),
        gx_r=(32,),
        dk_s=(8,),
        dk_r=(8,),
        xh_s=(2,),
        xh_r=(2,),
        yh_s=(2, 3),
        yh_r=(2, 6),
        sm_s=(32,),
        sm_r=(32,),
        nr_s=(16,),
        nr_r=(8,),
    )
    names = list(inputs) + list(outputs) + list(scratch) + list(sems)
    results = pl.pallas_call(
        make_kernel(names, micro, width // 8, local),
        out_shape=[jax.ShapeDtypeStruct(*spec) for spec in outputs.values()],
        in_specs=[
            pl.BlockSpec(memory_space=spaces.get(name, pltpu.VMEM))
            for name in inputs
        ],
        out_specs=[pl.BlockSpec(memory_space=pltpu.VMEM) for name in outputs],
        scratch_shapes=[pltpu.VMEM(*spec) for spec in scratch.values()]
        + [dma(shape) for shape in sems.values()],
        compiler_params=pltpu.CompilerParams(
            collective_id=0, has_side_effects=True, vmem_limit_bytes=62 * 2**20
        ),
        name="blocks",
    )(*inputs.values())
    results = pl.pallas_call(
        hand_over,
        out_shape=[jax.ShapeDtypeStruct(*spec) for spec in outputs.values()],
        in_specs=[pl.BlockSpec(memory_space=pltpu.VMEM)] * len(outputs),
        out_specs=[pl.BlockSpec(memory_space=pltpu.VMEM)] * len(outputs),
        name="results",
    )(*results)
    o = types.SimpleNamespace(**dict(zip(outputs, results)))
    dp_count = lax.axis_size("dp")
    if dp_count > 2:
        d = lax.rem(lax.axis_index("dp"), 2)

        def scattered(value):
            placed = jnp.zeros((value.shape[0], 2 * part_rows, value.shape[2]), F32)
            placed = lax.dynamic_update_slice(placed, value, (0, d * part_rows, 0))
            return lax.psum_scatter(placed, "dp", scatter_dimension=1, tiled=True)

        o.o_out = scattered(o.o_out.transpose(0, 2, 1)).transpose(0, 2, 1)
        o.o_qkv, o.o_fc, o.o_pj = map(scattered, (o.o_qkv, o.o_fc, o.o_pj))
        sums = (o.o_gain, o.o_bias, o.o_ob, o.o_qv, o.o_score, o.o_fcb)
        o.o_gain, o.o_bias, o.o_ob, o.o_qv, o.o_score, o.o_fcb = jax.tree.map(
            lambda value: 0.5 * value, lax.psum(sums, "dp")
        )
    rows = o.o_fc.shape[1]
    return (
        o.y.transpose(0, 2, 1),
        o.dx.transpose(0, 2, 1),
        o.o_gain,
        o.o_bias,
        o.o_ob,
        o.o_qkv.reshape(layers, 3, rows, 192).transpose(0, 2, 1, 3),
        o.o_qv,
        o.o_score.transpose(1, 2, 0),
        o.o_out,
        o.o_fc,
        o.o_fcb,
        o.o_pj.transpose(0, 2, 1),
    )


def solution(mesh):
    return jax.shard_map(
        shards,
        mesh=mesh,
        in_specs=(
            P("dp", None, "head"),
            P("dp", None, "head"),
            P("dp"),
            P("dp", "head", None, None),
            P("section", None),
            P("section", None),
            P("section", "head"),
            P(None, None, None, "head"),
            P(None, None, "head"),
            P(None, None, "head"),
            P(None, "head", None),
            P(None, None, "head"),
            P(None, "head"),
            P(None, "head", None),
        ),
        out_specs=(
            P("dp", "section", "head"),
            P("dp", "section", "head"),
            P("section", "head"),
            P("section", "head"),
            P("section", "head"),
            P(None, ("section", "dp"), None, "head"),
            P(None, None, "head"),
            P(None, None, "head"),
            P(None, "head", ("section", "dp")),
            P(None, ("section", "dp"), "head"),
            P(None, "head"),
            P(None, "head", ("section", "dp")),
        ),
        check_vma=False,
    )
```

```python
import types

import jax
import jax.numpy as jnp
from jax import lax
from jax.experimental import pallas as pl
from jax.experimental.pallas import tpu as pltpu
from jax.sharding import PartitionSpec as P

MESH = pl.DeviceIdType.MESH
BLOCK = 128
HALF = 64
DIRECT = 1
FEED_PARTS = ((20, 20, 21, 21), (28, 28, 28, 28))
ATTEND_PARTS = ((24, 24, 25, 25), (31, 31, 31, 31))
FEED_SHARE, FEED_COLLECT = (22, 29), (26, 34)
ATTEND_SHARE, ATTEND_COLLECT = (26, 32), (30, 35)
WINDOW = 64
NT = (((1,), (1,)), ((), ()))
TN = (((0,), (0,)), ((), ()))
F32 = jnp.float32
BF16 = jnp.bfloat16
ROOT = 0.7978845608028654
CUBE = 0.044715


def dot(left, right, dims=(((1,), (0,)), ((), ()))):
    return lax.dot_general(left, right, dims, preferred_element_type=F32)


def lanes(shape):
    return lax.broadcasted_iota(jnp.int32, shape, len(shape) - 1)


def rows_of(shape):
    return lax.broadcasted_iota(jnp.int32, shape, len(shape) - 2)


def head_lanes(lane, hh):
    return (lane >= 64 + 3 * hh) & (lane < 67 + 3 * hh)


def pieces(value, lane):
    high = value.astype(BF16)
    rest = value - high.astype(F32)
    middle = rest.astype(BF16)
    low = (rest - middle.astype(F32)).astype(BF16)
    zero = jnp.zeros_like(high)
    used = (lane >= 64) & (lane < 73)
    which = lax.rem(lane - 64 + 3 * 64, 3)
    return jnp.where(
        used & (which == 0),
        high,
        jnp.where(used & (which == 1), middle, jnp.where(used & (which == 2), low, zero)),
    )


def make_kernel(names, micro, part_rows, local):
    def kernel(*refs):
        r = types.SimpleNamespace(**dict(zip(names, refs)))
        wides = (r.wide_f, r.wide_a)
        halves = ((r.xo_f, r.xi_f), (r.xo_a, r.xi_a))
        shares = ((r.yo_f, r.yi_f), (r.yo_a, r.yi_a))
        s, h, dp = lax.axis_index("section"), lax.axis_index("head"), lax.axis_index("dp")
        d = lax.rem(dp, 2)
        pair = dp - d
        mid = (h == 1) | (h == 2)
        mate = h + 1 - 2 * lax.rem(h, 2)
        other = 3 - h
        owner = lax.div(s, micro)
        slot = lax.rem(s, micro)

        def at(section, head, core):
            return (section, head, pair + core)

        def remote(src, dst, send, recv, device):
            return pltpu.make_async_remote_copy(
                src_ref=src,
                dst_ref=dst,
                send_sem=send,
                recv_sem=recv,
                device_id=device,
                device_id_type=MESH,
            )

        partner = at(s, h, 1 - d)
        mate_id = at(s, mate, d)
        other_id = at(s, other, d)

        def arrived(dst, recv):
            remote(dst, dst, recv, recv, partner).wait_recv()

        barrier = pltpu.get_barrier_semaphore()
        flat = (s * 4 + h) * 2 + d

        def greet(step, carry):
            whom = lax.rem(flat + step, 32)
            pl.semaphore_signal(
                barrier,
                inc=1,
                device_id=at(lax.div(whom, 8), lax.rem(lax.div(whom, 2), 4), lax.rem(whom, 2)),
                device_id_type=MESH,
            )
            return carry

        lax.fori_loop(1, 32, greet, 0)

        attend_loads, feed_loads = [], []
        for l in range(2):
            for hh in range(3):
                rows = slice(hh * 64, hh * 64 + 64)
                for part, place in ((0, 0), (1, 128), (2, 192)):
                    attend_loads.append(
                        pltpu.make_async_copy(
                            r.wqkv.at[l, part, rows],
                            r.w1.at[l, hh * 256 + place : hh * 256 + place + 64],
                            r.load.at[l],
                        )
                    )
                attend_loads.append(
                    pltpu.make_async_copy(
                        r.wout.at[l, rows],
                        r.wo.at[l, hh * 128 + 64 : hh * 128 + 128],
                        r.load.at[l],
                    )
                )
            feed_loads.append(pltpu.make_async_copy(r.wfc.at[l], r.fc.at[l], r.load.at[2]))
            feed_loads.append(pltpu.make_async_copy(r.wpj.at[l], r.pj.at[l], r.load.at[2]))

        for copy in attend_loads + feed_loads:
            copy.start()

        r.nrm[...] = jnp.zeros_like(r.nrm)
        r.sm[...] = jnp.zeros_like(r.sm)
        for j in range(micro):
            r.pk_out[j, 0:24] = r.picks[j]
            r.pk_out[j, 24:32] = jnp.zeros((8, 64), jnp.int32) + r.lengths[j]
        short = jnp.concatenate([r.ob[...].astype(F32), jnp.zeros((1, 256 - local), F32)], axis=1)
        r.prm[...] = jnp.concatenate(
            [
                row[:, j * 128 : j * 128 + 128]
                for row, count in ((r.gain[...].astype(F32), 6), (r.shift[...].astype(F32), 6), (short, 2))
                for j in range(count)
            ]
            + [jnp.zeros((2, 128), F32)],
            axis=0,
        ).astype(BF16)

        r.keyset[...] = jnp.zeros_like(r.keyset)
        r.far[...] = jnp.zeros_like(r.far)
        r.kv[:, 0:WINDOW] = jnp.zeros((8, WINDOW, 128), BF16)
        for l in range(2):
            for hh in range(3):
                score = jnp.where(
                    (rows_of((64, 768)) >= 3 * hh) & (rows_of((64, 768)) < 3 * hh + 3),
                    r.wscore[hh, l : l + 1, :].astype(F32),
                    0.0,
                )
                r.w1[l, hh * 256 + 64 : hh * 256 + 128] = score.astype(BF16)
                r.wo[l, hh * 128 : hh * 128 + 64] = jnp.zeros((64, 768), BF16)
            gap = jnp.zeros((1, 128), F32)
            r.fcb[l] = r.bfc[l : l + 1, :].astype(F32)
            bias = r.bqv[l].astype(F32)
            r.bq[l] = jnp.concatenate(
                [
                    piece
                    for hh in range(3)
                    for piece in (
                        bias[0:1, hh * 64 : hh * 64 + 64],
                        gap,
                        bias[1:2, hh * 64 : hh * 64 + 64],
                    )
                ],
                axis=1,
            )

        pl.semaphore_wait(barrier, 31)

        def spread(source, landing, sends, recvs, k, heads):
            copies = []
            for hm in heads:
                for core in (0, 1):
                    src = source.at[slot, :, (2 * k + core) * BLOCK : (2 * k + core + 1) * BLOCK]
                    dst = landing.at[k, pl.ds(pl.multiple_of(h * local, local), local)]
                    recv = recvs.at[h, k]
                    copies.append(
                        (
                            (h == hm) & (d == core),
                            pltpu.make_async_copy(src, dst, recv),
                            remote(
                                src, dst, sends.at[hm * 2 + core, k], recv, at(s, hm, core)
                            ),
                        )
                    )
            return copies

        def launch(copies):
            for own, local, far in copies:
                pl.when(own)(local.start)
                pl.when(jnp.logical_not(own))(far.start)

        def sent(copies):
            for own, local, far in copies:
                pl.when(jnp.logical_not(own))(far.wait_send)

        chunks = 4
        stream_parts = [
            spread(r.stream, r.stream_in, r.xs_s, r.xs_r, k, (1, 2, 0, 3)[: 4 if k < DIRECT else 2])
            for k in range(chunks)
        ]
        cot_parts = [
            spread(r.cot, r.cot_in, r.xc_s, r.xc_r, k, (1, 2)) for k in range(chunks)
        ]
        norm_rows = []
        for step in range(4):
            section = lax.rem(s + step, 4)
            for hm in (1, 2):
                norm_rows.append(
                    (
                        (h == hm) if step == 0 else (h == 4),
                        pltpu.make_async_copy(
                            r.prm, r.prm_in.at[s, h], r.prm_r.at[s, h]
                        ),
                        remote(
                            r.prm,
                            r.prm_in.at[s, h],
                            r.prm_s.at[step, hm - 1],
                            r.prm_r.at[s, h],
                            at(section, hm, d),
                        ),
                    )
                )
        end_rows = [
            (
                s == step,
                pltpu.make_async_copy(r.prm, r.prm_in.at[0, h], r.prm_r.at[0, h]),
                remote(
                    r.prm, r.prm_in.at[0, h], r.prm_e.at[step], r.prm_r.at[0, h], at(step, h, d)
                ),
            )
            for step in range(4)
        ]
        pick_copies = (
            pltpu.make_async_copy(r.pk_out, r.pk_in.at[d], r.pick_s.at[0]),
            remote(r.pk_out, r.pk_in.at[d], r.pick_s.at[1], r.pick_r.at[0], partner),
        )

        launch(norm_rows)

        @pl.when((s == 0) & jnp.logical_not(mid))
        def _():
            launch(end_rows)

        @pl.when(d == owner)
        def _():
            for copies in stream_parts:
                launch(copies)

        for copy in pick_copies:
            copy.start()

        lane = lanes((BLOCK, 128))
        ones_tiles = [jnp.where(head_lanes(lane, hh), 1.0, 0.0).astype(BF16) for hh in range(3)]

        def norm_parts(x):
            center = x - jnp.mean(x, axis=-1, keepdims=True)
            inverse = lax.rsqrt(jnp.mean(center * center, axis=-1, keepdims=True) + 1e-05)
            return center * inverse, inverse

        def unpacked(tile, first, count):
            return jnp.concatenate([tile[first + j : first + j + 1] for j in range(count)], axis=1)

        def prepare():
            arrived(r.prm_in.at[0, h], r.prm_r.at[0, h])
            tile = r.prm_in[0, h].astype(F32)
            r.par[0, 0:1] = unpacked(tile, 0, 6)
            r.par[0, 1:2] = unpacked(tile, 6, 6)

        def prepare_rest():
            for c in range(4):
                for j in range(4):
                    pl.when(jnp.logical_not((c == 0) & (h == j)))(
                        lambda: arrived(r.prm_in.at[c, j], r.prm_r.at[c, j])
                    )
            for c in range(4):
                if c:
                    tile = r.prm_in[c, h].astype(F32)
                    r.par[c, 0:1] = unpacked(tile, 0, 6)
                    r.par[c, 1:2] = unpacked(tile, 6, 6)
                r.par[c, 2:3] = jnp.concatenate(
                    [unpacked(r.prm_in[c, j].astype(F32), 12, 2)[:, 0:local] for j in range(4)],
                    axis=1,
                )

        def publish(c, k, half, state):
            rows = slice(half * HALF, half * HALF + HALF)
            r.state[c * 4 + k, rows] = state
            scaled, _ = norm_parts(state.astype(F32))
            normed = scaled * r.par[c, 0:1] + r.par[c, 1:2]
            r.normed[c * 4 + k, rows] = normed.astype(BF16)
            send_normed(c * 4 + k, half).start()

        def send_normed(n, half):
            rows = r.normed.at[n, half * HALF : half * HALF + HALF]
            return remote(rows, rows, r.nx_s.at[n * 2 + half], r.nx_r.at[n * 2 + half], mate_id)

        def turned(landing, recvs, k):
            for j in range(4):
                arrived(landing.at[k, j * local : j * local + local], recvs.at[j, k])
            return landing[k].astype(F32).T.astype(BF16)

        def enter(k):
            @pl.when(k == 0)
            def _():
                prepare()

            state = turned(r.stream_in, r.xs_r, k)
            r.state[k] = state
            scaled, _ = norm_parts(state.astype(F32))
            r.normed[k] = (scaled * r.par[0, 0:1] + r.par[0, 1:2]).astype(BF16)

            @pl.when(k >= DIRECT)
            def _():
                for half in (0, 1):
                    send_normed(k, half).start()

        def project(l, k):
            x = r.normed[8 * l + k]
            block = 2 * k + d
            place = pl.ds(pl.multiple_of(WINDOW + block * BLOCK, WINDOW), BLOCK)
            score = jnp.zeros((BLOCK, 128), F32)
            for hh in range(3):
                out = dot(x, r.w1[l, hh * 256 : hh * 256 + 256, :], NT)
                out = out + r.bq[l, :, hh * 256 : hh * 256 + 256]
                q, kv = out[:, :128], out[:, 128:]
                r.q[(l * 4 + k) * 3 + hh] = jnp.where(lane < 64, q, 0.0).astype(
                    BF16
                ) * jnp.asarray(0.125, BF16)
                score = score + jnp.where(head_lanes(lane, hh), q, 0.0)
                r.kv[l * 4 + hh, place] = kv.astype(BF16)
            gates = jnp.minimum(score, 0.0) - jnp.log1p(jnp.exp(-jnp.abs(score)))
            r.sig[l * 4 + k] = 1.0 / (1.0 + jnp.exp(score))
            r.kv[l * 4 + 3, place] = pieces(gates, lane)
            send_kv(l, k).start()

        def send_kv(l, k):
            place = pl.ds(pl.multiple_of(WINDOW + (2 * k + d) * BLOCK, WINDOW), BLOCK)
            rows = r.kv.at[pl.ds(l * 4, 4), place]
            return remote(rows, rows, r.kv_s.at[l * 4 + k], r.kv_r.at[l * 4 + k], partner)

        def wait_kv(l, k):
            place = pl.ds(pl.multiple_of(WINDOW + (2 * k + 1 - d) * BLOCK, WINDOW), BLOCK)
            arrived(r.kv.at[pl.ds(l * 4, 4), place], r.kv_r.at[l * 4 + k])

        def attend(l, k):
            block = 2 * k + d
            start = block * BLOCK
            length = r.pk[24:25, 0:1]
            column = lanes((BLOCK, 256))
            row = rows_of((BLOCK, 256))
            distance = row + WINDOW - column
            near_pos = start - WINDOW + column
            near_ok = (
                (column < 192)
                & (near_pos >= 0)
                & (distance >= 0)
                & (distance < WINDOW)
                & ((near_pos < length) | (distance == 0))
            )
            pick_cols = [
                jnp.sum(
                    jnp.where(lanes((64, 128)) == hh * 8 + block, r.pt[...], 0.0),
                    axis=1,
                    keepdims=True,
                ).astype(jnp.int32)
                for hh in range(3)
            ]

            def some(first, count):
                rows = pl.ds(pl.multiple_of(WINDOW + first, WINDOW), count)
                place = lanes((64, count)) + first
                gates = r.kv[l * 4 + 3, rows]
                return tuple(
                    dot(
                        (place == pick_cols[hh]).astype(F32).astype(BF16),
                        jnp.concatenate([r.kv[l * 4 + hh, rows], gates], axis=1),
                    )
                    for hh in range(3)
                )

            def adding(totals, more):
                return tuple(total + one for total, one in zip(totals, more))

            totals = some(pl.multiple_of(k * 256, 256), BLOCK)
            totals = lax.fori_loop(0, k, lambda j, t: adding(t, some(j * 256, 256)), totals)
            totals = lax.fori_loop(0, d, lambda j, t: adding(t, some(start, BLOCK)), totals)
            near = pl.ds(pl.multiple_of(start, BLOCK), 192)
            for hh in range(3):
                index = hh * 8 + block
                chosen = totals[hh].astype(BF16)
                where = (l * 4 + k) * 3 + hh
                r.chosen[where] = chosen[:, 0:128]
                r.keyset[hh, 0:192, 0:128] = r.kv[l * 4 + hh, near]
                r.keyset[hh, 192:256, :] = chosen
                query = jnp.concatenate([r.q[where], ones_tiles[hh]], axis=1)
                logits = dot(query, r.keyset[hh], NT)
                pick_row = r.pk[pl.ds(index, 1), :][:, 128:384]
                far_ok = (
                    (column >= 192) & (pick_row <= start - WINDOW + row) & (pick_row < length)
                )
                masked = jnp.where(near_ok | far_ok, logits, -1e30)
                raised = jnp.exp(masked - jnp.max(masked, axis=1, keepdims=True))
                soft = raised / jnp.sum(raised, axis=1, keepdims=True)
                r.soft[where] = soft
                mixed = dot(soft.astype(BF16), r.keyset[hh, :, 0:128])
                r.merged[l * 4 + k, :, hh * 128 : hh * 128 + 128] = mixed.astype(BF16)
            return dot(r.merged[l * 4 + k], r.wo[l])

        def feed(l, k, half):
            rows = slice(half * HALF, half * HALF + HALF)
            pre = dot(r.normed[8 * l + 4 + k, rows], r.fc[l]) + r.fcb[l]
            square = pre * pre
            wave = jnp.tanh(ROOT * pre * (1.0 + CUBE * square))
            both = 0.5 * (1.0 + wave)
            slope = both + 0.5 * pre * (1.0 - wave * wave) * (ROOT * (1.0 + 3.0 * CUBE * square))
            hidden = (pre * both).astype(BF16)
            r.hidden[l * 4 + k, rows] = hidden
            r.slope[l * 4 + k, rows] = slope.astype(BF16)
            return dot(hidden, r.pj[l])

        def send_part(n, half):
            rows = pl.ds(half * HALF, HALF)
            return remote(
                r.part_out.at[lax.rem(n, 4), rows],
                r.part_in.at[lax.rem(n, 8), rows],
                r.ps_s.at[n * 2 + half],
                r.ps_r.at[n * 2 + half],
                mate_id,
            )

        def give(n, half, part):
            rows = slice(half * HALF, half * HALF + HALF)

            @pl.when(mid)
            def _():
                r.own[lax.rem(n, 4), rows] = part

            @pl.when(jnp.logical_not(mid))
            def _():
                @pl.when(n >= 4)
                def _():
                    send_part(n - 4, half).wait_send()

                r.part_out[lax.rem(n, 4), rows] = part.astype(BF16)
                send_part(n, half).start()

        def give_both(n, part):
            for half in (0, 1):
                give(n, half, part[half * HALF : half * HALF + HALF])

        def send_pair(n, half):
            rows = pl.ds(half * HALF, HALF)
            return remote(
                r.pair_out.at[lax.rem(n, 4), rows],
                r.pair_in.at[lax.rem(n, 8), rows],
                r.mm_s.at[n * 2 + half],
                r.mm_r.at[n * 2 + half],
                other_id,
            )

        def fold(n, half):
            rows = slice(half * HALF, half * HALF + HALF)
            arrived(r.part_in.at[lax.rem(n, 8), rows], r.ps_r.at[n * 2 + half])

            @pl.when(n >= 4)
            def _():
                send_pair(n - 4, half).wait_send()

            both = r.own[lax.rem(n, 4), rows] + r.part_in[lax.rem(n, 8), rows].astype(F32)
            r.pair_out[lax.rem(n, 4), rows] = both.astype(BF16)
            send_pair(n, half).start()

        def total_of(n, half):
            rows = slice(half * HALF, half * HALF + HALF)
            arrived(r.pair_in.at[lax.rem(n, 8), rows], r.mm_r.at[n * 2 + half])
            return r.pair_out[lax.rem(n, 4), rows].astype(F32) + r.pair_in[
                lax.rem(n, 8), rows
            ].astype(F32)

        y_way = (r.y, r.y_stage, r.y_s, r.y_r)
        dx_way = (r.dx, r.dx_stage, r.dx_s, r.dx_r)

        def hand_out(way, k, value):
            way[1][k] = value.astype(F32).T.astype(BF16)
            for side in (0, 1):
                target = 2 * (h - 1) + side
                own = (k == s) & (target == h) & (d == owner)
                local, far = hand_copy(way, k, side)
                pl.when(own)(local.start)
                pl.when(jnp.logical_not(own))(far.start)

        def hand_copy(way, k, side):
            src = way[1].at[k, pl.ds(pl.multiple_of((2 * (h - 1) + side) * local, local), local)]
            dst = way[0].at[slot, :, pl.ds(pl.multiple_of(d * BLOCK, BLOCK), BLOCK)]
            recv = way[3].at[slot, d]
            return (
                pltpu.make_async_copy(src, dst, recv),
                remote(
                    src, dst, way[2].at[k, side], recv, at(k, 2 * (h - 1) + side, owner)
                ),
            )

        def finish_hand(way):
            @pl.when(mid)
            def _():
                for k in range(chunks):
                    for side in (0, 1):
                        own = (k == s) & (2 * (h - 1) + side == h) & (d == owner)
                        pl.when(jnp.logical_not(own))(hand_copy(way, k, side)[1].wait_send)

            for j in range(micro):
                for core in (0, 1):
                    arrived(
                        way[0].at[j, :, core * BLOCK : core * BLOCK + BLOCK],
                        way[3].at[j, core],
                    )

        def leave(n, half):
            c, k = lax.div(n, 4), lax.rem(n, 4)
            rows = slice(half * HALF, half * HALF + HALF)
            state = r.state[n, rows].astype(F32) + total_of(n, half) + r.par[c, 2:3]
            state = state.astype(BF16)

            @pl.when(c < 3)
            def _():
                publish(c + 1, k, half, state)

            @pl.when(c == 3)
            def _():
                r.last[rows] = state
                if half:
                    hand_out(y_way, k, r.last[...])

        def send_grad(index, half):
            rows = r.grad.at[index, half * HALF : half * HALF + HALF]
            return remote(
                rows, rows, r.gx_s.at[index * 2 + half], r.gx_r.at[index * 2 + half], mate_id
            )

        def send_cot(i):
            rows = r.grad.at[
                15 - lax.div(i, 4), pl.ds(pl.multiple_of(lax.rem(i, 4) * 32, 32), 32)
            ]
            return remote(rows, rows, r.cx_s.at[i], r.cx_r.at[i], mate_id)

        def enter_back(i):
            @pl.when(lax.rem(i, 4) == 0)
            def _():
                k = 3 - lax.div(i, 4)
                r.grad[12 + k] = turned(r.cot_in, r.xc_r, k)

            send_cot(i).start()

        def send_norms(c, side, core):
            target = 2 * (h - 1) + side
            recv = r.nr_r.at[s * 2 + d]
            return (
                (c == s) & (target == h) & (d == core),
                pltpu.make_async_copy(r.nrm.at[c], r.nrm_in.at[s * 2 + d], recv),
                remote(
                    r.nrm.at[c],
                    r.nrm_in.at[s * 2 + d],
                    r.nr_s.at[c * 4 + side * 2 + core],
                    recv,
                    at(c, target, core),
                ),
            )

        def all_norms(c):
            return [send_norms(c, side, core) for side in (0, 1) for core in (0, 1)]

        def send_small(c, step):
            whom = lax.rem(s * 2 + d + step, 8)
            return remote(
                r.sm.at[c],
                r.sm_in.at[c * 8 + s * 2 + d],
                r.sm_s.at[c * 8 + step],
                r.sm_r.at[c * 8 + s * 2 + d],
                at(lax.div(whom, 2), h, lax.rem(whom, 2)),
            )

        def push_small(c):
            for step in range(1, 8):
                send_small(c, step).start()

        def leave_back(m, half):
            c, k = 3 - lax.div(m, 4), 3 - lax.rem(m, 4)
            index = c * 4 + k
            rows = slice(half * HALF, half * HALF + HALF)
            total = total_of(16 + m, half)
            scaled, inverse = norm_parts(r.state[index, rows].astype(F32))
            above = r.grad[index, rows].astype(F32)
            t = total * r.par[c, 0:1]
            inner = (
                t
                - jnp.mean(t, axis=-1, keepdims=True)
                - scaled * jnp.mean(t * scaled, axis=-1, keepdims=True)
            )
            below = (above + inverse * inner).astype(BF16)

            @pl.when(c > 0)
            def _():
                r.grad[index - 4, rows] = below
                send_grad(index - 4, half).start()

            @pl.when(c == 0)
            def _():
                r.last[rows] = below
                if half:
                    hand_out(dx_way, k, r.last[...])

            for i, value in enumerate((total * scaled, total, above)):
                r.nrm[c, i : i + 1] = r.nrm[c, i : i + 1] + jnp.sum(value, axis=0, keepdims=True)
            if half:

                @pl.when(k == 0)
                def _():
                    launch(all_norms(c))

        def send_keys(l, step):
            ring = lax.rem(step, 2) * 4
            return remote(
                r.sums.at[pl.ds(ring, 4), 0:BLOCK],
                r.sums_in.at[pl.ds(step * 4, 4)],
                r.dk_s.at[l * 4 + step],
                r.dk_r.at[l * 4 + step],
                partner,
            )

        def attend_back(l, k):
            step = 3 - k
            ring = lax.rem(step, 2) * 4
            block = 2 * k + d
            start = block * BLOCK
            grad_merged = dot(r.grad[8 * l + k], r.wo[l], NT).astype(BF16)

            @pl.when(step >= 2)
            def _():
                send_keys(l, step - 2).wait_send()

            gate_total = jnp.zeros((256, 128), F32)
            for hh in range(3):
                where = (l * 4 + k) * 3 + hh
                near = pl.ds(pl.multiple_of(start, BLOCK), 192)
                keys = jnp.concatenate([r.kv[l * 4 + hh, near], r.chosen[where]], axis=0)
                mixed = grad_merged[:, hh * 128 : hh * 128 + 128]
                soft = r.soft[where]
                grad_soft = dot(mixed, keys, NT)
                grad_logits = (
                    soft * (grad_soft - jnp.sum(grad_soft * soft, axis=1, keepdims=True))
                ).astype(BF16)
                grad_query = dot(grad_logits, keys) * 0.125
                r.dqkv[k, :, hh * 256 : hh * 256 + 128] = jnp.where(
                    lane < 64, grad_query, 0.0
                ).astype(BF16)
                left = jnp.concatenate([grad_logits, soft.astype(BF16)], axis=0)
                right = jnp.concatenate(
                    [
                        jnp.concatenate([r.q[where], ones_tiles[hh]], axis=1),
                        jnp.concatenate([mixed, jnp.zeros_like(mixed)], axis=1),
                    ],
                    axis=0,
                )
                grad_set = dot(left, right, TN)
                far = grad_set[192:256]
                high = far.astype(BF16)
                r.far[hh, pl.ds(k * 128, 64)] = high
                r.far[hh, pl.ds(k * 128 + 64, 64)] = (far - high.astype(F32)).astype(BF16)
                hots = []
                for kk in range(4):
                    pick_row = r.pk[pl.ds(hh * 8 + 2 * kk + d, 1), :][:, 0:128]
                    hit = rows_of((256, 128)) + (start - BLOCK) == pick_row
                    hots.append((hit & (kk >= k)).astype(F32).astype(BF16))
                total = dot(jnp.concatenate(hots, axis=1), r.far[hh])
                r.sums[ring + hh, 0:WINDOW] = total[0:WINDOW, 0:128]
                r.sums[ring + hh, WINDOW:256] = total[WINDOW:256, 0:128] + grad_set[0:192, 0:128]
                gate_total = gate_total + total[:, 128:256]
            r.sums[ring + 3] = gate_total

            @pl.when(block > 0)
            def _():
                send_keys(l, step).start()

        def finish_back(l, k):
            step = 3 - k
            ring = lax.rem(step, 2) * 4
            came = step - d

            @pl.when(came >= 0)
            def _():
                arrived(r.sums_in.at[pl.ds(came * 4, 4)], r.dk_r.at[l * 4 + came])
                for j in range(4):
                    r.sums[ring + j, BLOCK:256] = (
                        r.sums[ring + j, BLOCK:256] + r.sums_in[came * 4 + j]
                    )

            scores = pieces(r.sums[ring + 3, BLOCK:256] * r.sig[l * 4 + k], lane)
            for hh in range(3):
                head = slice(hh * 256, hh * 256 + 128)
                r.dqkv[k, :, head] = jnp.where(
                    head_lanes(lane, hh), scores, r.dqkv[k, :, head]
                )
                r.dqkv[k, :, hh * 256 + 128 : hh * 256 + 256] = r.sums[
                    ring + hh, BLOCK:256
                ].astype(BF16)
            return dot(r.dqkv[k], r.w1[l])

        def feed_back(l, k, half):
            rows = slice(half * HALF, half * HALF + HALF)
            grad_hidden = dot(r.grad[8 * l + 4 + k, rows], r.pj[l], NT)
            grad_pre = (grad_hidden * r.slope[l * 4 + k, rows].astype(F32)).astype(BF16)
            r.dpre[k, rows] = grad_pre
            return dot(grad_pre, r.fc[l], NT)

        def four(ref, first):
            value = ref[pl.ds(first, 4)]
            return value.reshape(4 * BLOCK, value.shape[2])

        ones_rows = jnp.ones((8, 4 * BLOCK), BF16)

        def split(kind, width):
            for step in (1, 2, 3, 0):
                section = lax.rem(s + step, 4)
                rows = pl.ds(pl.multiple_of((2 * section + 1 - d) * part_rows, 8), part_rows)
                halves[kind][0][section] = wides[kind][rows, 0:width].astype(BF16)
                send_half(kind, section).start()

        def send_half(kind, section):
            return remote(
                halves[kind][0].at[section],
                halves[kind][1].at[section],
                r.xh_s.at[kind, section],
                r.xh_r.at[kind, section],
                partner,
            )

        def send_share(kind, l, step):
            place = l * 3 + step - 1
            return remote(
                shares[kind][0].at[step - 1],
                shares[kind][1].at[place],
                r.yh_s.at[kind, step - 1],
                r.yh_r.at[kind, place],
                at(lax.rem(s + step, 4), h, d),
            )

        def share(kind, width, l):
            for step in (1, 2, 3, 0):
                section = lax.rem(s + step, 4)
                arrived(halves[kind][1].at[section], r.xh_r.at[kind, section])
                send_half(kind, section).wait_send()
                rows = pl.ds(pl.multiple_of((2 * section + d) * part_rows, 8), part_rows)
                both = wides[kind][rows, 0:width] + halves[kind][1][section].astype(F32)
                if step:
                    shares[kind][0][step - 1] = both.astype(BF16)
                    send_share(kind, l, step).start()
                else:
                    wides[kind][rows, 0:width] = both

        def collect(kind, width, l):
            rows = pl.ds(pl.multiple_of((2 * s + d) * part_rows, 8), part_rows)
            total = wides[kind][rows, 0:width]
            for step in (1, 2, 3):
                place = l * 3 + step - 1
                arrived(shares[kind][1].at[place], r.yh_r.at[kind, place])
                total = total + shares[kind][1][place].astype(F32)
                send_share(kind, l, step).wait_send()
            return total

        def weights_feed(l, part):
            left = four(r.normed, 8 * l + 4) if part < 2 else four(r.grad, 8 * l + 4)
            right = four(r.dpre, 0) if part < 2 else four(r.hidden, 4 * l)
            rows = slice(part % 2 * 384, part % 2 * 384 + 384)
            columns = slice(part // 2 * 768, part // 2 * 768 + 768)
            r.wide_f[rows, columns] = dot(left[:, rows], right, TN)
            if part == 0:
                r.sm[2 * l + 1, 0:1] = dot(ones_rows, right)[0:1]
                push_small(2 * l + 1)
            if part == 3:
                split(0, 1536)

        def weights_attend(l, part):
            wide_lane = lanes((4 * BLOCK, 128))
            if part == 0:
                grads = four(r.dqkv, 0)
                t = [grads[:, i * 256 : i * 256 + 128].astype(F32) for i in range(3)]
                first = jnp.where(wide_lane < 64, t[0], pltpu.roll(t[1], 64, 1))
                second = jnp.where(wide_lane < 64, t[2], t[0] + t[1] + t[2])
                r.packed[:, 0:128] = first.astype(BF16)
                r.packed[:, 128:256] = second.astype(BF16)
                for i in range(3):
                    r.packed[:, 256 + 128 * i : 384 + 128 * i] = grads[
                        :, i * 256 + 128 : i * 256 + 256
                    ]
                r.sm[2 * l, 0:1] = dot(ones_rows, grads)[0:1]
            if part < 2:
                rows = slice(part * 384, part * 384 + 384)
                r.wide_a[rows, 0:640] = dot(four(r.normed, 8 * l)[:, rows], r.packed[...], TN)
            if part == 2:
                merged = four(r.merged, 4 * l)
                u = [merged[:, i * 128 : i * 128 + 128].astype(F32) for i in range(3)]
                packed = jnp.concatenate(
                    [
                        jnp.where(wide_lane < 64, pltpu.roll(u[0], 64, 1), u[1]),
                        jnp.where(wide_lane < 64, pltpu.roll(u[2], 64, 1), 0.0),
                    ],
                    axis=1,
                ).astype(BF16)
                r.wide_a[:, 640:896] = dot(four(r.grad, 8 * l), packed, TN)
            if part == 3:
                send_keys(l, 2).wait_send()

                @pl.when(d == 1)
                def _():
                    send_keys(l, 3).wait_send()

                scores = dot(r.packed[:, 128:256], four(r.normed, 8 * l), TN)
                for hh in range(3):
                    row = 64 + 3 * hh
                    r.sm[2 * l, 1 + hh : 2 + hh] = (
                        scores[row : row + 1] + scores[row + 1 : row + 2] + scores[row + 2 : row + 3]
                    )
                push_small(2 * l)
                split(1, 896)

        def collect_feed(l):
            total = collect(0, 1536, l)
            r.o_fc[l] = total[:, 0:768]
            r.o_pj[l] = total[:, 768:1536]

        def collect_attend(l):
            total = collect(1, 896, l)
            r.o_qkv[3 * l] = total[:, 0:192]
            for i in (0, 1):
                r.o_qkv[3 * l + 1 + i] = jnp.concatenate(
                    [total[:, 256 + 128 * j + 64 * i : 320 + 128 * j + 64 * i] for j in range(3)],
                    axis=1,
                )
            r.o_out[l] = total[:, 640:896].T[0:192]

        def small_sums(c):
            for step in range(1, 8):
                whose = c * 8 + lax.rem(s * 2 + d + step, 8)
                arrived(r.sm_in.at[whose], r.sm_r.at[whose])
            r.sm_in[c * 8 + s * 2 + d] = r.sm[c]
            total = r.sm_in[c * 8]
            for j in range(1, 8):
                total = total + r.sm_in[c * 8 + j]
            l = c // 2
            if c % 2:
                r.o_fcb[l : l + 1, :] = total[0:1]
            else:
                for i in (0, 1):
                    r.o_qv[l, i : i + 1, :] = jnp.concatenate(
                        [total[0:1, j * 256 + 192 * i : j * 256 + 192 * i + 64] for j in range(3)],
                        axis=1,
                    )
                for j in range(3):
                    r.o_score[j, l : l + 1, :] = total[1 + j : 2 + j]

        def end_sends():
            @pl.when(d == owner)
            def _():
                for copies in stream_parts + cot_parts:
                    sent(copies)

            sent(norm_rows)

            @pl.when((s == 0) & jnp.logical_not(mid))
            def _():
                sent(end_rows)

            def drain_kv(i, carry):
                send_kv(lax.div(i, 4), lax.rem(i, 4)).wait_send()
                return carry

            lax.fori_loop(0, 8, drain_kv, 0)

            @pl.when(d == 0)
            def _():
                wait_kv(0, 3)
                wait_kv(1, 3)

        def end_middle_sends():
            def drain(i, carry):
                for half in (0, 1):
                    pl.when(i >= DIRECT)(send_normed(i, half).wait_send)
                    pl.when((i >= 4) & (i < 12))(send_grad(i, half).wait_send)
                send_cot(i).wait_send()
                return carry

            lax.fori_loop(0, 16, drain, 0)

        def end_small_sends():
            finish_hand(y_way)
            for c in range(1, 4):
                small_sums(c)
                for step in range(1, 8):
                    send_small(c, step).wait_send()

            @pl.when(mid)
            def _():
                for c in range(1, 4):
                    sent(all_norms(c))

        def slot_of(n, carry):
            ahead = n < 16
            c = jnp.where(ahead, lax.div(n, 4), 7 - lax.div(n, 4))
            k = jnp.where(ahead, lax.rem(n, 4), 3 - lax.rem(n, 4))
            l = lax.div(c, 2)
            works = n < 32
            attends = lax.rem(c, 2) == 0

            @pl.when((n < DIRECT) | (mid & (n < 4)))
            def _():
                enter(n)

            pl.when(mid & (n == 2))(prepare_rest)

            @pl.when((n == 0) & (d == owner))
            def _():
                launch(cot_parts[3])

            @pl.when((n == 4) & (d == owner))
            def _():
                launch(cot_parts[2])

            @pl.when((n == 8) & (d == owner))
            def _():
                launch(cot_parts[1])

            @pl.when((n == 12) & (d == owner))
            def _():
                launch(cot_parts[0])

            @pl.when(mid & (n >= 4) & (n < 20))
            def _():
                leave(n - 4, 0)

            @pl.when(mid & (n >= 20))
            def _():
                leave_back(n - 20, 0)

            @pl.when(mid & (n >= 3) & (n < 35))
            def _():
                fold(n - 3, 1)

            @pl.when(mid & (n >= 4) & (n < 20))
            def _():
                leave(n - 4, 1)

            @pl.when(mid & (n >= 3) & (n < 19))
            def _():
                enter_back(n - 3)

            @pl.when(mid & (n >= 20))
            def _():
                leave_back(n - 20, 1)

            def come(half):
                rows = slice(half * HALF, half * HALF + HALF)

                @pl.when(jnp.logical_not(mid) & ahead & (n >= DIRECT))
                def _():
                    arrived(r.normed.at[n, rows], r.nx_r.at[n * 2 + half])

                @pl.when(jnp.logical_not(mid) & (n >= 16) & (n < 20))
                def _():
                    for i in (0, 1):
                        piece = (n - 16) * 4 + half * 2 + i
                        arrived(r.grad.at[c * 4 + k, pl.ds(half * HALF + i * 32, 32)], r.cx_r.at[piece])

                @pl.when(jnp.logical_not(mid) & (n >= 20) & works)
                def _():
                    index = c * 4 + k
                    arrived(r.grad.at[index, rows], r.gx_r.at[index * 2 + half])

            @pl.when(attends)
            def _():
                come(0)
                come(1)

            @pl.when((n == 0) | (n == 8))
            def _():
                for copy in attend_loads[0:12]:
                    pltpu.make_async_copy(copy.src_ref, copy.dst_ref, r.load.at[l]).wait()

            @pl.when(n == 4)
            def _():
                for copy in feed_loads:
                    copy.wait()

            @pl.when(ahead & attends)
            def _():
                project(l, k)

            @pl.when(n == 0)
            def _():
                for copy in pick_copies:
                    copy.wait()
                chosen = r.pk_in[owner, slot]
                r.pk[...] = jnp.concatenate(
                    [chosen, chosen, jnp.zeros((32, 192), jnp.int32), chosen], axis=1
                )
                square = jnp.concatenate([chosen.astype(F32), jnp.zeros((32, 64), F32)], axis=1)
                square = jnp.concatenate([square, jnp.zeros((96, 128), F32)], axis=0)
                r.pt[...] = square.T[0:64]

            @pl.when(ahead & attends)
            def _():
                came = k - 1 + d
                pl.when(came >= 0)(lambda: wait_kv(l, came))
                give_both(n, attend(l, k))

            @pl.when(ahead & jnp.logical_not(attends))
            def _():
                for half in (0, 1):
                    come(half)
                    give(n, half, feed(l, k, half))

            @pl.when(jnp.logical_not(ahead) & works & attends)
            def _():
                attend_back(l, k)
                give_both(n, finish_back(l, k))

            @pl.when(jnp.logical_not(ahead) & works & jnp.logical_not(attends))
            def _():
                for half in (0, 1):
                    come(half)
                    give(n, half, feed_back(l, k, half))

            @pl.when(mid & (n >= 2) & (n < 34))
            def _():
                fold(n - 2, 0)

            feed_l, attend_l = 1 - lax.div(n, 28), 1 - lax.div(n, 31)
            for part in range(4):

                @pl.when((n == FEED_PARTS[0][part]) | (n == FEED_PARTS[1][part]))
                def _():
                    weights_feed(feed_l, part)

                @pl.when((n == ATTEND_PARTS[0][part]) | (n == ATTEND_PARTS[1][part]))
                def _():
                    weights_attend(attend_l, part)

            @pl.when((n == FEED_COLLECT[0]) | (n == FEED_COLLECT[1]))
            def _():
                collect_feed(feed_l)

            @pl.when((n == ATTEND_COLLECT[0]) | (n == ATTEND_COLLECT[1]))
            def _():
                collect_attend(attend_l)

            @pl.when((n == FEED_SHARE[0]) | (n == FEED_SHARE[1]))
            def _():
                share(0, 1536, feed_l)

            @pl.when((n == ATTEND_SHARE[0]) | (n == ATTEND_SHARE[1]))
            def _():
                share(1, 896, attend_l)

            pl.when(n == 32)(end_sends)
            pl.when(mid & (n == 33))(end_middle_sends)
            pl.when(n == 34)(end_small_sends)
            return carry

        lax.fori_loop(0, 36, slot_of, 0)

        small_sums(0)
        for j in range(8):
            arrived(r.nrm_in.at[j], r.nr_r.at[j])
        total = r.nrm_in[0]
        for j in range(1, 8):
            total = total + r.nrm_in[j]
        for j in range(4):

            @pl.when(h == j)
            def _():
                for i, ref in enumerate((r.o_gain, r.o_bias, r.o_ob)):
                    ref[...] = total[i : i + 1, j * 192 : j * 192 + 192]

        finish_hand(dx_way)
        for step in range(1, 8):
            send_small(0, step).wait_send()

        @pl.when(mid)
        def _():
            sent(all_norms(0))
            for i in range(4):
                for half in (0, 1):
                    send_grad(i, half).wait_send()
            for n in range(28, 32):
                for half in (0, 1):
                    send_pair(n, half).wait_send()

        @pl.when(jnp.logical_not(mid))
        def _():
            for n in range(28, 32):
                for half in (0, 1):
                    send_part(n, half).wait_send()

    return kernel


def hand_over(*refs):
    count = len(refs) // 2
    for i in range(count):
        refs[count + i][...] = refs[i][...]


def shards(
    stream,
    cotangent,
    lengths,
    picks,
    norm_gain,
    norm_bias,
    out_bias,
    weight_qkv,
    bias_qv,
    weight_score,
    weight_out,
    weight_fc,
    bias_fc,
    weight_proj,
):
    micro, tokens, local = stream.shape
    layers, width = weight_qkv.shape[0], weight_qkv.shape[1]
    inputs = dict(
        stream=stream.transpose(0, 2, 1),
        cot=cotangent.transpose(0, 2, 1),
        lengths=lengths,
        picks=picks.reshape(micro, 24, 64),
        gain=norm_gain,
        shift=norm_bias,
        ob=out_bias,
        wqkv=weight_qkv.transpose(0, 2, 3, 1),
        bqv=bias_qv,
        wscore=weight_score.transpose(2, 0, 1),
        wout=weight_out,
        wfc=weight_fc,
        bfc=bias_fc,
        wpj=weight_proj,
    )
    spaces = dict(
        stream=pl.ANY, cot=pl.ANY, lengths=pltpu.SMEM, wqkv=pl.ANY, wout=pl.ANY, wfc=pl.ANY, wpj=pl.ANY
    )
    part_rows = width // 8
    outputs = dict(
        y=((micro, local, 2 * BLOCK), BF16),
        dx=((micro, local, 2 * BLOCK), BF16),
        o_gain=((1, 192), F32),
        o_bias=((1, 192), F32),
        o_ob=((1, 192), F32),
        o_qkv=((6, part_rows, 192), F32),
        o_qv=((2, 2, 192), F32),
        o_score=((3, 2, 768), F32),
        o_out=((2, 192, part_rows), F32),
        o_fc=((2, part_rows, 768), F32),
        o_fcb=((2, 768), F32),
        o_pj=((2, part_rows, 768), F32),
    )
    dma = pltpu.SemaphoreType.DMA
    scratch = dict(
        stream_in=((4, 768, BLOCK), BF16),
        cot_in=((4, 768, BLOCK), BF16),
        prm=((16, 128), BF16),
        w1=((2, 768, 768), BF16),
        wo=((2, 384, 768), BF16),
        fc=((2, 768, 768), BF16),
        pj=((2, 768, 768), BF16),
        bq=((2, 1, 768), F32),
        fcb=((2, 1, 768), F32),
        prm_in=((4, 4, 16, 128), BF16),
        par=((4, 8, 768), F32),
        last=((BLOCK, 768), BF16),
        pk_out=((micro, 32, 64), jnp.int32),
        pk_in=((2, micro, 32, 64), jnp.int32),
        pk=((32, 384), jnp.int32),
        pt=((64, 128), F32),
        state=((16, BLOCK, 768), BF16),
        normed=((16, BLOCK, 768), BF16),
        q=((24, BLOCK, 128), BF16),
        sig=((8, BLOCK, 128), F32),
        kv=((8, WINDOW + tokens, 128), BF16),
        chosen=((24, 64, 128), BF16),
        keyset=((3, 256, 256), BF16),
        soft=((24, BLOCK, 256), F32),
        merged=((8, BLOCK, 384), BF16),
        hidden=((8, BLOCK, 768), BF16),
        slope=((8, BLOCK, 768), BF16),
        part_out=((4, BLOCK, 768), BF16),
        part_in=((8, BLOCK, 768), BF16),
        own=((4, BLOCK, 768), F32),
        pair_out=((4, BLOCK, 768), BF16),
        pair_in=((8, BLOCK, 768), BF16),
        y_stage=((4, 768, BLOCK), BF16),
        dx_stage=((4, 768, BLOCK), BF16),
        grad=((16, BLOCK, 768), BF16),
        dpre=((4, BLOCK, 768), BF16),
        dqkv=((4, BLOCK, 768), BF16),
        far=((3, 512, 256), BF16),
        sums=((8, 256, 128), F32),
        sums_in=((16, BLOCK, 128), F32),
        wide_f=((768, 1536), F32),
        wide_a=((768, 896), F32),
        packed=((512, 640), BF16),
        xo_f=((4, part_rows, 1536), BF16),
        xi_f=((4, part_rows, 1536), BF16),
        yo_f=((3, part_rows, 1536), BF16),
        yi_f=((6, part_rows, 1536), BF16),
        xo_a=((4, part_rows, 896), BF16),
        xi_a=((4, part_rows, 896), BF16),
        yo_a=((3, part_rows, 896), BF16),
        yi_a=((6, part_rows, 896), BF16),
        nrm=((4, 8, 768), F32),
        nrm_in=((8, 8, 768), F32),
        sm=((4, 8, 768), F32),
        sm_in=((32, 8, 768), F32),
    )
    sems = dict(
        xs_s=(8, 4),
        xs_r=(4, 4),
        xc_s=(8, 4),
        xc_r=(4, 4),
        load=(3,),
        prm_s=(4, 2),
        prm_e=(4,),
        prm_r=(4, 4),
        pick_s=(2,),
        pick_r=(1,),
        nx_s=(32,),
        nx_r=(32,),
        kv_s=(8,),
        kv_r=(8,),
        ps_s=(64,),
        ps_r=(64,),
        mm_s=(64,),
        mm_r=(64,),
        y_s=(4, 2),
        y_r=(2, 2),
        dx_s=(4, 2),
        dx_r=(2, 2),
        cx_s=(16,),
        cx_r=(16,),
        gx_s=(32,),
        gx_r=(32,),
        dk_s=(8,),
        dk_r=(8,),
        xh_s=(2, 4),
        xh_r=(2, 4),
        yh_s=(2, 3),
        yh_r=(2, 6),
        sm_s=(32,),
        sm_r=(32,),
        nr_s=(16,),
        nr_r=(8,),
    )
    names = list(inputs) + list(outputs) + list(scratch) + list(sems)
    results = pl.pallas_call(
        make_kernel(names, micro, width // 8, local),
        out_shape=[jax.ShapeDtypeStruct(*spec) for spec in outputs.values()],
        in_specs=[
            pl.BlockSpec(memory_space=spaces.get(name, pltpu.VMEM))
            for name in inputs
        ],
        out_specs=[pl.BlockSpec(memory_space=pltpu.VMEM) for name in outputs],
        scratch_shapes=[pltpu.VMEM(*spec) for spec in scratch.values()]
        + [dma(shape) for shape in sems.values()],
        compiler_params=pltpu.CompilerParams(
            collective_id=0, has_side_effects=True, vmem_limit_bytes=62 * 2**20
        ),
        name="blocks",
    )(*inputs.values())
    results = pl.pallas_call(
        hand_over,
        out_shape=[jax.ShapeDtypeStruct(*spec) for spec in outputs.values()],
        in_specs=[pl.BlockSpec(memory_space=pltpu.VMEM)] * len(outputs),
        out_specs=[pl.BlockSpec(memory_space=pltpu.VMEM)] * len(outputs),
        name="results",
    )(*results)
    o = types.SimpleNamespace(**dict(zip(outputs, results)))
    dp_count = lax.axis_size("dp")
    if dp_count > 2:
        d = lax.rem(lax.axis_index("dp"), 2)

        def scattered(value):
            placed = jnp.zeros((value.shape[0], 2 * part_rows, value.shape[2]), F32)
            placed = lax.dynamic_update_slice(placed, value, (0, d * part_rows, 0))
            return lax.psum_scatter(placed, "dp", scatter_dimension=1, tiled=True)

        o.o_out = scattered(o.o_out.transpose(0, 2, 1)).transpose(0, 2, 1)
        o.o_qkv, o.o_fc, o.o_pj = map(scattered, (o.o_qkv, o.o_fc, o.o_pj))
        sums = (o.o_gain, o.o_bias, o.o_ob, o.o_qv, o.o_score, o.o_fcb)
        o.o_gain, o.o_bias, o.o_ob, o.o_qv, o.o_score, o.o_fcb = jax.tree.map(
            lambda value: 0.5 * value, lax.psum(sums, "dp")
        )
    rows = o.o_fc.shape[1]
    return (
        o.y.transpose(0, 2, 1),
        o.dx.transpose(0, 2, 1),
        o.o_gain,
        o.o_bias,
        o.o_ob,
        o.o_qkv.reshape(layers, 3, rows, 192).transpose(0, 2, 1, 3),
        o.o_qv,
        o.o_score.transpose(1, 2, 0),
        o.o_out,
        o.o_fc,
        o.o_fcb,
        o.o_pj.transpose(0, 2, 1),
    )


def solution(mesh):
    return jax.shard_map(
        shards,
        mesh=mesh,
        in_specs=(
            P("dp", None, "head"),
            P("dp", None, "head"),
            P("dp"),
            P("dp", "head", None, None),
            P("section", None),
            P("section", None),
            P("section", "head"),
            P(None, None, None, "head"),
            P(None, None, "head"),
            P(None, None, "head"),
            P(None, "head", None),
            P(None, None, "head"),
            P(None, "head"),
            P(None, "head", None),
        ),
        out_specs=(
            P("dp", "section", "head"),
            P("dp", "section", "head"),
            P("section", "head"),
            P("section", "head"),
            P("section", "head"),
            P(None, ("section", "dp"), None, "head"),
            P(None, None, "head"),
            P(None, None, "head"),
            P(None, "head", ("section", "dp")),
            P(None, ("section", "dp"), "head"),
            P(None, "head"),
            P(None, "head", ("section", "dp")),
        ),
        check_vma=False,
    )
```

```python
import types

import jax
import jax.numpy as jnp
from jax import lax
from jax.experimental import pallas as pl
from jax.experimental.pallas import tpu as pltpu
from jax.sharding import PartitionSpec as P

MESH = pl.DeviceIdType.MESH
BLOCK = 128
HALF = 64
DIRECT = 1
FEED_PARTS = ((20, 20, 21, 21), (28, 28, 28, 28))
ATTEND_PARTS = ((24, 24, 25, 25), (31, 31, 31, 31))
FEED_SHARE, FEED_COLLECT = (22, 29), (26, 34)
ATTEND_SHARE, ATTEND_COLLECT = (26, 32), (30, 35)
WINDOW = 64
NT = (((1,), (1,)), ((), ()))
TN = (((0,), (0,)), ((), ()))
F32 = jnp.float32
BF16 = jnp.bfloat16
ROOT = 0.7978845608028654
CUBE = 0.044715


def dot(left, right, dims=(((1,), (0,)), ((), ()))):
    return lax.dot_general(left, right, dims, preferred_element_type=F32)


def lanes(shape):
    return lax.broadcasted_iota(jnp.int32, shape, len(shape) - 1)


def rows_of(shape):
    return lax.broadcasted_iota(jnp.int32, shape, len(shape) - 2)


def head_lanes(lane, hh):
    return (lane >= 64 + 3 * hh) & (lane < 67 + 3 * hh)


def pieces(value, lane):
    high = value.astype(BF16)
    rest = value - high.astype(F32)
    middle = rest.astype(BF16)
    low = (rest - middle.astype(F32)).astype(BF16)
    zero = jnp.zeros_like(high)
    used = (lane >= 64) & (lane < 73)
    which = lax.rem(lane - 64 + 3 * 64, 3)
    return jnp.where(
        used & (which == 0),
        high,
        jnp.where(used & (which == 1), middle, jnp.where(used & (which == 2), low, zero)),
    )


def make_kernel(names, micro, part_rows, local):
    def kernel(*refs):
        r = types.SimpleNamespace(**dict(zip(names, refs)))
        wides = (r.wide_f, r.wide_a)
        halves = ((r.xo_f, r.xi_f), (r.xo_a, r.xi_a))
        shares = ((r.yo_f, r.yi_f), (r.yo_a, r.yi_a))
        s, h, dp = lax.axis_index("section"), lax.axis_index("head"), lax.axis_index("dp")
        d = lax.rem(dp, 2)
        pair = dp - d
        mid = (h == 1) | (h == 2)
        mate = h + 1 - 2 * lax.rem(h, 2)
        other = 3 - h
        owner = lax.div(s, micro)
        slot = lax.rem(s, micro)

        def at(section, head, core):
            return (section, head, pair + core)

        def remote(src, dst, send, recv, device):
            return pltpu.make_async_remote_copy(
                src_ref=src,
                dst_ref=dst,
                send_sem=send,
                recv_sem=recv,
                device_id=device,
                device_id_type=MESH,
            )

        partner = at(s, h, 1 - d)
        mate_id = at(s, mate, d)
        other_id = at(s, other, d)

        def arrived(dst, recv):
            remote(dst, dst, recv, recv, partner).wait_recv()

        barrier = pltpu.get_barrier_semaphore()
        flat = (s * 4 + h) * 2 + d

        def greet(step, carry):
            whom = lax.rem(flat + step, 32)
            pl.semaphore_signal(
                barrier,
                inc=1,
                device_id=at(lax.div(whom, 8), lax.rem(lax.div(whom, 2), 4), lax.rem(whom, 2)),
                device_id_type=MESH,
            )
            return carry

        lax.fori_loop(1, 32, greet, 0)

        attend_loads, feed_loads = [], []
        for l in range(2):
            for hh in range(3):
                rows = slice(hh * 64, hh * 64 + 64)
                for part, place in ((0, 0), (1, 128), (2, 192)):
                    attend_loads.append(
                        pltpu.make_async_copy(
                            r.wqkv.at[l, part, rows],
                            r.w1.at[l, hh * 256 + place : hh * 256 + place + 64],
                            r.load.at[l],
                        )
                    )
                attend_loads.append(
                    pltpu.make_async_copy(
                        r.wout.at[l, rows],
                        r.wo.at[l, hh * 128 + 64 : hh * 128 + 128],
                        r.load.at[l],
                    )
                )
            feed_loads.append(pltpu.make_async_copy(r.wfc.at[l], r.fc.at[l], r.load.at[2]))
            feed_loads.append(pltpu.make_async_copy(r.wpj.at[l], r.pj.at[l], r.load.at[2]))

        for copy in attend_loads + feed_loads:
            copy.start()

        r.nrm[...] = jnp.zeros_like(r.nrm)
        r.nrm_out[...] = jnp.zeros_like(r.nrm_out)
        r.sm[...] = jnp.zeros_like(r.sm)
        for j in range(micro):
            r.pk_out[j, 0:24] = r.picks[j]
            r.pk_out[j, 24:32] = jnp.zeros((8, 64), jnp.int32) + r.lengths[j]
        short = jnp.concatenate([r.ob[...].astype(F32), jnp.zeros((1, 256 - local), F32)], axis=1)
        r.prm[...] = jnp.concatenate(
            [
                row[:, j * 128 : j * 128 + 128]
                for row, count in ((r.gain[...].astype(F32), 6), (r.shift[...].astype(F32), 6), (short, 2))
                for j in range(count)
            ]
            + [jnp.zeros((2, 128), F32)],
            axis=0,
        ).astype(BF16)

        r.keyset[...] = jnp.zeros_like(r.keyset)
        r.far[...] = jnp.zeros_like(r.far)
        r.kv[:, 0:WINDOW] = jnp.zeros((8, WINDOW, 128), BF16)
        for l in range(2):
            for hh in range(3):
                score = jnp.where(
                    (rows_of((64, 768)) >= 3 * hh) & (rows_of((64, 768)) < 3 * hh + 3),
                    r.wscore[hh, l : l + 1, :].astype(F32),
                    0.0,
                )
                r.w1[l, hh * 256 + 64 : hh * 256 + 128] = score.astype(BF16)
                r.wo[l, hh * 128 : hh * 128 + 64] = jnp.zeros((64, 768), BF16)
            gap = jnp.zeros((1, 128), F32)
            r.fcb[l] = r.bfc[l : l + 1, :].astype(F32)
            bias = r.bqv[l].astype(F32)
            r.bq[l] = jnp.concatenate(
                [
                    piece
                    for hh in range(3)
                    for piece in (
                        bias[0:1, hh * 64 : hh * 64 + 64],
                        gap,
                        bias[1:2, hh * 64 : hh * 64 + 64],
                    )
                ],
                axis=1,
            )

        pl.semaphore_wait(barrier, 31)

        def spread(source, landing, sends, recvs, k, heads):
            copies = []
            for hm in heads:
                for core in (0, 1):
                    src = source.at[slot, :, (2 * k + core) * BLOCK : (2 * k + core + 1) * BLOCK]
                    dst = landing.at[k, pl.ds(pl.multiple_of(h * local, local), local)]
                    recv = recvs.at[h, k]
                    copies.append(
                        (
                            (h == hm) & (d == core),
                            pltpu.make_async_copy(src, dst, recv),
                            remote(
                                src, dst, sends.at[hm * 2 + core, k], recv, at(s, hm, core)
                            ),
                        )
                    )
            return copies

        def launch(copies):
            for own, local, far in copies:
                pl.when(own)(local.start)
                pl.when(jnp.logical_not(own))(far.start)

        def sent(copies):
            for own, local, far in copies:
                pl.when(jnp.logical_not(own))(far.wait_send)

        chunks = 4
        stream_parts = [
            spread(r.stream, r.stream_in, r.xs_s, r.xs_r, k, (1, 2, 0, 3)[: 4 if k < DIRECT else 2])
            for k in range(chunks)
        ]
        cot_parts = [
            spread(r.cot, r.cot_in, r.xc_s, r.xc_r, k, (1, 2)) for k in range(chunks)
        ]
        norm_rows = []
        for step in range(4):
            section = lax.rem(s + step, 4)
            for hm in (1, 2):
                norm_rows.append(
                    (
                        (h == hm) if step == 0 else (h == 4),
                        pltpu.make_async_copy(
                            r.prm, r.prm_in.at[s, h], r.prm_r.at[s, h]
                        ),
                        remote(
                            r.prm,
                            r.prm_in.at[s, h],
                            r.prm_s.at[step, hm - 1],
                            r.prm_r.at[s, h],
                            at(section, hm, d),
                        ),
                    )
                )
        end_rows = [
            (
                s == step,
                pltpu.make_async_copy(r.prm, r.prm_in.at[0, h], r.prm_r.at[0, h]),
                remote(
                    r.prm, r.prm_in.at[0, h], r.prm_e.at[step], r.prm_r.at[0, h], at(step, h, d)
                ),
            )
            for step in range(4)
        ]
        pick_copies = (
            pltpu.make_async_copy(r.pk_out, r.pk_in.at[d], r.pick_s.at[0]),
            remote(r.pk_out, r.pk_in.at[d], r.pick_s.at[1], r.pick_r.at[0], partner),
        )

        launch(norm_rows)

        @pl.when((s == 0) & jnp.logical_not(mid))
        def _():
            launch(end_rows)

        @pl.when(d == owner)
        def _():
            for copies in stream_parts:
                launch(copies)

        for copy in pick_copies:
            copy.start()

        lane = lanes((BLOCK, 128))
        ones_tiles = [jnp.where(head_lanes(lane, hh), 1.0, 0.0).astype(BF16) for hh in range(3)]

        def norm_parts(x):
            center = x - jnp.mean(x, axis=-1, keepdims=True)
            inverse = lax.rsqrt(jnp.mean(center * center, axis=-1, keepdims=True) + 1e-05)
            return center * inverse, inverse

        def unpacked(tile, first, count):
            return jnp.concatenate([tile[first + j : first + j + 1] for j in range(count)], axis=1)

        def prepare():
            arrived(r.prm_in.at[0, h], r.prm_r.at[0, h])
            tile = r.prm_in[0, h].astype(F32)
            r.par[0, 0:1] = unpacked(tile, 0, 6)
            r.par[0, 1:2] = unpacked(tile, 6, 6)

        def prepare_rest():
            for c in range(4):
                for j in range(4):
                    pl.when(jnp.logical_not((c == 0) & (h == j)))(
                        lambda: arrived(r.prm_in.at[c, j], r.prm_r.at[c, j])
                    )
            for c in range(4):
                if c:
                    tile = r.prm_in[c, h].astype(F32)
                    r.par[c, 0:1] = unpacked(tile, 0, 6)
                    r.par[c, 1:2] = unpacked(tile, 6, 6)
                r.par[c, 2:3] = jnp.concatenate(
                    [unpacked(r.prm_in[c, j].astype(F32), 12, 2)[:, 0:local] for j in range(4)],
                    axis=1,
                )

        def publish(c, k, half, state):
            rows = slice(half * HALF, half * HALF + HALF)
            r.state[c * 4 + k, rows] = state
            scaled, _ = norm_parts(state.astype(F32))
            normed = scaled * r.par[c, 0:1] + r.par[c, 1:2]
            r.normed[c * 4 + k, rows] = normed.astype(BF16)
            send_normed(c * 4 + k, half).start()

        def send_normed(n, half):
            rows = r.normed.at[n, half * HALF : half * HALF + HALF]
            return remote(rows, rows, r.nx_s.at[n * 2 + half], r.nx_r.at[n * 2 + half], mate_id)

        def turned(landing, recvs, k):
            for j in range(4):
                arrived(landing.at[k, j * local : j * local + local], recvs.at[j, k])
            return landing[k].astype(F32).T.astype(BF16)

        def enter(k):
            @pl.when(k == 0)
            def _():
                prepare()

            state = turned(r.stream_in, r.xs_r, k)
            r.state[k] = state
            scaled, _ = norm_parts(state.astype(F32))
            r.normed[k] = (scaled * r.par[0, 0:1] + r.par[0, 1:2]).astype(BF16)

            @pl.when(k >= DIRECT)
            def _():
                for half in (0, 1):
                    send_normed(k, half).start()

        def project(l, k):
            x = r.normed[8 * l + k]
            block = 2 * k + d
            place = pl.ds(pl.multiple_of(WINDOW + block * BLOCK, WINDOW), BLOCK)
            score = jnp.zeros((BLOCK, 128), F32)
            for hh in range(3):
                out = dot(x, r.w1[l, hh * 256 : hh * 256 + 256, :], NT)
                out = out + r.bq[l, :, hh * 256 : hh * 256 + 256]
                q, kv = out[:, :128], out[:, 128:]
                r.q[(l * 4 + k) * 3 + hh] = jnp.where(lane < 64, q, 0.0).astype(
                    BF16
                ) * jnp.asarray(0.125, BF16)
                score = score + jnp.where(head_lanes(lane, hh), q, 0.0)
                r.kv[l * 4 + hh, place] = kv.astype(BF16)
            gates = jnp.minimum(score, 0.0) - jnp.log1p(jnp.exp(-jnp.abs(score)))
            r.sig[l * 4 + k] = 1.0 / (1.0 + jnp.exp(score))
            r.kv[l * 4 + 3, place] = pieces(gates, lane)
            send_kv(l, k).start()

        def send_kv(l, k):
            place = pl.ds(pl.multiple_of(WINDOW + (2 * k + d) * BLOCK, WINDOW), BLOCK)
            rows = r.kv.at[pl.ds(l * 4, 4), place]
            return remote(rows, rows, r.kv_s.at[l * 4 + k], r.kv_r.at[l * 4 + k], partner)

        def wait_kv(l, k):
            place = pl.ds(pl.multiple_of(WINDOW + (2 * k + 1 - d) * BLOCK, WINDOW), BLOCK)
            arrived(r.kv.at[pl.ds(l * 4, 4), place], r.kv_r.at[l * 4 + k])

        def attend(l, k):
            block = 2 * k + d
            start = block * BLOCK
            length = r.pk[24:25, 0:1]
            column = lanes((BLOCK, 256))
            row = rows_of((BLOCK, 256))
            distance = row + WINDOW - column
            near_pos = start - WINDOW + column
            near_ok = (
                (column < 192)
                & (near_pos >= 0)
                & (distance >= 0)
                & (distance < WINDOW)
                & ((near_pos < length) | (distance == 0))
            )
            pick_cols = [
                jnp.sum(
                    jnp.where(lanes((64, 128)) == hh * 8 + block, r.pt[...], 0.0),
                    axis=1,
                    keepdims=True,
                ).astype(jnp.int32)
                for hh in range(3)
            ]

            def some(first, count):
                rows = pl.ds(pl.multiple_of(WINDOW + first, WINDOW), count)
                place = lanes((64, count)) + first
                gates = r.kv[l * 4 + 3, rows]
                return tuple(
                    dot(
                        (place == pick_cols[hh]).astype(F32).astype(BF16),
                        jnp.concatenate([r.kv[l * 4 + hh, rows], gates], axis=1),
                    )
                    for hh in range(3)
                )

            def adding(totals, more):
                return tuple(total + one for total, one in zip(totals, more))

            totals = some(pl.multiple_of(k * 256, 256), BLOCK)
            totals = lax.fori_loop(0, k, lambda j, t: adding(t, some(j * 256, 256)), totals)
            totals = lax.fori_loop(0, d, lambda j, t: adding(t, some(start, BLOCK)), totals)
            near = pl.ds(pl.multiple_of(start, BLOCK), 192)
            for hh in range(3):
                index = hh * 8 + block
                chosen = totals[hh].astype(BF16)
                where = (l * 4 + k) * 3 + hh
                r.chosen[where] = chosen[:, 0:128]
                r.keyset[hh, 0:192, 0:128] = r.kv[l * 4 + hh, near]
                r.keyset[hh, 192:256, :] = chosen
                query = jnp.concatenate([r.q[where], ones_tiles[hh]], axis=1)
                logits = dot(query, r.keyset[hh], NT)
                pick_row = r.pk[pl.ds(index, 1), :][:, 128:384]
                far_ok = (
                    (column >= 192) & (pick_row <= start - WINDOW + row) & (pick_row < length)
                )
                masked = jnp.where(near_ok | far_ok, logits, -1e30)
                raised = jnp.exp(masked - jnp.max(masked, axis=1, keepdims=True))
                soft = raised / jnp.sum(raised, axis=1, keepdims=True)
                r.soft[where] = soft
                mixed = dot(soft.astype(BF16), r.keyset[hh, :, 0:128])
                r.merged[l * 4 + k, :, hh * 128 : hh * 128 + 128] = mixed.astype(BF16)
            return dot(r.merged[l * 4 + k], r.wo[l])

        def feed(l, k, half):
            rows = slice(half * HALF, half * HALF + HALF)
            pre = dot(r.normed[8 * l + 4 + k, rows], r.fc[l]) + r.fcb[l]
            square = pre * pre
            wave = jnp.tanh(ROOT * pre * (1.0 + CUBE * square))
            both = 0.5 * (1.0 + wave)
            slope = both + 0.5 * pre * (1.0 - wave * wave) * (ROOT * (1.0 + 3.0 * CUBE * square))
            hidden = (pre * both).astype(BF16)
            r.hidden[l * 4 + k, rows] = hidden
            r.slope[l * 4 + k, rows] = slope.astype(BF16)
            return dot(hidden, r.pj[l])

        def send_part(n, half):
            rows = pl.ds(half * HALF, HALF)
            return remote(
                r.part_out.at[lax.rem(n, 4), rows],
                r.part_in.at[lax.rem(n, 8), rows],
                r.ps_s.at[n * 2 + half],
                r.ps_r.at[n * 2 + half],
                mate_id,
            )

        def give(n, half, part):
            rows = slice(half * HALF, half * HALF + HALF)

            @pl.when(mid)
            def _():
                r.own[lax.rem(n, 4), rows] = part

            @pl.when(jnp.logical_not(mid))
            def _():
                @pl.when(n >= 4)
                def _():
                    send_part(n - 4, half).wait_send()

                r.part_out[lax.rem(n, 4), rows] = part.astype(BF16)
                send_part(n, half).start()

        def give_both(n, part):
            for half in (0, 1):
                give(n, half, part[half * HALF : half * HALF + HALF])

        def send_pair(n, half):
            rows = pl.ds(half * HALF, HALF)
            return remote(
                r.pair_out.at[lax.rem(n, 4), rows],
                r.pair_in.at[lax.rem(n, 8), rows],
                r.mm_s.at[n * 2 + half],
                r.mm_r.at[n * 2 + half],
                other_id,
            )

        def fold(n, half):
            rows = slice(half * HALF, half * HALF + HALF)
            arrived(r.part_in.at[lax.rem(n, 8), rows], r.ps_r.at[n * 2 + half])

            @pl.when(n >= 4)
            def _():
                send_pair(n - 4, half).wait_send()

            both = r.own[lax.rem(n, 4), rows] + r.part_in[lax.rem(n, 8), rows].astype(F32)
            r.pair_out[lax.rem(n, 4), rows] = both.astype(BF16)
            send_pair(n, half).start()

        def total_of(n, half):
            rows = slice(half * HALF, half * HALF + HALF)
            arrived(r.pair_in.at[lax.rem(n, 8), rows], r.mm_r.at[n * 2 + half])
            return r.pair_out[lax.rem(n, 4), rows].astype(F32) + r.pair_in[
                lax.rem(n, 8), rows
            ].astype(F32)

        y_way = (r.y, r.y_stage, r.y_s, r.y_r)
        dx_way = (r.dx, r.dx_stage, r.dx_s, r.dx_r)

        def hand_out(way, k, value):
            way[1][k] = value.astype(F32).T.astype(BF16)
            for side in (0, 1):
                target = 2 * (h - 1) + side
                own = (k == s) & (target == h) & (d == owner)
                local, far = hand_copy(way, k, side)
                pl.when(own)(local.start)
                pl.when(jnp.logical_not(own))(far.start)

        def hand_copy(way, k, side):
            src = way[1].at[k, pl.ds(pl.multiple_of((2 * (h - 1) + side) * local, local), local)]
            dst = way[0].at[slot, :, pl.ds(pl.multiple_of(d * BLOCK, BLOCK), BLOCK)]
            recv = way[3].at[slot, d]
            return (
                pltpu.make_async_copy(src, dst, recv),
                remote(
                    src, dst, way[2].at[k, side], recv, at(k, 2 * (h - 1) + side, owner)
                ),
            )

        def finish_hand(way):
            @pl.when(mid)
            def _():
                for k in range(chunks):
                    for side in (0, 1):
                        own = (k == s) & (2 * (h - 1) + side == h) & (d == owner)
                        pl.when(jnp.logical_not(own))(hand_copy(way, k, side)[1].wait_send)

            for j in range(micro):
                for core in (0, 1):
                    arrived(
                        way[0].at[j, :, core * BLOCK : core * BLOCK + BLOCK],
                        way[3].at[j, core],
                    )

        def leave(n, half):
            c, k = lax.div(n, 4), lax.rem(n, 4)
            rows = slice(half * HALF, half * HALF + HALF)
            state = r.state[n, rows].astype(F32) + total_of(n, half) + r.par[c, 2:3]
            state = state.astype(BF16)

            @pl.when(c < 3)
            def _():
                publish(c + 1, k, half, state)

            @pl.when(c == 3)
            def _():
                r.last[rows] = state
                if half:
                    hand_out(y_way, k, r.last[...])

        def send_grad(index, half):
            rows = r.grad.at[index, half * HALF : half * HALF + HALF]
            return remote(
                rows, rows, r.gx_s.at[index * 2 + half], r.gx_r.at[index * 2 + half], mate_id
            )

        def send_cot(i):
            rows = r.grad.at[
                15 - lax.div(i, 4), pl.ds(pl.multiple_of(lax.rem(i, 4) * 32, 32), 32)
            ]
            return remote(rows, rows, r.cx_s.at[i], r.cx_r.at[i], mate_id)

        def enter_back(i):
            @pl.when(lax.rem(i, 4) == 0)
            def _():
                k = 3 - lax.div(i, 4)
                r.grad[12 + k] = turned(r.cot_in, r.xc_r, k)

            send_cot(i).start()

        def send_norms(c, side, core):
            target = 2 * (h - 1) + side
            recv = r.nr_r.at[s * 2 + d]
            src = r.nrm_out.at[c * 2 + side]
            return (
                (c == s) & (target == h) & (d == core),
                pltpu.make_async_copy(src, r.nrm_in.at[s * 2 + d], recv),
                remote(
                    src,
                    r.nrm_in.at[s * 2 + d],
                    r.nr_s.at[c * 4 + side * 2 + core],
                    recv,
                    at(c, target, core),
                ),
            )

        def all_norms(c):
            return [send_norms(c, side, core) for side in (0, 1) for core in (0, 1)]

        def send_small(c, step):
            whom = lax.rem(s * 2 + d + step, 8)
            return remote(
                r.sm.at[c],
                r.sm_in.at[c * 8 + s * 2 + d],
                r.sm_s.at[c * 8 + step],
                r.sm_r.at[c * 8 + s * 2 + d],
                at(lax.div(whom, 2), h, lax.rem(whom, 2)),
            )

        def folded(row):
            return jnp.concatenate([row[:, j * 128 : j * 128 + 128] for j in range(6)], axis=0)

        def push_small(c):
            for step in range(1, 8):
                send_small(c, step).start()

        def leave_back(m, half):
            c, k = 3 - lax.div(m, 4), 3 - lax.rem(m, 4)
            index = c * 4 + k
            rows = slice(half * HALF, half * HALF + HALF)
            total = total_of(16 + m, half)
            scaled, inverse = norm_parts(r.state[index, rows].astype(F32))
            above = r.grad[index, rows].astype(F32)
            t = total * r.par[c, 0:1]
            inner = (
                t
                - jnp.mean(t, axis=-1, keepdims=True)
                - scaled * jnp.mean(t * scaled, axis=-1, keepdims=True)
            )
            below = (above + inverse * inner).astype(BF16)

            @pl.when(c > 0)
            def _():
                r.grad[index - 4, rows] = below
                send_grad(index - 4, half).start()

            @pl.when(c == 0)
            def _():
                r.last[rows] = below
                if half:
                    hand_out(dx_way, k, r.last[...])

            for i, value in enumerate((total * scaled, total, above)):
                r.nrm[c, i : i + 1] = r.nrm[c, i : i + 1] + jnp.sum(value, axis=0, keepdims=True)
            if half:

                @pl.when(k == 0)
                def _():
                    for hm in (1, 2):

                        @pl.when(h == hm)
                        def _():
                            for side in (0, 1):
                                first = (2 * (hm - 1) + side) * local
                                r.nrm_out[c * 2 + side, :, 0:local] = r.nrm[
                                    c, :, first : first + local
                                ]

                    launch(all_norms(c))

        def send_keys(l, step):
            ring = lax.rem(step, 2) * 4
            return remote(
                r.sums.at[pl.ds(ring, 4), 0:BLOCK],
                r.sums_in.at[pl.ds(step * 4, 4)],
                r.dk_s.at[l * 4 + step],
                r.dk_r.at[l * 4 + step],
                partner,
            )

        def attend_back(l, k):
            step = 3 - k
            ring = lax.rem(step, 2) * 4
            block = 2 * k + d
            start = block * BLOCK
            grad_merged = dot(r.grad[8 * l + k], r.wo[l], NT).astype(BF16)

            @pl.when(step >= 2)
            def _():
                send_keys(l, step - 2).wait_send()

            gate_total = jnp.zeros((256, 128), F32)
            for hh in range(3):
                where = (l * 4 + k) * 3 + hh
                near = pl.ds(pl.multiple_of(start, BLOCK), 192)
                keys = jnp.concatenate([r.kv[l * 4 + hh, near], r.chosen[where]], axis=0)
                mixed = grad_merged[:, hh * 128 : hh * 128 + 128]
                soft = r.soft[where]
                grad_soft = dot(mixed, keys, NT)
                grad_logits = (
                    soft * (grad_soft - jnp.sum(grad_soft * soft, axis=1, keepdims=True))
                ).astype(BF16)
                grad_query = dot(grad_logits, keys) * 0.125
                r.dqkv[k, :, hh * 256 : hh * 256 + 128] = jnp.where(
                    lane < 64, grad_query, 0.0
                ).astype(BF16)
                left = jnp.concatenate([grad_logits, soft.astype(BF16)], axis=0)
                right = jnp.concatenate(
                    [
                        jnp.concatenate([r.q[where], ones_tiles[hh]], axis=1),
                        jnp.concatenate([mixed, jnp.zeros_like(mixed)], axis=1),
                    ],
                    axis=0,
                )
                grad_set = dot(left, right, TN)
                far = grad_set[192:256]
                high = far.astype(BF16)
                r.far[hh, pl.ds(k * 128, 64)] = high
                r.far[hh, pl.ds(k * 128 + 64, 64)] = (far - high.astype(F32)).astype(BF16)
                hots = []
                for kk in range(4):
                    pick_row = r.pk[pl.ds(hh * 8 + 2 * kk + d, 1), :][:, 0:128]
                    hit = rows_of((256, 128)) + (start - BLOCK) == pick_row
                    hots.append((hit & (kk >= k)).astype(F32).astype(BF16))
                total = dot(jnp.concatenate(hots, axis=1), r.far[hh])
                r.sums[ring + hh, 0:WINDOW] = total[0:WINDOW, 0:128]
                r.sums[ring + hh, WINDOW:256] = total[WINDOW:256, 0:128] + grad_set[0:192, 0:128]
                gate_total = gate_total + total[:, 128:256]
            r.sums[ring + 3] = gate_total

            @pl.when(block > 0)
            def _():
                send_keys(l, step).start()

        def finish_back(l, k):
            step = 3 - k
            ring = lax.rem(step, 2) * 4
            came = step - d

            @pl.when(came >= 0)
            def _():
                arrived(r.sums_in.at[pl.ds(came * 4, 4)], r.dk_r.at[l * 4 + came])
                for j in range(4):
                    r.sums[ring + j, BLOCK:256] = (
                        r.sums[ring + j, BLOCK:256] + r.sums_in[came * 4 + j]
                    )

            scores = pieces(r.sums[ring + 3, BLOCK:256] * r.sig[l * 4 + k], lane)
            for hh in range(3):
                head = slice(hh * 256, hh * 256 + 128)
                r.dqkv[k, :, head] = jnp.where(
                    head_lanes(lane, hh), scores, r.dqkv[k, :, head]
                )
                r.dqkv[k, :, hh * 256 + 128 : hh * 256 + 256] = r.sums[
                    ring + hh, BLOCK:256
                ].astype(BF16)
            return dot(r.dqkv[k], r.w1[l])

        def feed_back(l, k, half):
            rows = slice(half * HALF, half * HALF + HALF)
            grad_hidden = dot(r.grad[8 * l + 4 + k, rows], r.pj[l], NT)
            grad_pre = (grad_hidden * r.slope[l * 4 + k, rows].astype(F32)).astype(BF16)
            r.dpre[k, rows] = grad_pre
            return dot(grad_pre, r.fc[l], NT)

        def four(ref, first):
            value = ref[pl.ds(first, 4)]
            return value.reshape(4 * BLOCK, value.shape[2])

        ones_rows = jnp.ones((8, 4 * BLOCK), BF16)

        def split(kind, width):
            for step in (1, 2, 3, 0):
                section = lax.rem(s + step, 4)
                rows = pl.ds(pl.multiple_of((2 * section + 1 - d) * part_rows, 8), part_rows)
                halves[kind][0][section] = wides[kind][rows, 0:width].astype(BF16)
                send_half(kind, section).start()

        def send_half(kind, section):
            return remote(
                halves[kind][0].at[section],
                halves[kind][1].at[section],
                r.xh_s.at[kind, section],
                r.xh_r.at[kind, section],
                partner,
            )

        def send_share(kind, l, step):
            place = l * 3 + step - 1
            return remote(
                shares[kind][0].at[step - 1],
                shares[kind][1].at[place],
                r.yh_s.at[kind, step - 1],
                r.yh_r.at[kind, place],
                at(lax.rem(s + step, 4), h, d),
            )

        def share(kind, width, l):
            for step in (1, 2, 3, 0):
                section = lax.rem(s + step, 4)
                arrived(halves[kind][1].at[section], r.xh_r.at[kind, section])
                send_half(kind, section).wait_send()
                rows = pl.ds(pl.multiple_of((2 * section + d) * part_rows, 8), part_rows)
                both = wides[kind][rows, 0:width] + halves[kind][1][section].astype(F32)
                if step:
                    shares[kind][0][step - 1] = both.astype(BF16)
                    send_share(kind, l, step).start()
                else:
                    wides[kind][rows, 0:width] = both

        def collect(kind, width, l):
            rows = pl.ds(pl.multiple_of((2 * s + d) * part_rows, 8), part_rows)
            total = wides[kind][rows, 0:width]
            for step in (1, 2, 3):
                place = l * 3 + step - 1
                arrived(shares[kind][1].at[place], r.yh_r.at[kind, place])
                total = total + shares[kind][1][place].astype(F32)
                send_share(kind, l, step).wait_send()
            return total

        def weights_feed(l, part):
            left = four(r.normed, 8 * l + 4) if part < 2 else four(r.grad, 8 * l + 4)
            right = four(r.dpre, 0) if part < 2 else four(r.hidden, 4 * l)
            rows = slice(part % 2 * 384, part % 2 * 384 + 384)
            columns = slice(part // 2 * 768, part // 2 * 768 + 768)
            r.wide_f[rows, columns] = dot(left[:, rows], right, TN)
            if part == 0:
                r.sm[2 * l + 1, 0:6] = folded(dot(ones_rows, right)[0:1])
                push_small(2 * l + 1)
            if part == 3:
                split(0, 1536)

        def weights_attend(l, part):
            wide_lane = lanes((4 * BLOCK, 128))
            if part == 0:
                grads = four(r.dqkv, 0)
                t = [grads[:, i * 256 : i * 256 + 128].astype(F32) for i in range(3)]
                first = jnp.where(wide_lane < 64, t[0], pltpu.roll(t[1], 64, 1))
                second = jnp.where(wide_lane < 64, t[2], t[0] + t[1] + t[2])
                r.packed[:, 0:128] = first.astype(BF16)
                r.packed[:, 128:256] = second.astype(BF16)
                for i in range(3):
                    r.packed[:, 256 + 128 * i : 384 + 128 * i] = grads[
                        :, i * 256 + 128 : i * 256 + 256
                    ]
                r.sm[2 * l, 0:6] = folded(dot(ones_rows, grads)[0:1])
            if part < 2:
                rows = slice(part * 384, part * 384 + 384)
                r.wide_a[rows, 0:640] = dot(four(r.normed, 8 * l)[:, rows], r.packed[...], TN)
            if part == 2:
                merged = four(r.merged, 4 * l)
                u = [merged[:, i * 128 : i * 128 + 128].astype(F32) for i in range(3)]
                packed = jnp.concatenate(
                    [
                        jnp.where(wide_lane < 64, pltpu.roll(u[0], 64, 1), u[1]),
                        jnp.where(wide_lane < 64, pltpu.roll(u[2], 64, 1), 0.0),
                    ],
                    axis=1,
                ).astype(BF16)
                r.wide_a[:, 640:896] = dot(four(r.grad, 8 * l), packed, TN)
            if part == 3:
                send_keys(l, 2).wait_send()

                @pl.when(d == 1)
                def _():
                    send_keys(l, 3).wait_send()

                scores = dot(r.packed[:, 128:256], four(r.normed, 8 * l), TN)
                for hh in range(3):
                    row = 64 + 3 * hh
                    r.sm[2 * l, 6 + 6 * hh : 12 + 6 * hh] = folded(
                        scores[row : row + 1] + scores[row + 1 : row + 2] + scores[row + 2 : row + 3]
                    )
                push_small(2 * l)
                split(1, 896)

        def collect_feed(l):
            total = collect(0, 1536, l)
            r.o_fc[l] = total[:, 0:768]
            r.o_pj[l] = total[:, 768:1536]

        def collect_attend(l):
            total = collect(1, 896, l)
            r.o_qkv[3 * l] = total[:, 0:192]
            for i in (0, 1):
                r.o_qkv[3 * l + 1 + i] = jnp.concatenate(
                    [total[:, 256 + 128 * j + 64 * i : 320 + 128 * j + 64 * i] for j in range(3)],
                    axis=1,
                )
            r.o_out[l] = total[:, 640:896].T[0:192]

        def small_sums(c):
            for step in range(1, 8):
                whose = c * 8 + lax.rem(s * 2 + d + step, 8)
                arrived(r.sm_in.at[whose], r.sm_r.at[whose])
            r.sm_in[c * 8 + s * 2 + d] = r.sm[c]
            total = r.sm_in[c * 8]
            for j in range(1, 8):
                total = total + r.sm_in[c * 8 + j]
            l = c // 2
            if c % 2:
                r.o_fcb[l : l + 1, :] = unpacked(total, 0, 6)
            else:
                biases = unpacked(total, 0, 6)
                for i in (0, 1):
                    r.o_qv[l, i : i + 1, :] = jnp.concatenate(
                        [biases[:, j * 256 + 192 * i : j * 256 + 192 * i + 64] for j in range(3)],
                        axis=1,
                    )
                for j in range(3):
                    r.o_score[j, l : l + 1, :] = unpacked(total, 6 + 6 * j, 6)

        def end_sends():
            @pl.when(d == owner)
            def _():
                for copies in stream_parts + cot_parts:
                    sent(copies)

            sent(norm_rows)

            @pl.when((s == 0) & jnp.logical_not(mid))
            def _():
                sent(end_rows)

            def drain_kv(i, carry):
                send_kv(lax.div(i, 4), lax.rem(i, 4)).wait_send()
                return carry

            lax.fori_loop(0, 8, drain_kv, 0)

            @pl.when(d == 0)
            def _():
                wait_kv(0, 3)
                wait_kv(1, 3)

        def end_middle_sends():
            def drain(i, carry):
                for half in (0, 1):
                    pl.when(i >= DIRECT)(send_normed(i, half).wait_send)
                    pl.when((i >= 4) & (i < 12))(send_grad(i, half).wait_send)
                send_cot(i).wait_send()
                return carry

            lax.fori_loop(0, 16, drain, 0)

        def end_small_sends():
            finish_hand(y_way)
            for c in range(1, 4):
                small_sums(c)
                for step in range(1, 8):
                    send_small(c, step).wait_send()

            @pl.when(mid)
            def _():
                for c in range(1, 4):
                    sent(all_norms(c))

        def slot_of(n, carry):
            ahead = n < 16
            c = jnp.where(ahead, lax.div(n, 4), 7 - lax.div(n, 4))
            k = jnp.where(ahead, lax.rem(n, 4), 3 - lax.rem(n, 4))
            l = lax.div(c, 2)
            works = n < 32
            attends = lax.rem(c, 2) == 0

            @pl.when((n < DIRECT) | (mid & (n < 4)))
            def _():
                enter(n)

            pl.when(mid & (n == 2))(prepare_rest)

            @pl.when((n == 0) & (d == owner))
            def _():
                launch(cot_parts[3])

            @pl.when((n == 4) & (d == owner))
            def _():
                launch(cot_parts[2])

            @pl.when((n == 8) & (d == owner))
            def _():
                launch(cot_parts[1])

            @pl.when((n == 12) & (d == owner))
            def _():
                launch(cot_parts[0])

            @pl.when(mid & (n >= 4) & (n < 20))
            def _():
                leave(n - 4, 0)

            @pl.when(mid & (n >= 20))
            def _():
                leave_back(n - 20, 0)

            @pl.when(mid & (n >= 3) & (n < 35))
            def _():
                fold(n - 3, 1)

            @pl.when(mid & (n >= 4) & (n < 20))
            def _():
                leave(n - 4, 1)

            @pl.when(mid & (n >= 3) & (n < 19))
            def _():
                enter_back(n - 3)

            @pl.when(mid & (n >= 20))
            def _():
                leave_back(n - 20, 1)

            def come(half):
                rows = slice(half * HALF, half * HALF + HALF)

                @pl.when(jnp.logical_not(mid) & ahead & (n >= DIRECT))
                def _():
                    arrived(r.normed.at[n, rows], r.nx_r.at[n * 2 + half])

                @pl.when(jnp.logical_not(mid) & (n >= 16) & (n < 20))
                def _():
                    for i in (0, 1):
                        piece = (n - 16) * 4 + half * 2 + i
                        arrived(r.grad.at[c * 4 + k, pl.ds(half * HALF + i * 32, 32)], r.cx_r.at[piece])

                @pl.when(jnp.logical_not(mid) & (n >= 20) & works)
                def _():
                    index = c * 4 + k
                    arrived(r.grad.at[index, rows], r.gx_r.at[index * 2 + half])

            @pl.when(attends)
            def _():
                come(0)
                come(1)

            @pl.when((n == 0) | (n == 8))
            def _():
                for copy in attend_loads[0:12]:
                    pltpu.make_async_copy(copy.src_ref, copy.dst_ref, r.load.at[l]).wait()

            @pl.when(n == 4)
            def _():
                for copy in feed_loads:
                    copy.wait()

            @pl.when(ahead & attends)
            def _():
                project(l, k)

            @pl.when(n == 0)
            def _():
                for copy in pick_copies:
                    copy.wait()
                chosen = r.pk_in[owner, slot]
                r.pk[...] = jnp.concatenate(
                    [chosen, chosen, jnp.zeros((32, 192), jnp.int32), chosen], axis=1
                )
                square = jnp.concatenate([chosen.astype(F32), jnp.zeros((32, 64), F32)], axis=1)
                square = jnp.concatenate([square, jnp.zeros((96, 128), F32)], axis=0)
                r.pt[...] = square.T[0:64]

            @pl.when(ahead & attends)
            def _():
                came = k - 1 + d
                pl.when(came >= 0)(lambda: wait_kv(l, came))
                give_both(n, attend(l, k))

            @pl.when(ahead & jnp.logical_not(attends))
            def _():
                for half in (0, 1):
                    come(half)
                    give(n, half, feed(l, k, half))

            @pl.when(jnp.logical_not(ahead) & works & attends)
            def _():
                attend_back(l, k)
                give_both(n, finish_back(l, k))

            @pl.when(jnp.logical_not(ahead) & works & jnp.logical_not(attends))
            def _():
                for half in (0, 1):
                    come(half)
                    give(n, half, feed_back(l, k, half))

            @pl.when(mid & (n >= 2) & (n < 34))
            def _():
                fold(n - 2, 0)

            feed_l, attend_l = 1 - lax.div(n, 28), 1 - lax.div(n, 31)
            for part in range(4):

                @pl.when((n == FEED_PARTS[0][part]) | (n == FEED_PARTS[1][part]))
                def _():
                    weights_feed(feed_l, part)

                @pl.when((n == ATTEND_PARTS[0][part]) | (n == ATTEND_PARTS[1][part]))
                def _():
                    weights_attend(attend_l, part)

            @pl.when((n == FEED_COLLECT[0]) | (n == FEED_COLLECT[1]))
            def _():
                collect_feed(feed_l)

            @pl.when((n == ATTEND_COLLECT[0]) | (n == ATTEND_COLLECT[1]))
            def _():
                collect_attend(attend_l)

            @pl.when((n == FEED_SHARE[0]) | (n == FEED_SHARE[1]))
            def _():
                share(0, 1536, feed_l)

            @pl.when((n == ATTEND_SHARE[0]) | (n == ATTEND_SHARE[1]))
            def _():
                share(1, 896, attend_l)

            pl.when(n == 32)(end_sends)
            pl.when(mid & (n == 33))(end_middle_sends)
            pl.when(n == 34)(end_small_sends)
            return carry

        lax.fori_loop(0, 36, slot_of, 0)

        small_sums(0)
        for j in range(8):
            arrived(r.nrm_in.at[j], r.nr_r.at[j])
        total = r.nrm_in[0]
        for j in range(1, 8):
            total = total + r.nrm_in[j]
        for i, ref in enumerate((r.o_gain, r.o_bias, r.o_ob)):
            ref[...] = total[i : i + 1, 0:local]

        finish_hand(dx_way)
        for step in range(1, 8):
            send_small(0, step).wait_send()

        @pl.when(mid)
        def _():
            sent(all_norms(0))
            for i in range(4):
                for half in (0, 1):
                    send_grad(i, half).wait_send()
            for n in range(28, 32):
                for half in (0, 1):
                    send_pair(n, half).wait_send()

        @pl.when(jnp.logical_not(mid))
        def _():
            for n in range(28, 32):
                for half in (0, 1):
                    send_part(n, half).wait_send()

    return kernel


def hand_over(*refs):
    count = len(refs) // 3
    loads, stores = [], []
    for i in range(count):
        loads.append(pltpu.make_async_copy(refs[i], refs[2 * count + i], refs[-1].at[0, i]))
        stores.append(
            pltpu.make_async_copy(refs[2 * count + i], refs[count + i], refs[-1].at[1, i])
        )
    for load in loads:
        load.start()
    for load, store in zip(loads, stores):
        load.wait()
        store.start()
    for store in stores:
        store.wait()


def shards(
    stream,
    cotangent,
    lengths,
    picks,
    norm_gain,
    norm_bias,
    out_bias,
    weight_qkv,
    bias_qv,
    weight_score,
    weight_out,
    weight_fc,
    bias_fc,
    weight_proj,
):
    micro, tokens, local = stream.shape
    layers, width = weight_qkv.shape[0], weight_qkv.shape[1]
    inputs = dict(
        stream=stream.transpose(0, 2, 1),
        cot=cotangent.transpose(0, 2, 1),
        lengths=lengths,
        picks=picks.reshape(micro, 24, 64),
        gain=norm_gain,
        shift=norm_bias,
        ob=out_bias,
        wqkv=weight_qkv.transpose(0, 2, 3, 1),
        bqv=bias_qv,
        wscore=weight_score.transpose(2, 0, 1),
        wout=weight_out,
        wfc=weight_fc,
        bfc=bias_fc,
        wpj=weight_proj,
    )
    spaces = dict(
        stream=pl.ANY, cot=pl.ANY, lengths=pltpu.SMEM, wqkv=pl.ANY, wout=pl.ANY, wfc=pl.ANY, wpj=pl.ANY
    )
    part_rows = width // 8
    outputs = dict(
        y=((micro, local, 2 * BLOCK), BF16),
        dx=((micro, local, 2 * BLOCK), BF16),
        o_gain=((1, 192), F32),
        o_bias=((1, 192), F32),
        o_ob=((1, 192), F32),
        o_qkv=((6, part_rows, 192), F32),
        o_qv=((2, 2, 192), F32),
        o_score=((3, 2, 768), F32),
        o_out=((2, 192, part_rows), F32),
        o_fc=((2, part_rows, 768), F32),
        o_fcb=((2, 768), F32),
        o_pj=((2, part_rows, 768), F32),
    )
    dma = pltpu.SemaphoreType.DMA
    scratch = dict(
        stream_in=((4, 768, BLOCK), BF16),
        cot_in=((4, 768, BLOCK), BF16),
        prm=((16, 128), BF16),
        w1=((2, 768, 768), BF16),
        wo=((2, 384, 768), BF16),
        fc=((2, 768, 768), BF16),
        pj=((2, 768, 768), BF16),
        bq=((2, 1, 768), F32),
        fcb=((2, 1, 768), F32),
        prm_in=((4, 4, 16, 128), BF16),
        par=((4, 8, 768), F32),
        last=((BLOCK, 768), BF16),
        pk_out=((micro, 32, 64), jnp.int32),
        pk_in=((2, micro, 32, 64), jnp.int32),
        pk=((32, 384), jnp.int32),
        pt=((64, 128), F32),
        state=((16, BLOCK, 768), BF16),
        normed=((16, BLOCK, 768), BF16),
        q=((24, BLOCK, 128), BF16),
        sig=((8, BLOCK, 128), F32),
        kv=((8, WINDOW + tokens, 128), BF16),
        chosen=((24, 64, 128), BF16),
        keyset=((3, 256, 256), BF16),
        soft=((24, BLOCK, 256), F32),
        merged=((8, BLOCK, 384), BF16),
        hidden=((8, BLOCK, 768), BF16),
        slope=((8, BLOCK, 768), BF16),
        part_out=((4, BLOCK, 768), BF16),
        part_in=((8, BLOCK, 768), BF16),
        own=((4, BLOCK, 768), F32),
        pair_out=((4, BLOCK, 768), BF16),
        pair_in=((8, BLOCK, 768), BF16),
        y_stage=((4, 768, BLOCK), BF16),
        dx_stage=((4, 768, BLOCK), BF16),
        grad=((16, BLOCK, 768), BF16),
        dpre=((4, BLOCK, 768), BF16),
        dqkv=((4, BLOCK, 768), BF16),
        far=((3, 512, 256), BF16),
        sums=((8, 256, 128), F32),
        sums_in=((16, BLOCK, 128), F32),
        wide_f=((768, 1536), F32),
        wide_a=((768, 896), F32),
        packed=((512, 640), BF16),
        xo_f=((4, part_rows, 1536), BF16),
        xi_f=((4, part_rows, 1536), BF16),
        yo_f=((3, part_rows, 1536), BF16),
        yi_f=((6, part_rows, 1536), BF16),
        xo_a=((4, part_rows, 896), BF16),
        xi_a=((4, part_rows, 896), BF16),
        yo_a=((3, part_rows, 896), BF16),
        yi_a=((6, part_rows, 896), BF16),
        nrm=((4, 8, 768), F32),
        nrm_out=((8, 8, 256), F32),
        nrm_in=((8, 8, 256), F32),
        sm=((4, 24, 128), F32),
        sm_in=((32, 24, 128), F32),
    )
    sems = dict(
        xs_s=(8, 4),
        xs_r=(4, 4),
        xc_s=(8, 4),
        xc_r=(4, 4),
        load=(3,),
        prm_s=(4, 2),
        prm_e=(4,),
        prm_r=(4, 4),
        pick_s=(2,),
        pick_r=(1,),
        nx_s=(32,),
        nx_r=(32,),
        kv_s=(8,),
        kv_r=(8,),
        ps_s=(64,),
        ps_r=(64,),
        mm_s=(64,),
        mm_r=(64,),
        y_s=(4, 2),
        y_r=(2, 2),
        dx_s=(4, 2),
        dx_r=(2, 2),
        cx_s=(16,),
        cx_r=(16,),
        gx_s=(32,),
        gx_r=(32,),
        dk_s=(8,),
        dk_r=(8,),
        xh_s=(2, 4),
        xh_r=(2, 4),
        yh_s=(2, 3),
        yh_r=(2, 6),
        sm_s=(32,),
        sm_r=(32,),
        nr_s=(16,),
        nr_r=(8,),
    )
    names = list(inputs) + list(outputs) + list(scratch) + list(sems)
    results = pl.pallas_call(
        make_kernel(names, micro, width // 8, local),
        out_shape=[jax.ShapeDtypeStruct(*spec) for spec in outputs.values()],
        in_specs=[
            pl.BlockSpec(memory_space=spaces.get(name, pltpu.VMEM))
            for name in inputs
        ],
        out_specs=[pl.BlockSpec(memory_space=pltpu.VMEM) for name in outputs],
        scratch_shapes=[pltpu.VMEM(*spec) for spec in scratch.values()]
        + [dma(shape) for shape in sems.values()],
        compiler_params=pltpu.CompilerParams(
            collective_id=0, has_side_effects=True, vmem_limit_bytes=62 * 2**20
        ),
        name="blocks",
    )(*inputs.values())
    results = pl.pallas_call(
        hand_over,
        out_shape=[jax.ShapeDtypeStruct(*spec) for spec in outputs.values()],
        in_specs=[pl.BlockSpec(memory_space=pl.ANY)] * len(outputs),
        out_specs=[pl.BlockSpec(memory_space=pl.ANY)] * len(outputs),
        scratch_shapes=[pltpu.VMEM(*spec) for spec in outputs.values()] + [dma((2, len(outputs)))],
        name="results",
    )(*results)
    o = types.SimpleNamespace(**dict(zip(outputs, results)))
    dp_count = lax.axis_size("dp")
    if dp_count > 2:
        d = lax.rem(lax.axis_index("dp"), 2)

        def scattered(value):
            placed = jnp.zeros((value.shape[0], 2 * part_rows, value.shape[2]), F32)
            placed = lax.dynamic_update_slice(placed, value, (0, d * part_rows, 0))
            return lax.psum_scatter(placed, "dp", scatter_dimension=1, tiled=True)

        o.o_out = scattered(o.o_out.transpose(0, 2, 1)).transpose(0, 2, 1)
        o.o_qkv, o.o_fc, o.o_pj = map(scattered, (o.o_qkv, o.o_fc, o.o_pj))
        sums = (o.o_gain, o.o_bias, o.o_ob, o.o_qv, o.o_score, o.o_fcb)
        o.o_gain, o.o_bias, o.o_ob, o.o_qv, o.o_score, o.o_fcb = jax.tree.map(
            lambda value: 0.5 * value, lax.psum(sums, "dp")
        )
    rows = o.o_fc.shape[1]
    return (
        o.y.transpose(0, 2, 1),
        o.dx.transpose(0, 2, 1),
        o.o_gain,
        o.o_bias,
        o.o_ob,
        o.o_qkv.reshape(layers, 3, rows, 192).transpose(0, 2, 1, 3),
        o.o_qv,
        o.o_score.transpose(1, 2, 0),
        o.o_out,
        o.o_fc,
        o.o_fcb,
        o.o_pj.transpose(0, 2, 1),
    )


def solution(mesh):
    return jax.shard_map(
        shards,
        mesh=mesh,
        in_specs=(
            P("dp", None, "head"),
            P("dp", None, "head"),
            P("dp"),
            P("dp", "head", None, None),
            P("section", None),
            P("section", None),
            P("section", "head"),
            P(None, None, None, "head"),
            P(None, None, "head"),
            P(None, None, "head"),
            P(None, "head", None),
            P(None, None, "head"),
            P(None, "head"),
            P(None, "head", None),
        ),
        out_specs=(
            P("dp", "section", "head"),
            P("dp", "section", "head"),
            P("section", "head"),
            P("section", "head"),
            P("section", "head"),
            P(None, ("section", "dp"), None, "head"),
            P(None, None, "head"),
            P(None, None, "head"),
            P(None, "head", ("section", "dp")),
            P(None, ("section", "dp"), "head"),
            P(None, "head"),
            P(None, "head", ("section", "dp")),
        ),
        check_vma=False,
    )
```

```python
import types

import jax
import jax.numpy as jnp
from jax import lax
from jax.experimental import pallas as pl
from jax.experimental.pallas import tpu as pltpu
from jax.sharding import PartitionSpec as P

MESH = pl.DeviceIdType.MESH
BLOCK = 128
HALF = 64
DIRECT = 1
RELAY = 2
FEED_PARTS = ((20, 20, 21, 21), (28, 28, 28, 28))
ATTEND_PARTS = ((24, 24, 25, 25), (31, 31, 31, 31))
FEED_SHARE, FEED_COLLECT = (22, 29), (26, 34)
ATTEND_SHARE, ATTEND_COLLECT = (26, 32), (30, 35)
WINDOW = 64
NT = (((1,), (1,)), ((), ()))
TN = (((0,), (0,)), ((), ()))
F32 = jnp.float32
BF16 = jnp.bfloat16
ROOT = 0.7978845608028654
CUBE = 0.044715


def dot(left, right, dims=(((1,), (0,)), ((), ()))):
    return lax.dot_general(left, right, dims, preferred_element_type=F32)


def lanes(shape):
    return lax.broadcasted_iota(jnp.int32, shape, len(shape) - 1)


def rows_of(shape):
    return lax.broadcasted_iota(jnp.int32, shape, len(shape) - 2)


def head_lanes(lane, hh):
    return (lane >= 64 + 3 * hh) & (lane < 67 + 3 * hh)


def pieces(value, lane):
    high = value.astype(BF16)
    rest = value - high.astype(F32)
    middle = rest.astype(BF16)
    low = (rest - middle.astype(F32)).astype(BF16)
    zero = jnp.zeros_like(high)
    used = (lane >= 64) & (lane < 73)
    which = lax.rem(lane - 64 + 3 * 64, 3)
    return jnp.where(
        used & (which == 0),
        high,
        jnp.where(used & (which == 1), middle, jnp.where(used & (which == 2), low, zero)),
    )


def make_kernel(names, micro, part_rows, local):
    def kernel(*refs):
        r = types.SimpleNamespace(**dict(zip(names, refs)))
        wides = (r.wide_f, r.wide_a)
        halves = ((r.xo_f, r.xi_f), (r.xo_a, r.xi_a))
        shares = ((r.yo_f, r.yi_f), (r.yo_a, r.yi_a))
        s, h, dp = lax.axis_index("section"), lax.axis_index("head"), lax.axis_index("dp")
        d = lax.rem(dp, 2)
        pair = dp - d
        mid = (h == 1) | (h == 2)
        mate = h + 1 - 2 * lax.rem(h, 2)
        other = 3 - h
        owner = lax.div(s, micro)
        slot = lax.rem(s, micro)

        def at(section, head, core):
            return (section, head, pair + core)

        def remote(src, dst, send, recv, device):
            return pltpu.make_async_remote_copy(
                src_ref=src,
                dst_ref=dst,
                send_sem=send,
                recv_sem=recv,
                device_id=device,
                device_id_type=MESH,
            )

        partner = at(s, h, 1 - d)
        mate_id = at(s, mate, d)
        other_id = at(s, other, d)

        def arrived(dst, recv):
            remote(dst, dst, recv, recv, partner).wait_recv()

        barrier = pltpu.get_barrier_semaphore()
        flat = (s * 4 + h) * 2 + d

        def greet(step, carry):
            whom = lax.rem(flat + step, 32)
            pl.semaphore_signal(
                barrier,
                inc=1,
                device_id=at(lax.div(whom, 8), lax.rem(lax.div(whom, 2), 4), lax.rem(whom, 2)),
                device_id_type=MESH,
            )
            return carry

        lax.fori_loop(1, 32, greet, 0)

        attend_loads, feed_loads = [], []
        for l in range(2):
            for hh in range(3):
                rows = slice(hh * 64, hh * 64 + 64)
                for part, place in ((0, 0), (1, 128), (2, 192)):
                    attend_loads.append(
                        pltpu.make_async_copy(
                            r.wqkv.at[l, part, rows],
                            r.w1.at[l, hh * 256 + place : hh * 256 + place + 64],
                            r.load.at[l],
                        )
                    )
                attend_loads.append(
                    pltpu.make_async_copy(
                        r.wout.at[l, rows],
                        r.wo.at[l, hh * 128 + 64 : hh * 128 + 128],
                        r.load.at[l],
                    )
                )
            feed_loads.append(pltpu.make_async_copy(r.wfc.at[l], r.fc.at[l], r.load.at[2]))
            feed_loads.append(pltpu.make_async_copy(r.wpj.at[l], r.pj.at[l], r.load.at[2]))

        for copy in attend_loads + feed_loads:
            copy.start()

        r.nrm[...] = jnp.zeros_like(r.nrm)
        r.nrm_out[...] = jnp.zeros_like(r.nrm_out)
        r.sm[...] = jnp.zeros_like(r.sm)
        for j in range(micro):
            r.pk_out[j, 0:24] = r.picks[j]
            r.pk_out[j, 24:32] = jnp.zeros((8, 64), jnp.int32) + r.lengths[j]
        short = jnp.concatenate([r.ob[...].astype(F32), jnp.zeros((1, 256 - local), F32)], axis=1)
        r.prm[...] = jnp.concatenate(
            [
                row[:, j * 128 : j * 128 + 128]
                for row, count in ((r.gain[...].astype(F32), 6), (r.shift[...].astype(F32), 6), (short, 2))
                for j in range(count)
            ]
            + [jnp.zeros((2, 128), F32)],
            axis=0,
        ).astype(BF16)

        r.keyset[...] = jnp.zeros_like(r.keyset)
        r.far[...] = jnp.zeros_like(r.far)
        r.kv[:, 0:WINDOW] = jnp.zeros((8, WINDOW, 128), BF16)
        for l in range(2):
            for hh in range(3):
                score = jnp.where(
                    (rows_of((64, 768)) >= 3 * hh) & (rows_of((64, 768)) < 3 * hh + 3),
                    r.wscore[hh, l : l + 1, :].astype(F32),
                    0.0,
                )
                r.w1[l, hh * 256 + 64 : hh * 256 + 128] = score.astype(BF16)
                r.wo[l, hh * 128 : hh * 128 + 64] = jnp.zeros((64, 768), BF16)
            gap = jnp.zeros((1, 128), F32)
            r.fcb[l] = r.bfc[l : l + 1, :].astype(F32)
            bias = r.bqv[l].astype(F32)
            r.bq[l] = jnp.concatenate(
                [
                    piece
                    for hh in range(3)
                    for piece in (
                        bias[0:1, hh * 64 : hh * 64 + 64],
                        gap,
                        bias[1:2, hh * 64 : hh * 64 + 64],
                    )
                ],
                axis=1,
            )

        pl.semaphore_wait(barrier, 31)

        def spread(source, landing, sends, recvs, k, heads):
            copies = []
            for hm in heads:
                for core in (0, 1):
                    src = source.at[slot, :, (2 * k + core) * BLOCK : (2 * k + core + 1) * BLOCK]
                    dst = landing.at[k, pl.ds(pl.multiple_of(h * local, local), local)]
                    recv = recvs.at[h, k]
                    copies.append(
                        (
                            (h == hm) & (d == core),
                            pltpu.make_async_copy(src, dst, recv),
                            remote(
                                src, dst, sends.at[hm * 2 + core, k], recv, at(s, hm, core)
                            ),
                        )
                    )
            return copies

        def launch(copies):
            for own, local, far in copies:
                pl.when(own)(local.start)
                pl.when(jnp.logical_not(own))(far.start)

        def sent(copies):
            for own, local, far in copies:
                pl.when(jnp.logical_not(own))(far.wait_send)

        chunks = 4
        stream_parts = [
            spread(r.stream, r.stream_in, r.xs_s, r.xs_r, k, (1, 2, 0, 3)[: 4 if k < DIRECT else 2])
            for k in range(chunks)
        ]
        nearest = 1 + lax.div(h, 2)

        def spread_cot(k):
            copies = []
            for core in (0, 1):
                src = r.cot.at[slot, :, (2 * k + core) * BLOCK : (2 * k + core + 1) * BLOCK]
                dst = r.cot_in.at[k, pl.ds(pl.multiple_of(h * local, local), local)]
                recv = r.xc_r.at[h, k]
                copies.append(
                    (
                        (h == nearest) & (d == core),
                        pltpu.make_async_copy(src, dst, recv),
                        remote(src, dst, r.xc_s.at[core, k], recv, at(s, nearest, core)),
                    )
                )
            return copies

        cot_parts = [spread_cot(k) for k in range(chunks)]

        def send_relay(k):
            rows = pl.ds(pl.multiple_of((h - 1) * 2 * local, 2 * local), 2 * local)
            half = r.cot_in.at[k, rows]
            return remote(half, half, r.cr_s.at[k], r.cr_r.at[k], other_id)

        norm_rows = []
        for step in range(4):
            section = lax.rem(s + step, 4)
            for hm in (1, 2):
                norm_rows.append(
                    (
                        (h == hm) if step == 0 else (h == 4),
                        pltpu.make_async_copy(
                            r.prm, r.prm_in.at[s, h], r.prm_r.at[s, h]
                        ),
                        remote(
                            r.prm,
                            r.prm_in.at[s, h],
                            r.prm_s.at[step, hm - 1],
                            r.prm_r.at[s, h],
                            at(section, hm, d),
                        ),
                    )
                )
        end_rows = [
            (
                s == step,
                pltpu.make_async_copy(r.prm, r.prm_in.at[0, h], r.prm_r.at[0, h]),
                remote(
                    r.prm, r.prm_in.at[0, h], r.prm_e.at[step], r.prm_r.at[0, h], at(step, h, d)
                ),
            )
            for step in range(4)
        ]
        pick_copies = (
            pltpu.make_async_copy(r.pk_out, r.pk_in.at[d], r.pick_s.at[0]),
            remote(r.pk_out, r.pk_in.at[d], r.pick_s.at[1], r.pick_r.at[0], partner),
        )

        launch(norm_rows)

        @pl.when((s == 0) & jnp.logical_not(mid))
        def _():
            launch(end_rows)

        @pl.when(d == owner)
        def _():
            for copies in stream_parts:
                launch(copies)

        for copy in pick_copies:
            copy.start()

        lane = lanes((BLOCK, 128))
        ones_tiles = [jnp.where(head_lanes(lane, hh), 1.0, 0.0).astype(BF16) for hh in range(3)]

        def norm_parts(x):
            center = x - jnp.mean(x, axis=-1, keepdims=True)
            inverse = lax.rsqrt(jnp.mean(center * center, axis=-1, keepdims=True) + 1e-05)
            return center * inverse, inverse

        def unpacked(tile, first, count):
            return jnp.concatenate([tile[first + j : first + j + 1] for j in range(count)], axis=1)

        def prepare():
            arrived(r.prm_in.at[0, h], r.prm_r.at[0, h])
            tile = r.prm_in[0, h].astype(F32)
            r.par[0, 0:1] = unpacked(tile, 0, 6)
            r.par[0, 1:2] = unpacked(tile, 6, 6)

        def prepare_rest():
            for c in range(4):
                for j in range(4):
                    pl.when(jnp.logical_not((c == 0) & (h == j)))(
                        lambda: arrived(r.prm_in.at[c, j], r.prm_r.at[c, j])
                    )
            for c in range(4):
                if c:
                    tile = r.prm_in[c, h].astype(F32)
                    r.par[c, 0:1] = unpacked(tile, 0, 6)
                    r.par[c, 1:2] = unpacked(tile, 6, 6)
                r.par[c, 2:3] = jnp.concatenate(
                    [unpacked(r.prm_in[c, j].astype(F32), 12, 2)[:, 0:local] for j in range(4)],
                    axis=1,
                )

        def publish(c, k, half, state):
            rows = slice(half * HALF, half * HALF + HALF)
            r.state[c * 4 + k, rows] = state
            scaled, _ = norm_parts(state.astype(F32))
            normed = scaled * r.par[c, 0:1] + r.par[c, 1:2]
            r.normed[c * 4 + k, rows] = normed.astype(BF16)
            send_normed(c * 4 + k, half).start()

        def send_normed(n, half):
            rows = r.normed.at[n, half * HALF : half * HALF + HALF]
            return remote(rows, rows, r.nx_s.at[n * 2 + half], r.nx_r.at[n * 2 + half], mate_id)

        def turned(landing, recvs, k):
            for j in range(4):
                arrived(landing.at[k, j * local : j * local + local], recvs.at[j, k])
            return landing[k].astype(F32).T.astype(BF16)

        def enter(k):
            @pl.when(k == 0)
            def _():
                prepare()

            state = turned(r.stream_in, r.xs_r, k)
            r.state[k] = state
            scaled, _ = norm_parts(state.astype(F32))
            r.normed[k] = (scaled * r.par[0, 0:1] + r.par[0, 1:2]).astype(BF16)

            @pl.when(k >= DIRECT)
            def _():
                for half in (0, 1):
                    send_normed(k, half).start()

        def project(l, k):
            x = r.normed[8 * l + k]
            block = 2 * k + d
            place = pl.ds(pl.multiple_of(WINDOW + block * BLOCK, WINDOW), BLOCK)
            score = jnp.zeros((BLOCK, 128), F32)
            for hh in range(3):
                out = dot(x, r.w1[l, hh * 256 : hh * 256 + 256, :], NT)
                out = out + r.bq[l, :, hh * 256 : hh * 256 + 256]
                q, kv = out[:, :128], out[:, 128:]
                r.q[(l * 4 + k) * 3 + hh] = jnp.where(lane < 64, q, 0.0).astype(
                    BF16
                ) * jnp.asarray(0.125, BF16)
                score = score + jnp.where(head_lanes(lane, hh), q, 0.0)
                r.kv[l * 4 + hh, place] = kv.astype(BF16)
            gates = jnp.minimum(score, 0.0) - jnp.log1p(jnp.exp(-jnp.abs(score)))
            r.sig[l * 4 + k] = 1.0 / (1.0 + jnp.exp(score))
            r.kv[l * 4 + 3, place] = pieces(gates, lane)
            send_kv(l, k).start()

        def send_kv(l, k):
            place = pl.ds(pl.multiple_of(WINDOW + (2 * k + d) * BLOCK, WINDOW), BLOCK)
            rows = r.kv.at[pl.ds(l * 4, 4), place]
            return remote(rows, rows, r.kv_s.at[l * 4 + k], r.kv_r.at[l * 4 + k], partner)

        def wait_kv(l, k):
            place = pl.ds(pl.multiple_of(WINDOW + (2 * k + 1 - d) * BLOCK, WINDOW), BLOCK)
            arrived(r.kv.at[pl.ds(l * 4, 4), place], r.kv_r.at[l * 4 + k])

        def attend(l, k):
            block = 2 * k + d
            start = block * BLOCK
            length = r.pk[24:25, 0:1]
            column = lanes((BLOCK, 256))
            row = rows_of((BLOCK, 256))
            distance = row + WINDOW - column
            near_pos = start - WINDOW + column
            near_ok = (
                (column < 192)
                & (near_pos >= 0)
                & (distance >= 0)
                & (distance < WINDOW)
                & ((near_pos < length) | (distance == 0))
            )
            pick_cols = [
                jnp.sum(
                    jnp.where(lanes((64, 128)) == hh * 8 + block, r.pt[...], 0.0),
                    axis=1,
                    keepdims=True,
                ).astype(jnp.int32)
                for hh in range(3)
            ]

            def some(first, count):
                rows = pl.ds(pl.multiple_of(WINDOW + first, WINDOW), count)
                place = lanes((64, count)) + first
                gates = r.kv[l * 4 + 3, rows]
                return tuple(
                    dot(
                        (place == pick_cols[hh]).astype(F32).astype(BF16),
                        jnp.concatenate([r.kv[l * 4 + hh, rows], gates], axis=1),
                    )
                    for hh in range(3)
                )

            def adding(totals, more):
                return tuple(total + one for total, one in zip(totals, more))

            totals = some(pl.multiple_of(k * 256, 256), BLOCK)
            totals = lax.fori_loop(0, k, lambda j, t: adding(t, some(j * 256, 256)), totals)
            totals = lax.fori_loop(0, d, lambda j, t: adding(t, some(start, BLOCK)), totals)
            near = pl.ds(pl.multiple_of(start, BLOCK), 192)
            for hh in range(3):
                index = hh * 8 + block
                chosen = totals[hh].astype(BF16)
                where = (l * 4 + k) * 3 + hh
                r.chosen[where] = chosen[:, 0:128]
                r.keyset[hh, 0:192, 0:128] = r.kv[l * 4 + hh, near]
                r.keyset[hh, 192:256, :] = chosen
                query = jnp.concatenate([r.q[where], ones_tiles[hh]], axis=1)
                logits = dot(query, r.keyset[hh], NT)
                pick_row = r.pk[pl.ds(index, 1), :][:, 128:384]
                far_ok = (
                    (column >= 192) & (pick_row <= start - WINDOW + row) & (pick_row < length)
                )
                masked = jnp.where(near_ok | far_ok, logits, -1e30)
                raised = jnp.exp(masked - jnp.max(masked, axis=1, keepdims=True))
                soft = raised / jnp.sum(raised, axis=1, keepdims=True)
                r.soft[where] = soft
                mixed = dot(soft.astype(BF16), r.keyset[hh, :, 0:128])
                r.merged[l * 4 + k, :, hh * 128 : hh * 128 + 128] = mixed.astype(BF16)
            return dot(r.merged[l * 4 + k], r.wo[l])

        def feed(l, k, half):
            rows = slice(half * HALF, half * HALF + HALF)
            pre = dot(r.normed[8 * l + 4 + k, rows], r.fc[l]) + r.fcb[l]
            square = pre * pre
            wave = jnp.tanh(ROOT * pre * (1.0 + CUBE * square))
            both = 0.5 * (1.0 + wave)
            slope = both + 0.5 * pre * (1.0 - wave * wave) * (ROOT * (1.0 + 3.0 * CUBE * square))
            hidden = (pre * both).astype(BF16)
            r.hidden[l * 4 + k, rows] = hidden
            r.slope[l * 4 + k, rows] = slope.astype(BF16)
            return dot(hidden, r.pj[l])

        def send_part(n, half):
            rows = pl.ds(half * HALF, HALF)
            return remote(
                r.part_out.at[lax.rem(n, 4), rows],
                r.part_in.at[lax.rem(n, 8), rows],
                r.ps_s.at[n * 2 + half],
                r.ps_r.at[n * 2 + half],
                mate_id,
            )

        def give(n, half, part):
            rows = slice(half * HALF, half * HALF + HALF)

            @pl.when(mid)
            def _():
                r.own[lax.rem(n, 4), rows] = part

            @pl.when(jnp.logical_not(mid))
            def _():
                @pl.when(n >= 4)
                def _():
                    send_part(n - 4, half).wait_send()

                r.part_out[lax.rem(n, 4), rows] = part.astype(BF16)
                send_part(n, half).start()

        def give_both(n, part):
            for half in (0, 1):
                give(n, half, part[half * HALF : half * HALF + HALF])

        def send_pair(n, half):
            rows = pl.ds(half * HALF, HALF)
            return remote(
                r.pair_out.at[lax.rem(n, 4), rows],
                r.pair_in.at[lax.rem(n, 8), rows],
                r.mm_s.at[n * 2 + half],
                r.mm_r.at[n * 2 + half],
                other_id,
            )

        def fold(n, half):
            rows = slice(half * HALF, half * HALF + HALF)
            arrived(r.part_in.at[lax.rem(n, 8), rows], r.ps_r.at[n * 2 + half])

            @pl.when(n >= 4)
            def _():
                send_pair(n - 4, half).wait_send()

            both = r.own[lax.rem(n, 4), rows] + r.part_in[lax.rem(n, 8), rows].astype(F32)
            r.pair_out[lax.rem(n, 4), rows] = both.astype(BF16)
            send_pair(n, half).start()

        def total_of(n, half):
            rows = slice(half * HALF, half * HALF + HALF)
            arrived(r.pair_in.at[lax.rem(n, 8), rows], r.mm_r.at[n * 2 + half])
            return r.pair_out[lax.rem(n, 4), rows].astype(F32) + r.pair_in[
                lax.rem(n, 8), rows
            ].astype(F32)

        y_way = (r.y, r.y_stage, r.y_s, r.y_r)
        dx_way = (r.dx, r.dx_stage, r.dx_s, r.dx_r)

        def hand_out(way, k, value):
            way[1][k] = value.astype(F32).T.astype(BF16)
            for side in (0, 1):
                target = 2 * (h - 1) + side
                own = (k == s) & (target == h) & (d == owner)
                local, far = hand_copy(way, k, side)
                pl.when(own)(local.start)
                pl.when(jnp.logical_not(own))(far.start)

        def hand_copy(way, k, side):
            src = way[1].at[k, pl.ds(pl.multiple_of((2 * (h - 1) + side) * local, local), local)]
            dst = way[0].at[slot, :, pl.ds(pl.multiple_of(d * BLOCK, BLOCK), BLOCK)]
            recv = way[3].at[slot, d]
            return (
                pltpu.make_async_copy(src, dst, recv),
                remote(
                    src, dst, way[2].at[k, side], recv, at(k, 2 * (h - 1) + side, owner)
                ),
            )

        def finish_hand(way):
            @pl.when(mid)
            def _():
                for k in range(chunks):
                    for side in (0, 1):
                        own = (k == s) & (2 * (h - 1) + side == h) & (d == owner)
                        pl.when(jnp.logical_not(own))(hand_copy(way, k, side)[1].wait_send)

            for j in range(micro):
                for core in (0, 1):
                    arrived(
                        way[0].at[j, :, core * BLOCK : core * BLOCK + BLOCK],
                        way[3].at[j, core],
                    )

        def leave(n, half):
            c, k = lax.div(n, 4), lax.rem(n, 4)
            rows = slice(half * HALF, half * HALF + HALF)
            state = r.state[n, rows].astype(F32) + total_of(n, half) + r.par[c, 2:3]
            state = state.astype(BF16)

            @pl.when(c < 3)
            def _():
                publish(c + 1, k, half, state)

            @pl.when(c == 3)
            def _():
                r.last[rows] = state
                if half:
                    hand_out(y_way, k, r.last[...])

        def send_grad(index, half):
            rows = r.grad.at[index, half * HALF : half * HALF + HALF]
            return remote(
                rows, rows, r.gx_s.at[index * 2 + half], r.gx_r.at[index * 2 + half], mate_id
            )

        def send_cot(i):
            rows = r.grad.at[
                15 - lax.div(i, 4), pl.ds(pl.multiple_of(lax.rem(i, 4) * 32, 32), 32)
            ]
            return remote(rows, rows, r.cx_s.at[i], r.cx_r.at[i], mate_id)

        def relay(k):
            for j in (0, 1):
                whose = 2 * (h - 1) + j
                rows = pl.ds(pl.multiple_of(whose * local, local), local)
                arrived(r.cot_in.at[k, rows], r.xc_r.at[whose, k])
            send_relay(k).start()

        def enter_back(i):
            @pl.when(lax.rem(i, 4) == 0)
            def _():
                k = 3 - lax.div(i, 4)
                rows = pl.ds(pl.multiple_of((2 - h) * 2 * local, 2 * local), 2 * local)
                arrived(r.cot_in.at[k, rows], r.cr_r.at[k])
                r.grad[12 + k] = r.cot_in[k].astype(F32).T.astype(BF16)

            send_cot(i).start()

        def send_norms(c, side, core):
            target = 2 * (h - 1) + side
            recv = r.nr_r.at[s * 2 + d]
            src = r.nrm_out.at[c * 2 + side]
            return (
                (c == s) & (target == h) & (d == core),
                pltpu.make_async_copy(src, r.nrm_in.at[s * 2 + d], recv),
                remote(
                    src,
                    r.nrm_in.at[s * 2 + d],
                    r.nr_s.at[c * 4 + side * 2 + core],
                    recv,
                    at(c, target, core),
                ),
            )

        def all_norms(c):
            return [send_norms(c, side, core) for side in (0, 1) for core in (0, 1)]

        def send_small(c, step):
            whom = lax.rem(s * 2 + d + step, 8)
            return remote(
                r.sm.at[c],
                r.sm_in.at[c * 8 + s * 2 + d],
                r.sm_s.at[c * 8 + step],
                r.sm_r.at[c * 8 + s * 2 + d],
                at(lax.div(whom, 2), h, lax.rem(whom, 2)),
            )

        def folded(row):
            return jnp.concatenate([row[:, j * 128 : j * 128 + 128] for j in range(6)], axis=0)

        def push_small(c):
            for step in range(1, 8):
                send_small(c, step).start()

        def leave_back(m, half):
            c, k = 3 - lax.div(m, 4), 3 - lax.rem(m, 4)
            index = c * 4 + k
            rows = slice(half * HALF, half * HALF + HALF)
            total = total_of(16 + m, half)
            scaled, inverse = norm_parts(r.state[index, rows].astype(F32))
            above = r.grad[index, rows].astype(F32)
            t = total * r.par[c, 0:1]
            inner = (
                t
                - jnp.mean(t, axis=-1, keepdims=True)
                - scaled * jnp.mean(t * scaled, axis=-1, keepdims=True)
            )
            below = (above + inverse * inner).astype(BF16)

            @pl.when(c > 0)
            def _():
                r.grad[index - 4, rows] = below
                send_grad(index - 4, half).start()

            @pl.when(c == 0)
            def _():
                r.last[rows] = below
                if half:
                    hand_out(dx_way, k, r.last[...])

            for i, value in enumerate((total * scaled, total, above)):
                r.nrm[c, i : i + 1] = r.nrm[c, i : i + 1] + jnp.sum(value, axis=0, keepdims=True)
            if half:

                @pl.when(k == 0)
                def _():
                    for hm in (1, 2):

                        @pl.when(h == hm)
                        def _():
                            for side in (0, 1):
                                first = (2 * (hm - 1) + side) * local
                                r.nrm_out[c * 2 + side, :, 0:local] = r.nrm[
                                    c, :, first : first + local
                                ]

                    launch(all_norms(c))

        def send_keys(l, step):
            ring = lax.rem(step, 2) * 4
            return remote(
                r.sums.at[pl.ds(ring, 4), 0:BLOCK],
                r.sums_in.at[pl.ds(step * 4, 4)],
                r.dk_s.at[l * 4 + step],
                r.dk_r.at[l * 4 + step],
                partner,
            )

        def attend_back(l, k):
            step = 3 - k
            ring = lax.rem(step, 2) * 4
            block = 2 * k + d
            start = block * BLOCK
            grad_merged = dot(r.grad[8 * l + k], r.wo[l], NT).astype(BF16)

            @pl.when(step >= 2)
            def _():
                send_keys(l, step - 2).wait_send()

            gate_total = jnp.zeros((256, 128), F32)
            for hh in range(3):
                where = (l * 4 + k) * 3 + hh
                near = pl.ds(pl.multiple_of(start, BLOCK), 192)
                keys = jnp.concatenate([r.kv[l * 4 + hh, near], r.chosen[where]], axis=0)
                mixed = grad_merged[:, hh * 128 : hh * 128 + 128]
                soft = r.soft[where]
                grad_soft = dot(mixed, keys, NT)
                grad_logits = (
                    soft * (grad_soft - jnp.sum(grad_soft * soft, axis=1, keepdims=True))
                ).astype(BF16)
                grad_query = dot(grad_logits, keys) * 0.125
                r.dqkv[k, :, hh * 256 : hh * 256 + 128] = jnp.where(
                    lane < 64, grad_query, 0.0
                ).astype(BF16)
                left = jnp.concatenate([grad_logits, soft.astype(BF16)], axis=0)
                right = jnp.concatenate(
                    [
                        jnp.concatenate([r.q[where], ones_tiles[hh]], axis=1),
                        jnp.concatenate([mixed, jnp.zeros_like(mixed)], axis=1),
                    ],
                    axis=0,
                )
                grad_set = dot(left, right, TN)
                far = grad_set[192:256]
                high = far.astype(BF16)
                r.far[hh, pl.ds(k * 128, 64)] = high
                r.far[hh, pl.ds(k * 128 + 64, 64)] = (far - high.astype(F32)).astype(BF16)
                hots = []
                for kk in range(4):
                    pick_row = r.pk[pl.ds(hh * 8 + 2 * kk + d, 1), :][:, 0:128]
                    hit = rows_of((256, 128)) + (start - BLOCK) == pick_row
                    hots.append((hit & (kk >= k)).astype(F32).astype(BF16))
                total = dot(jnp.concatenate(hots, axis=1), r.far[hh])
                r.sums[ring + hh, 0:WINDOW] = total[0:WINDOW, 0:128]
                r.sums[ring + hh, WINDOW:256] = total[WINDOW:256, 0:128] + grad_set[0:192, 0:128]
                gate_total = gate_total + total[:, 128:256]
            r.sums[ring + 3] = gate_total

            @pl.when(block > 0)
            def _():
                send_keys(l, step).start()

        def finish_back(l, k):
            step = 3 - k
            ring = lax.rem(step, 2) * 4
            came = step - d

            @pl.when(came >= 0)
            def _():
                arrived(r.sums_in.at[pl.ds(came * 4, 4)], r.dk_r.at[l * 4 + came])
                for j in range(4):
                    r.sums[ring + j, BLOCK:256] = (
                        r.sums[ring + j, BLOCK:256] + r.sums_in[came * 4 + j]
                    )

            scores = pieces(r.sums[ring + 3, BLOCK:256] * r.sig[l * 4 + k], lane)
            for hh in range(3):
                head = slice(hh * 256, hh * 256 + 128)
                r.dqkv[k, :, head] = jnp.where(
                    head_lanes(lane, hh), scores, r.dqkv[k, :, head]
                )
                r.dqkv[k, :, hh * 256 + 128 : hh * 256 + 256] = r.sums[
                    ring + hh, BLOCK:256
                ].astype(BF16)
            return dot(r.dqkv[k], r.w1[l])

        def feed_back(l, k, half):
            rows = slice(half * HALF, half * HALF + HALF)
            grad_hidden = dot(r.grad[8 * l + 4 + k, rows], r.pj[l], NT)
            grad_pre = (grad_hidden * r.slope[l * 4 + k, rows].astype(F32)).astype(BF16)
            r.dpre[k, rows] = grad_pre
            return dot(grad_pre, r.fc[l], NT)

        def four(ref, first):
            value = ref[pl.ds(first, 4)]
            return value.reshape(4 * BLOCK, value.shape[2])

        ones_rows = jnp.ones((8, 4 * BLOCK), BF16)

        def split(kind, width):
            for step in (1, 2, 3, 0):
                section = lax.rem(s + step, 4)
                rows = pl.ds(pl.multiple_of((2 * section + 1 - d) * part_rows, 8), part_rows)
                halves[kind][0][section] = wides[kind][rows, 0:width].astype(BF16)
                send_half(kind, section).start()

        def send_half(kind, section):
            return remote(
                halves[kind][0].at[section],
                halves[kind][1].at[section],
                r.xh_s.at[kind, section],
                r.xh_r.at[kind, section],
                partner,
            )

        def send_share(kind, l, step):
            place = l * 3 + step - 1
            return remote(
                shares[kind][0].at[step - 1],
                shares[kind][1].at[place],
                r.yh_s.at[kind, step - 1],
                r.yh_r.at[kind, place],
                at(lax.rem(s + step, 4), h, d),
            )

        def share(kind, width, l):
            for step in (1, 2, 3, 0):
                section = lax.rem(s + step, 4)
                arrived(halves[kind][1].at[section], r.xh_r.at[kind, section])
                send_half(kind, section).wait_send()
                rows = pl.ds(pl.multiple_of((2 * section + d) * part_rows, 8), part_rows)
                both = wides[kind][rows, 0:width] + halves[kind][1][section].astype(F32)
                if step:
                    shares[kind][0][step - 1] = both.astype(BF16)
                    send_share(kind, l, step).start()
                else:
                    wides[kind][rows, 0:width] = both

        def collect(kind, width, l):
            rows = pl.ds(pl.multiple_of((2 * s + d) * part_rows, 8), part_rows)
            total = wides[kind][rows, 0:width]
            for step in (1, 2, 3):
                place = l * 3 + step - 1
                arrived(shares[kind][1].at[place], r.yh_r.at[kind, place])
                total = total + shares[kind][1][place].astype(F32)
                send_share(kind, l, step).wait_send()
            return total

        def weights_feed(l, part):
            left = four(r.normed, 8 * l + 4) if part < 2 else four(r.grad, 8 * l + 4)
            right = four(r.dpre, 0) if part < 2 else four(r.hidden, 4 * l)
            rows = slice(part % 2 * 384, part % 2 * 384 + 384)
            columns = slice(part // 2 * 768, part // 2 * 768 + 768)
            r.wide_f[rows, columns] = dot(left[:, rows], right, TN)
            if part == 0:
                r.sm[2 * l + 1, 0:6] = folded(dot(ones_rows, right)[0:1])
                push_small(2 * l + 1)
            if part == 3:
                split(0, 1536)

        def weights_attend(l, part):
            wide_lane = lanes((4 * BLOCK, 128))
            if part == 0:
                grads = four(r.dqkv, 0)
                t = [grads[:, i * 256 : i * 256 + 128].astype(F32) for i in range(3)]
                first = jnp.where(wide_lane < 64, t[0], pltpu.roll(t[1], 64, 1))
                second = jnp.where(wide_lane < 64, t[2], t[0] + t[1] + t[2])
                r.packed[:, 0:128] = first.astype(BF16)
                r.packed[:, 128:256] = second.astype(BF16)
                for i in range(3):
                    r.packed[:, 256 + 128 * i : 384 + 128 * i] = grads[
                        :, i * 256 + 128 : i * 256 + 256
                    ]
                r.sm[2 * l, 0:6] = folded(dot(ones_rows, grads)[0:1])
            if part < 2:
                rows = slice(part * 384, part * 384 + 384)
                r.wide_a[rows, 0:640] = dot(four(r.normed, 8 * l)[:, rows], r.packed[...], TN)
            if part == 2:
                merged = four(r.merged, 4 * l)
                u = [merged[:, i * 128 : i * 128 + 128].astype(F32) for i in range(3)]
                packed = jnp.concatenate(
                    [
                        jnp.where(wide_lane < 64, pltpu.roll(u[0], 64, 1), u[1]),
                        jnp.where(wide_lane < 64, pltpu.roll(u[2], 64, 1), 0.0),
                    ],
                    axis=1,
                ).astype(BF16)
                r.wide_a[:, 640:896] = dot(four(r.grad, 8 * l), packed, TN)
            if part == 3:
                send_keys(l, 2).wait_send()

                @pl.when(d == 1)
                def _():
                    send_keys(l, 3).wait_send()

                scores = dot(r.packed[:, 128:256], four(r.normed, 8 * l), TN)
                for hh in range(3):
                    row = 64 + 3 * hh
                    r.sm[2 * l, 6 + 6 * hh : 12 + 6 * hh] = folded(
                        scores[row : row + 1] + scores[row + 1 : row + 2] + scores[row + 2 : row + 3]
                    )
                push_small(2 * l)
                split(1, 896)

        def collect_feed(l):
            total = collect(0, 1536, l)
            r.o_fc[l] = total[:, 0:768]
            r.o_pj[l] = total[:, 768:1536]

        def collect_attend(l):
            total = collect(1, 896, l)
            r.o_qkv[3 * l] = total[:, 0:192]
            for i in (0, 1):
                r.o_qkv[3 * l + 1 + i] = jnp.concatenate(
                    [total[:, 256 + 128 * j + 64 * i : 320 + 128 * j + 64 * i] for j in range(3)],
                    axis=1,
                )
            r.o_out[l] = total[:, 640:896].T[0:192]

        def small_sums(c):
            for step in range(1, 8):
                whose = c * 8 + lax.rem(s * 2 + d + step, 8)
                arrived(r.sm_in.at[whose], r.sm_r.at[whose])
            r.sm_in[c * 8 + s * 2 + d] = r.sm[c]
            total = r.sm_in[c * 8]
            for j in range(1, 8):
                total = total + r.sm_in[c * 8 + j]
            l = c // 2
            if c % 2:
                r.o_fcb[l : l + 1, :] = unpacked(total, 0, 6)
            else:
                biases = unpacked(total, 0, 6)
                for i in (0, 1):
                    r.o_qv[l, i : i + 1, :] = jnp.concatenate(
                        [biases[:, j * 256 + 192 * i : j * 256 + 192 * i + 64] for j in range(3)],
                        axis=1,
                    )
                for j in range(3):
                    r.o_score[j, l : l + 1, :] = unpacked(total, 6 + 6 * j, 6)

        def end_sends():
            @pl.when(d == owner)
            def _():
                for copies in stream_parts + cot_parts:
                    sent(copies)

            sent(norm_rows)

            @pl.when((s == 0) & jnp.logical_not(mid))
            def _():
                sent(end_rows)

            def drain_kv(i, carry):
                send_kv(lax.div(i, 4), lax.rem(i, 4)).wait_send()
                return carry

            lax.fori_loop(0, 8, drain_kv, 0)

            @pl.when(d == 0)
            def _():
                wait_kv(0, 3)
                wait_kv(1, 3)

        def end_middle_sends():
            def drain(i, carry):
                for half in (0, 1):
                    pl.when(i >= DIRECT)(send_normed(i, half).wait_send)
                    pl.when((i >= 4) & (i < 12))(send_grad(i, half).wait_send)
                send_cot(i).wait_send()
                pl.when(i < 4)(lambda: send_relay(i).wait_send())
                return carry

            lax.fori_loop(0, 16, drain, 0)

        def end_small_sends():
            finish_hand(y_way)
            for c in range(1, 4):
                small_sums(c)
                for step in range(1, 8):
                    send_small(c, step).wait_send()

            @pl.when(mid)
            def _():
                for c in range(1, 4):
                    sent(all_norms(c))

        def slot_of(n, carry):
            ahead = n < 16
            c = jnp.where(ahead, lax.div(n, 4), 7 - lax.div(n, 4))
            k = jnp.where(ahead, lax.rem(n, 4), 3 - lax.rem(n, 4))
            l = lax.div(c, 2)
            works = n < 32
            attends = lax.rem(c, 2) == 0

            @pl.when((n < DIRECT) | (mid & (n < 4)))
            def _():
                enter(n)

            pl.when(mid & (n == 2))(prepare_rest)

            @pl.when((n == 0) & (d == owner))
            def _():
                launch(cot_parts[3])

            @pl.when((n == 1) & (d == owner))
            def _():
                launch(cot_parts[2])

            @pl.when((n == 5) & (d == owner))
            def _():
                launch(cot_parts[1])

            @pl.when((n == 9) & (d == owner))
            def _():
                launch(cot_parts[0])

            @pl.when(mid & (n >= 4) & (n < 20))
            def _():
                leave(n - 4, 0)

            @pl.when(mid & (n >= 20))
            def _():
                leave_back(n - 20, 0)

            @pl.when(mid & (n >= 3) & (n < 35))
            def _():
                fold(n - 3, 1)

            @pl.when(mid & (n >= 4) & (n < 20))
            def _():
                leave(n - 4, 1)

            @pl.when(mid & (n >= 3) & (n < 19))
            def _():
                enter_back(n - 3)

            @pl.when(mid & (n < 16) & (lax.rem(n, 4) == RELAY))
            def _():
                relay(3 - lax.div(n, 4))

            @pl.when(mid & (n >= 20))
            def _():
                leave_back(n - 20, 1)

            def come(half):
                rows = slice(half * HALF, half * HALF + HALF)

                @pl.when(jnp.logical_not(mid) & ahead & (n >= DIRECT))
                def _():
                    arrived(r.normed.at[n, rows], r.nx_r.at[n * 2 + half])

                @pl.when(jnp.logical_not(mid) & (n >= 16) & (n < 20))
                def _():
                    for i in (0, 1):
                        piece = (n - 16) * 4 + half * 2 + i
                        arrived(r.grad.at[c * 4 + k, pl.ds(half * HALF + i * 32, 32)], r.cx_r.at[piece])

                @pl.when(jnp.logical_not(mid) & (n >= 20) & works)
                def _():
                    index = c * 4 + k
                    arrived(r.grad.at[index, rows], r.gx_r.at[index * 2 + half])

            @pl.when(attends)
            def _():
                come(0)
                come(1)

            @pl.when((n == 0) | (n == 8))
            def _():
                for copy in attend_loads[0:12]:
                    pltpu.make_async_copy(copy.src_ref, copy.dst_ref, r.load.at[l]).wait()

            @pl.when(n == 4)
            def _():
                for copy in feed_loads:
                    copy.wait()

            @pl.when(ahead & attends)
            def _():
                project(l, k)

            @pl.when(n == 0)
            def _():
                for copy in pick_copies:
                    copy.wait()
                chosen = r.pk_in[owner, slot]
                r.pk[...] = jnp.concatenate(
                    [chosen, chosen, jnp.zeros((32, 192), jnp.int32), chosen], axis=1
                )
                square = jnp.concatenate([chosen.astype(F32), jnp.zeros((32, 64), F32)], axis=1)
                square = jnp.concatenate([square, jnp.zeros((96, 128), F32)], axis=0)
                r.pt[...] = square.T[0:64]

            @pl.when(ahead & attends)
            def _():
                came = k - 1 + d
                pl.when(came >= 0)(lambda: wait_kv(l, came))
                give_both(n, attend(l, k))

            @pl.when(ahead & jnp.logical_not(attends))
            def _():
                for half in (0, 1):
                    come(half)
                    give(n, half, feed(l, k, half))

            @pl.when(jnp.logical_not(ahead) & works & attends)
            def _():
                attend_back(l, k)
                give_both(n, finish_back(l, k))

            @pl.when(jnp.logical_not(ahead) & works & jnp.logical_not(attends))
            def _():
                for half in (0, 1):
                    come(half)
                    give(n, half, feed_back(l, k, half))

            @pl.when(mid & (n >= 2) & (n < 34))
            def _():
                fold(n - 2, 0)

            feed_l, attend_l = 1 - lax.div(n, 28), 1 - lax.div(n, 31)
            for part in range(4):

                @pl.when((n == FEED_PARTS[0][part]) | (n == FEED_PARTS[1][part]))
                def _():
                    weights_feed(feed_l, part)

                @pl.when((n == ATTEND_PARTS[0][part]) | (n == ATTEND_PARTS[1][part]))
                def _():
                    weights_attend(attend_l, part)

            @pl.when((n == FEED_COLLECT[0]) | (n == FEED_COLLECT[1]))
            def _():
                collect_feed(feed_l)

            @pl.when((n == ATTEND_COLLECT[0]) | (n == ATTEND_COLLECT[1]))
            def _():
                collect_attend(attend_l)

            @pl.when((n == FEED_SHARE[0]) | (n == FEED_SHARE[1]))
            def _():
                share(0, 1536, feed_l)

            @pl.when((n == ATTEND_SHARE[0]) | (n == ATTEND_SHARE[1]))
            def _():
                share(1, 896, attend_l)

            pl.when(n == 32)(end_sends)
            pl.when(mid & (n == 33))(end_middle_sends)
            pl.when(n == 34)(end_small_sends)
            return carry

        lax.fori_loop(0, 36, slot_of, 0)

        small_sums(0)
        for j in range(8):
            arrived(r.nrm_in.at[j], r.nr_r.at[j])
        total = r.nrm_in[0]
        for j in range(1, 8):
            total = total + r.nrm_in[j]
        for i, ref in enumerate((r.o_gain, r.o_bias, r.o_ob)):
            ref[...] = total[i : i + 1, 0:local]

        finish_hand(dx_way)
        for step in range(1, 8):
            send_small(0, step).wait_send()

        @pl.when(mid)
        def _():
            sent(all_norms(0))
            for i in range(4):
                for half in (0, 1):
                    send_grad(i, half).wait_send()
            for n in range(28, 32):
                for half in (0, 1):
                    send_pair(n, half).wait_send()

        @pl.when(jnp.logical_not(mid))
        def _():
            for n in range(28, 32):
                for half in (0, 1):
                    send_part(n, half).wait_send()

    return kernel


def hand_over(*refs):
    count = len(refs) // 3
    loads, stores = [], []
    for i in range(count):
        loads.append(pltpu.make_async_copy(refs[i], refs[2 * count + i], refs[-1].at[0, i]))
        stores.append(
            pltpu.make_async_copy(refs[2 * count + i], refs[count + i], refs[-1].at[1, i])
        )
    for load in loads:
        load.start()
    for load, store in zip(loads, stores):
        load.wait()
        store.start()
    for store in stores:
        store.wait()


def shards(
    stream,
    cotangent,
    lengths,
    picks,
    norm_gain,
    norm_bias,
    out_bias,
    weight_qkv,
    bias_qv,
    weight_score,
    weight_out,
    weight_fc,
    bias_fc,
    weight_proj,
):
    micro, tokens, local = stream.shape
    layers, width = weight_qkv.shape[0], weight_qkv.shape[1]
    inputs = dict(
        stream=stream.transpose(0, 2, 1),
        cot=cotangent.transpose(0, 2, 1),
        lengths=lengths,
        picks=picks.reshape(micro, 24, 64),
        gain=norm_gain,
        shift=norm_bias,
        ob=out_bias,
        wqkv=weight_qkv.transpose(0, 2, 3, 1),
        bqv=bias_qv,
        wscore=weight_score.transpose(2, 0, 1),
        wout=weight_out,
        wfc=weight_fc,
        bfc=bias_fc,
        wpj=weight_proj,
    )
    spaces = dict(
        stream=pl.ANY, cot=pl.ANY, lengths=pltpu.SMEM, wqkv=pl.ANY, wout=pl.ANY, wfc=pl.ANY, wpj=pl.ANY
    )
    part_rows = width // 8
    outputs = dict(
        y=((micro, local, 2 * BLOCK), BF16),
        dx=((micro, local, 2 * BLOCK), BF16),
        o_gain=((1, 192), F32),
        o_bias=((1, 192), F32),
        o_ob=((1, 192), F32),
        o_qkv=((6, part_rows, 192), F32),
        o_qv=((2, 2, 192), F32),
        o_score=((3, 2, 768), F32),
        o_out=((2, 192, part_rows), F32),
        o_fc=((2, part_rows, 768), F32),
        o_fcb=((2, 768), F32),
        o_pj=((2, part_rows, 768), F32),
    )
    dma = pltpu.SemaphoreType.DMA
    scratch = dict(
        stream_in=((4, 768, BLOCK), BF16),
        cot_in=((4, 768, BLOCK), BF16),
        prm=((16, 128), BF16),
        w1=((2, 768, 768), BF16),
        wo=((2, 384, 768), BF16),
        fc=((2, 768, 768), BF16),
        pj=((2, 768, 768), BF16),
        bq=((2, 1, 768), F32),
        fcb=((2, 1, 768), F32),
        prm_in=((4, 4, 16, 128), BF16),
        par=((4, 8, 768), F32),
        last=((BLOCK, 768), BF16),
        pk_out=((micro, 32, 64), jnp.int32),
        pk_in=((2, micro, 32, 64), jnp.int32),
        pk=((32, 384), jnp.int32),
        pt=((64, 128), F32),
        state=((16, BLOCK, 768), BF16),
        normed=((16, BLOCK, 768), BF16),
        q=((24, BLOCK, 128), BF16),
        sig=((8, BLOCK, 128), F32),
        kv=((8, WINDOW + tokens, 128), BF16),
        chosen=((24, 64, 128), BF16),
        keyset=((3, 256, 256), BF16),
        soft=((24, BLOCK, 256), F32),
        merged=((8, BLOCK, 384), BF16),
        hidden=((8, BLOCK, 768), BF16),
        slope=((8, BLOCK, 768), BF16),
        part_out=((4, BLOCK, 768), BF16),
        part_in=((8, BLOCK, 768), BF16),
        own=((4, BLOCK, 768), F32),
        pair_out=((4, BLOCK, 768), BF16),
        pair_in=((8, BLOCK, 768), BF16),
        y_stage=((4, 768, BLOCK), BF16),
        dx_stage=((4, 768, BLOCK), BF16),
        grad=((16, BLOCK, 768), BF16),
        dpre=((4, BLOCK, 768), BF16),
        dqkv=((4, BLOCK, 768), BF16),
        far=((3, 512, 256), BF16),
        sums=((8, 256, 128), F32),
        sums_in=((16, BLOCK, 128), F32),
        wide_f=((768, 1536), F32),
        wide_a=((768, 896), F32),
        packed=((512, 640), BF16),
        xo_f=((4, part_rows, 1536), BF16),
        xi_f=((4, part_rows, 1536), BF16),
        yo_f=((3, part_rows, 1536), BF16),
        yi_f=((6, part_rows, 1536), BF16),
        xo_a=((4, part_rows, 896), BF16),
        xi_a=((4, part_rows, 896), BF16),
        yo_a=((3, part_rows, 896), BF16),
        yi_a=((6, part_rows, 896), BF16),
        nrm=((4, 8, 768), F32),
        nrm_out=((8, 8, 256), F32),
        nrm_in=((8, 8, 256), F32),
        sm=((4, 24, 128), F32),
        sm_in=((32, 24, 128), F32),
    )
    sems = dict(
        xs_s=(8, 4),
        xs_r=(4, 4),
        cr_s=(4,),
        cr_r=(4,),
        xc_s=(2, 4),
        xc_r=(4, 4),
        load=(3,),
        prm_s=(4, 2),
        prm_e=(4,),
        prm_r=(4, 4),
        pick_s=(2,),
        pick_r=(1,),
        nx_s=(32,),
        nx_r=(32,),
        kv_s=(8,),
        kv_r=(8,),
        ps_s=(64,),
        ps_r=(64,),
        mm_s=(64,),
        mm_r=(64,),
        y_s=(4, 2),
        y_r=(2, 2),
        dx_s=(4, 2),
        dx_r=(2, 2),
        cx_s=(16,),
        cx_r=(16,),
        gx_s=(32,),
        gx_r=(32,),
        dk_s=(8,),
        dk_r=(8,),
        xh_s=(2, 4),
        xh_r=(2, 4),
        yh_s=(2, 3),
        yh_r=(2, 6),
        sm_s=(32,),
        sm_r=(32,),
        nr_s=(16,),
        nr_r=(8,),
    )
    names = list(inputs) + list(outputs) + list(scratch) + list(sems)
    results = pl.pallas_call(
        make_kernel(names, micro, width // 8, local),
        out_shape=[jax.ShapeDtypeStruct(*spec) for spec in outputs.values()],
        in_specs=[
            pl.BlockSpec(memory_space=spaces.get(name, pltpu.VMEM))
            for name in inputs
        ],
        out_specs=[pl.BlockSpec(memory_space=pltpu.VMEM) for name in outputs],
        scratch_shapes=[pltpu.VMEM(*spec) for spec in scratch.values()]
        + [dma(shape) for shape in sems.values()],
        compiler_params=pltpu.CompilerParams(
            collective_id=0, has_side_effects=True, vmem_limit_bytes=62 * 2**20
        ),
        name="blocks",
    )(*inputs.values())
    results = pl.pallas_call(
        hand_over,
        out_shape=[jax.ShapeDtypeStruct(*spec) for spec in outputs.values()],
        in_specs=[pl.BlockSpec(memory_space=pl.ANY)] * len(outputs),
        out_specs=[pl.BlockSpec(memory_space=pl.ANY)] * len(outputs),
        scratch_shapes=[pltpu.VMEM(*spec) for spec in outputs.values()] + [dma((2, len(outputs)))],
        name="results",
    )(*results)
    o = types.SimpleNamespace(**dict(zip(outputs, results)))
    dp_count = lax.axis_size("dp")
    if dp_count > 2:
        d = lax.rem(lax.axis_index("dp"), 2)

        def scattered(value):
            placed = jnp.zeros((value.shape[0], 2 * part_rows, value.shape[2]), F32)
            placed = lax.dynamic_update_slice(placed, value, (0, d * part_rows, 0))
            return lax.psum_scatter(placed, "dp", scatter_dimension=1, tiled=True)

        o.o_out = scattered(o.o_out.transpose(0, 2, 1)).transpose(0, 2, 1)
        o.o_qkv, o.o_fc, o.o_pj = map(scattered, (o.o_qkv, o.o_fc, o.o_pj))
        sums = (o.o_gain, o.o_bias, o.o_ob, o.o_qv, o.o_score, o.o_fcb)
        o.o_gain, o.o_bias, o.o_ob, o.o_qv, o.o_score, o.o_fcb = jax.tree.map(
            lambda value: 0.5 * value, lax.psum(sums, "dp")
        )
    rows = o.o_fc.shape[1]
    return (
        o.y.transpose(0, 2, 1),
        o.dx.transpose(0, 2, 1),
        o.o_gain,
        o.o_bias,
        o.o_ob,
        o.o_qkv.reshape(layers, 3, rows, 192).transpose(0, 2, 1, 3),
        o.o_qv,
        o.o_score.transpose(1, 2, 0),
        o.o_out,
        o.o_fc,
        o.o_fcb,
        o.o_pj.transpose(0, 2, 1),
    )


def solution(mesh):
    return jax.shard_map(
        shards,
        mesh=mesh,
        in_specs=(
            P("dp", None, "head"),
            P("dp", None, "head"),
            P("dp"),
            P("dp", "head", None, None),
            P("section", None),
            P("section", None),
            P("section", "head"),
            P(None, None, None, "head"),
            P(None, None, "head"),
            P(None, None, "head"),
            P(None, "head", None),
            P(None, None, "head"),
            P(None, "head"),
            P(None, "head", None),
        ),
        out_specs=(
            P("dp", "section", "head"),
            P("dp", "section", "head"),
            P("section", "head"),
            P("section", "head"),
            P("section", "head"),
            P(None, ("section", "dp"), None, "head"),
            P(None, None, "head"),
            P(None, None, "head"),
            P(None, "head", ("section", "dp")),
            P(None, ("section", "dp"), "head"),
            P(None, "head"),
            P(None, "head", ("section", "dp")),
        ),
        check_vma=False,
    )
```
